128 devices in a mesh: bx: 16 (over x, y), by: 8 (over z, core).
Axes of the slice: x: 4, y: 4, z: 4, core: 2. Of those that a mesh axis runs over, the one named last changes fastest.
Arguments:
- estimate: float32 [512, 16384], P('bx', 'by'), may hold values from 0.5 to 2
- views: float32 [8, 512, 16384], P(None, 'bx', 'by'), may hold values from 0.25 to 4
- psf: float32 [8, 64, 4096], replicated, as said below
- view_list: int32 [16, 8, 8], P('bx', 'by'), may hold values from 0 to 7, as said below
- view_count: int32 [16, 8], P('bx', 'by'), may hold values from 1 to 5, as said below
Outputs:
- refined: float32 [512, 16384], P('bx', 'by')
The draws below stay inside these ranges and needn't reach their ends.
Inputs may be any that keep to these rules, and one draw needn't show every extreme that they name: Each row of view_list is an ordering of all 8 views. `view_count`: a block is seen either by 5 views or by at most 2; a block seen by 5 views is never followed along x (the last block by the first) by another such block; some block is seen by 5 views and some by one. `psf`: every entry is positive.
All inputs are finite; a program needn't handle non-finite values.
Results may differ from the reference program's by a relative error of at most 0.0001.
Values sent between devices are 32-bit elements; how exact they have to be, the bound alone decides.
No kernel may reach another device: no remote copies, remote signals or barrier semaphores. Data moves between devices by JAX's collectives and lax.ppermute only.
A program may use at most 256 MiB of HBM per device.

```python
import math
import jax
import jax.numpy as jnp

V = 8
K = 64
SZ = 64
BX = 32
BY = 32
CMAX = 5
LEND = 2
BLOCKS_X = 16
BLOCKS_Y = 8
NX = 512
NY = 256


def draw_estimate(key, part):
    key = jax.random.fold_in(key, 5)
    level_key = jax.random.fold_in(key, 0)
    shape = (NX, NY * SZ)
    level = jax.random.uniform(level_key, shape, jnp.float32, -1.0, 1.0)
    return 0.5 * jnp.exp(math.log(4.0) * (0.5 + 0.5 * jnp.cbrt(level)))


def draw_psf(key, part):
    key = jax.random.fold_in(key, 11)
    width_key, lobe_key, heading_key, tilt_key, rough_key = jax.random.split(key, 5)
    widths = 0.6 + K * (0.006 + 0.012 * jax.random.uniform(width_key, (V, 3), jnp.float32))
    lobe_draw = jax.random.uniform(lobe_key, (V, 2), jnp.float32)
    lobe_long = (K * (0.19 + 0.12 * lobe_draw[:, 0]))[:, None, None, None]
    lobe_short = (0.6 + K * (0.01 + 0.01 * lobe_draw[:, 1]))[:, None, None, None]
    heading = math.pi * jax.random.uniform(heading_key, (V,), jnp.float32)
    tilt_angle = 0.3 * (2.0 * jax.random.uniform(tilt_key, (V,), jnp.float32) - 1.0)
    axis_a = (jnp.cos(heading) * jnp.cos(tilt_angle))[:, None, None, None]
    axis_b = (jnp.sin(heading) * jnp.cos(tilt_angle))[:, None, None, None]
    axis_c = jnp.sin(tilt_angle)[:, None, None, None]
    offsets = jnp.arange(K, dtype=jnp.float32) - K // 2
    offset_a = offsets[None, :, None, None]
    offset_b = offsets[None, None, :, None]
    offset_c = offsets[None, None, None, :]
    sigma_a = widths[:, 0][:, None, None, None]
    sigma_b = widths[:, 1][:, None, None, None]
    sigma_c = widths[:, 2][:, None, None, None]
    spread = (offset_a / sigma_a) ** 2 + (offset_b / sigma_b) ** 2 + (offset_c / sigma_c) ** 2
    peak_part = 0.58 / ((2.0 * math.pi) ** 1.5 * sigma_a * sigma_b * sigma_c) * jnp.exp(-0.5 * spread)
    along_axis = offset_a * axis_a + offset_b * axis_b + offset_c * axis_c
    radius_sq = offset_a ** 2 + offset_b ** 2 + offset_c ** 2
    across_sq = jnp.maximum(radius_sq - along_axis ** 2, 0.0)
    lobe_part = 0.4 / ((2.0 * math.pi) ** 1.5 * lobe_long * lobe_short * lobe_short) * jnp.exp(-0.5 * (along_axis ** 2 / lobe_long ** 2 + across_sq / lobe_short ** 2))
    floor_level = 0.2 / float(K) ** 3
    roughness = jnp.exp(jax.random.uniform(rough_key, (V, K, K, K), jnp.float32, math.log(0.5), math.log(2.0)))
    return ((peak_part + lobe_part + floor_level) * roughness).reshape(V, K, K * K)


def draw_view_list(key, part):
    key = jax.random.fold_in(key, 37)
    scores = jax.random.randint(key, (BLOCKS_X, BLOCKS_Y, V), 0, 1 << 20) * V + jnp.arange(V, dtype=jnp.int32)
    return jnp.argsort(scores, axis=-1).astype(jnp.int32)


def draw_view_count(key, part):
    key = jax.random.fold_in(key, 23)
    heavy_key, light_key = jax.random.split(key)
    chosen = jax.random.randint(heavy_key, (BLOCKS_X, BLOCKS_Y), 0, 3) == 0
    chosen = chosen.at[0, 0].set(True).at[BLOCKS_X - 1, 0].set(False)
    heavy_block = chosen & jnp.logical_not(jnp.roll(chosen, 1, axis=0))
    light_count = jax.random.randint(light_key, (BLOCKS_X, BLOCKS_Y), 1, CMAX - LEND)
    light_count = light_count.at[BLOCKS_X - 1, 0].set(1)
    return jnp.where(heavy_block, CMAX, light_count).astype(jnp.int32)


def block_levels(key, extent, pieces, low, high):
    level, own = 1.0, jax.random.fold_in(key, 6)
    for axis_at, blocks in pieces:
        steps = jnp.exp(jax.random.uniform(jax.random.fold_in(own, axis_at), (blocks,), jnp.float32, low / len(pieces), high / len(pieces)))
        level = level * jnp.repeat(steps, extent[axis_at] // blocks).reshape([-1 if axis == axis_at else 1 for axis in range(len(extent))])
    return level


def setup_inputs(seed: int = 0) -> dict:
    seeds = jax.random.split(jax.random.key(seed), 6)
    return {
        "estimate": draw_estimate(jax.random.fold_in(seeds[5], 71), 0),
        "views": jnp.clip(jnp.exp(math.log(4.0) - 2.7725887 * jax.random.uniform(seeds[1], (V, NX, NY * SZ), jnp.float32) ** block_levels(seeds[1], (V, NX, NY * SZ), ((1, 16), (2, 8)), -0.2, 0.2)), 0.25, 4.0),
        "psf": draw_psf(jax.random.fold_in(seeds[5], 71), 0),
        "view_list": draw_view_list(jax.random.fold_in(seeds[5], 71), 0),
        "view_count": draw_view_count(jax.random.fold_in(seeds[5], 71), 0),
    }


def reference(estimate, views, psf, view_list, view_count):
    half_psf = K // 2
    volume = estimate.reshape(NX, NY, SZ)
    images = views.reshape(V, NX, NY, SZ)
    kernels = psf.reshape(V, K, K, K)
    pad_shape = (NX + K, NY + K, SZ + K)
    view_ids = jnp.arange(V, dtype=jnp.int32)
    listed = view_ids[None, None, :] < view_count[:, :, None]
    member = (view_list[:, :, :, None] == view_ids[None, None, None, :]) & listed[:, :, :, None]
    cover_mask = jnp.any(member, axis=2).astype(estimate.dtype)
    cover_mask = jnp.repeat(jnp.repeat(cover_mask, BX, axis=0), BY, axis=1)
    seen_by = jnp.repeat(jnp.repeat(view_count, BX, axis=0), BY, axis=1).astype(estimate.dtype)
    spec_field = jnp.fft.rfftn(volume, pad_shape)
    correction = jnp.zeros_like(volume)
    for view_id in range(V):
        spec_kernel = jnp.fft.rfftn(kernels[view_id], pad_shape)
        blurred_full = jnp.fft.irfftn(spec_field * spec_kernel, pad_shape)
        blurred = blurred_full[half_psf:half_psf + NX, half_psf:half_psf + NY, half_psf:half_psf + SZ]
        rel_error = cover_mask[:, :, view_id, None] * (images[view_id] / blurred - 1.0)
        back_full = jnp.fft.irfftn(jnp.fft.rfftn(rel_error, pad_shape) * jnp.conj(spec_kernel), pad_shape)
        back_full = jnp.roll(back_full, (half_psf, half_psf, half_psf), axis=(0, 1, 2))
        correction = correction + back_full[:NX, :NY, :SZ]
    refined = volume * (1.0 + correction / seen_by[:, :, None])
    return refined.reshape(NX, NY * SZ)
```

```python
import functools

import jax
import jax.numpy as jnp
import ml_dtypes
import numpy as np
from jax import lax
from jax.experimental import pallas as pl
from jax.experimental.pallas import tpu as pltpu
from jax.sharding import PartitionSpec as P

V = 8
K = 64
SZ = 64
HALF = K // 2
BX = 32
BY = 32
CMAX = 5
PX = 128
PY = 96
PZ = 96
LANES = 128
WX = BX + K
VMEM_LIMIT = 60 * 1024 * 1024

F32 = jnp.float32
BF16 = jnp.bfloat16


def two_parts(table):
    high = table.astype(ml_dtypes.bfloat16)
    low = (table - high.astype(np.float64)).astype(ml_dtypes.bfloat16)
    return high, low


def x_angles(entries, offset):
    position = np.arange(entries) + offset
    turns = np.mod((2 * np.arange(PX // 2)[None, :] + 1) * position[:, None], 2 * PX)
    return turns * (np.pi / PX)


def x_forward(entries, offset):
    angles = x_angles(entries, offset)
    high, low = two_parts(np.concatenate([np.cos(angles), -np.sin(angles)], axis=1))
    return np.concatenate([high, high, low], axis=0)


def x_inverse(entries, offset):
    angles = x_angles(entries, offset)
    table = np.concatenate([np.cos(angles), -np.sin(angles)], axis=1) * (2.0 / PX)
    high, low = two_parts(table)
    return np.concatenate([high, high, low], axis=1)


def angles_full(period, entries, offset):
    turns = np.mod(np.arange(period)[:, None] * (np.arange(entries) + offset)[None, :], period)
    return turns * (2.0 * np.pi / period)


def forward_rows(period, entries, offset):
    angles = angles_full(period, entries, offset)
    high, low = two_parts(np.concatenate([np.cos(angles), -np.sin(angles)], axis=0))
    return np.concatenate([high, high, low], axis=1)


def forward_wide(period, entries, offset):
    angles = angles_full(period, entries, offset)
    high, low = two_parts(np.concatenate([np.cos(angles), -np.sin(angles)], axis=1))
    return np.concatenate([high, high, low], axis=1)


def inverse_rows(period, entries, offset):
    angles = angles_full(period, entries, offset).T
    high, low = two_parts(np.concatenate([np.cos(angles), np.sin(angles)], axis=0) / period)
    return np.concatenate([high, high, low], axis=1)


def split(data):
    high = data.astype(BF16)
    low = (data - high.astype(F32)).astype(BF16)
    return high, low


def stacked(data):
    high, low = split(data)
    return jnp.concatenate([high, low, high], axis=0)


def dot(a, b):
    return lax.dot_general(a, b, (((1,), (0,)), ((), ())), preferred_element_type=F32)


def dot_tn(a, b):
    return lax.dot_general(a, b, (((0,), (0,)), ((), ())), preferred_element_type=F32)


def dot_nt(a, b):
    return lax.dot_general(a, b, (((1,), (1,)), ((), ())), preferred_element_type=F32)


def swap_halves(data):
    return pltpu.roll(data, LANES // 2, 1)


def first_half(shape):
    return lax.broadcasted_iota(jnp.int32, shape, 1) < LANES // 2


def times_i(data):
    swapped = swap_halves(data)
    return jnp.where(first_half(data.shape), -swapped, swapped)


def left_rows(table, pair):
    half = table.shape[0] // 2
    both = dot(table, stacked(jnp.concatenate(pair, axis=1)))
    out = []
    for part in range(2):
        piece = both[:, part * LANES:(part + 1) * LANES]
        out.append(piece[:half] + times_i(piece[half:]))
    return out


def left_wide(table, pair):
    data = jnp.concatenate(pair, axis=1)
    turned = jnp.concatenate([times_i(piece) for piece in pair], axis=1)
    both = dot(table, stacked(jnp.concatenate([data, turned], axis=0)))
    return [both[:, :LANES], both[:, LANES:]]


def loop(count, body, unroll=1):
    def step(index, carry):
        body(index)
        return carry

    lax.fori_loop(0, count, step, 0, unroll=unroll)


def xz_forward(source, wx, wz, target, groups, base):
    def body(j):
        across = dot_tn(stacked(source(j)), wx)
        for pair in range(4):
            first = across[pair * 128:pair * 128 + 64]
            second = across[pair * 128 + 64:pair * 128 + 128]
            low, high = left_rows(wz, (first, second))
            row = pl.multiple_of((base + j * 8 + pair * 2) * PZ, PZ)
            target[pl.ds(row, PZ), :] = low
            target[pl.ds(row + PZ, PZ), :] = high

    loop(groups, body)


def otf_kernel(count_ref, ids_ref, psf_ref, wx_ref, wz_ref, wy_ref, out_ref, mid):
    @pl.when(pl.program_id(0) < count_ref[0])
    def _():
        def source(j):
            return psf_ref[0, :, pl.ds(pl.multiple_of(j * 512, 512), 512)]

        xz_forward(source, wx_ref[...], wz_ref[...], mid, K // 8, 0)

        def body(j):
            for pair in range(2):
                kz = j * 4 + pair * 2
                first = mid[pl.ds(kz, K, stride=PZ), :]
                second = mid[pl.ds(kz + 1, K, stride=PZ), :]
                low, high = left_rows(wy_ref[...], (first, second))
                out_ref[0, kz] = low
                out_ref[0, kz + 1] = high

        loop(PZ // 4, body)


def spread(values):
    swapped = swap_halves(values)
    lane = first_half(values.shape)
    return jnp.where(lane, values, swapped), jnp.where(lane, swapped, values)


def main_kernel(
    count_ref, ids_ref, left_ref, own_ref, right_ref, image_ref, otf_ref,
    wxf_ref, wzf_ref, wyf_ref, wyi_ref, wzi_ref, wxi_ref,
    wxe_ref, wye_ref, wyo_ref, wxo_ref,
    left_out, own_out, right_out,
    field, turned, total, big, mid, lines, error,
):
    slot = pl.program_id(0)

    @pl.when(slot == 0)
    def _():
        for part, ref in enumerate((left_ref, own_ref, right_ref)):
            def source(j, ref=ref):
                return ref[:, pl.ds(pl.multiple_of(j * 512, 512), 512)]

            xz_forward(source, wxf_ref[...], wzf_ref[...], big, BY // 8, part * BY)

        def body(j):
            kz = j * 2
            first = big[pl.ds(kz, PY, stride=PZ), :]
            second = big[pl.ds(kz + 1, PY, stride=PZ), :]
            for at, value in enumerate(left_rows(wyf_ref[...], (first, second))):
                field[kz + at] = value
                turned[kz + at] = times_i(value)
                total[kz + at] = jnp.zeros((PY, LANES), F32)

        loop(PZ // 2, body)

    @pl.when(slot < count_ref[0])
    def _():
        def product(j):
            for pair in range(2):
                kz = j * 4 + pair * 2
                values = []
                for at in range(2):
                    real, imag = spread(otf_ref[0, kz + at])
                    values.append(real * field[kz + at] + imag * turned[kz + at])
                out = left_rows(wyi_ref[...], values)
                for at in range(2):
                    row = pl.multiple_of((kz + at) * BY, BY)
                    mid[pl.ds(row, BY), :] = out[at]

        loop(PZ // 4, product)

        def inverse_z(j):
            for pair in range(4):
                y = j * 8 + pair * 2
                first = mid[pl.ds(y, PZ, stride=BY), :]
                second = mid[pl.ds(y + 1, PZ, stride=BY), :]
                out = left_rows(wzi_ref[...], (first, second))
                for at in range(2):
                    high, low = split(out[at])
                    row = pl.multiple_of((y + at) * SZ, SZ)
                    lines[pl.ds(row, SZ), :] = jnp.concatenate([high, low, high], axis=1)

        loop(BY // 8, inverse_z)

        def relative(j):
            columns = pl.ds(pl.multiple_of(j * 512, 512), 512)
            blurred = dot_nt(wxi_ref[...], lines[columns, :])
            error[:, columns] = image_ref[0, :, columns] / blurred - 1.0

        loop(BY * SZ // 512, relative)

        def source(j):
            return error[:, pl.ds(pl.multiple_of(j * 512, 512), 512)]

        xz_forward(source, wxe_ref[...], wzf_ref[...], mid, BY // 8, 0)

        def gather(j):
            for pair in range(2):
                kz = j * 4 + pair * 2
                first = mid[pl.ds(kz, BY, stride=PZ), :]
                second = mid[pl.ds(kz + 1, BY, stride=PZ), :]
                for at, value in enumerate(left_wide(wye_ref[...], (first, second))):
                    real, imag = spread(otf_ref[0, kz + at])
                    total[kz + at] += real * value - imag * times_i(value)

        loop(PZ // 4, gather)

    @pl.when(slot == CMAX - 1)
    def _():
        def inverse_y(j):
            kz = j * 2
            out = left_rows(wyo_ref[...], (total[kz], total[kz + 1]))
            for at in range(2):
                row = pl.multiple_of((kz + at) * PY, PY)
                big[pl.ds(row, PY), :] = out[at]

        loop(PZ // 2, inverse_y)

        for part, ref in enumerate((left_out, own_out, right_out)):
            def inverse_zx(j, part=part, ref=ref):
                rows = []
                for pair in range(4):
                    y = part * BY + j * 8 + pair * 2
                    first = big[pl.ds(y, PZ, stride=PY), :]
                    second = big[pl.ds(y + 1, PZ, stride=PY), :]
                    rows += left_rows(wzi_ref[...], (first, second))
                high, low = split(jnp.concatenate(rows, axis=0))
                across = jnp.concatenate([high, low, high], axis=1)
                ref[:, pl.ds(pl.multiple_of(j * 512, 512), 512)] = dot_nt(wxo_ref[...], across)

            loop(BY // 8, inverse_zx)


def whole(shape):
    return pl.BlockSpec(shape, lambda *_: (0,) * len(shape))


def last_slot(slot, count):
    return jnp.minimum(slot, count[0] - 1)


def otf_call(count, ids, psf):
    tables = (x_forward(K, -HALF), forward_rows(PZ, K, -HALF), forward_rows(PY, K, -HALF))
    return pl.pallas_call(
        otf_kernel,
        out_shape=jax.ShapeDtypeStruct((CMAX, PZ, PY, LANES), F32),
        grid_spec=pltpu.PrefetchScalarGridSpec(
            num_scalar_prefetch=2,
            grid=(CMAX,),
            in_specs=[
                pl.BlockSpec((1, K, K * K), lambda s, c, i: (i[last_slot(s, c)], 0, 0)),
            ] + [whole(t.shape) for t in tables],
            out_specs=pl.BlockSpec(
                (1, PZ, PY, LANES), lambda s, c, i: (last_slot(s, c), 0, 0, 0)
            ),
            scratch_shapes=[pltpu.VMEM((K * PZ, LANES), F32)],
        ),
        compiler_params=pltpu.CompilerParams(vmem_limit_bytes=VMEM_LIMIT),
        cost_estimate=pl.CostEstimate(flops=20 * 10**9, bytes_accessed=30 * 10**6, transcendentals=0),
        name="otf",
    )(count, ids, psf, *[jnp.asarray(t) for t in tables])


def main_call(count, ids, window, views, otf):
    left, own, right = window
    rows_wide = (WX, BY * SZ)
    tables = (
        x_forward(WX, 0),
        forward_rows(PZ, SZ, 0),
        forward_rows(PY, PY, 0),
        inverse_rows(PY, BY, HALF),
        inverse_rows(PZ, SZ, 0),
        x_inverse(BX, HALF),
        x_forward(BX, HALF),
        forward_wide(PY, BY, HALF),
        inverse_rows(PY, PY, 0),
        x_inverse(WX, 0),
    )
    spectrum = pltpu.VMEM((PZ, PY, LANES), F32)
    return pl.pallas_call(
        main_kernel,
        out_shape=[jax.ShapeDtypeStruct(rows_wide, F32)] * 3,
        grid_spec=pltpu.PrefetchScalarGridSpec(
            num_scalar_prefetch=2,
            grid=(CMAX,),
            in_specs=[whole(rows_wide)] * 3 + [
                pl.BlockSpec((1, BX, BY * SZ), lambda s, c, i: (i[last_slot(s, c)], 0, 0)),
                pl.BlockSpec((1, PZ, PY, LANES), lambda s, c, i: (last_slot(s, c), 0, 0, 0)),
            ] + [whole(t.shape) for t in tables],
            out_specs=[whole(rows_wide)] * 3,
            scratch_shapes=[
                spectrum,
                spectrum,
                spectrum,
                pltpu.VMEM((PY * PZ, LANES), F32),
                pltpu.VMEM((BY * PZ, LANES), F32),
                pltpu.VMEM((BY * SZ, 3 * LANES), BF16),
                pltpu.VMEM((BX, BY * SZ), F32),
            ],
        ),
        compiler_params=pltpu.CompilerParams(vmem_limit_bytes=VMEM_LIMIT),
        cost_estimate=pl.CostEstimate(flops=30 * 10**9, bytes_accessed=40 * 10**6, transcendentals=0),
        name="views",
    )(count, ids, left, own, right, views, otf, *[jnp.asarray(t) for t in tables])


def shifts(axis):
    devices = lax.axis_size(axis)
    up = [(i, i + 1) for i in range(devices - 1)]
    down = [(i + 1, i) for i in range(devices - 1)]
    return up, down


def per_device(estimate, views, psf, view_list, view_count):
    ids = view_list.reshape(V)
    count = view_count.reshape(1)
    up_x, down_x = shifts("bx")
    up_y, down_y = shifts("by")
    before = lax.ppermute(estimate, "bx", up_x)
    after = lax.ppermute(estimate, "bx", down_x)
    own = jnp.concatenate([before, estimate, after], axis=0)
    left = lax.ppermute(own, "by", up_y)
    right = lax.ppermute(own, "by", down_y)
    otf = otf_call(count, ids, psf)
    left_sum, own_sum, right_sum = main_call(count, ids, (left, own, right), views, otf)
    sums = own_sum + lax.ppermute(left_sum, "by", down_y) + lax.ppermute(right_sum, "by", up_y)
    correction = (
        sums[BX:2 * BX]
        + lax.ppermute(sums[:BX], "bx", down_x)
        + lax.ppermute(sums[2 * BX:], "bx", up_x)
    )
    return estimate * (1.0 + correction / count.astype(F32))


def solution(mesh):
    return jax.shard_map(
        per_device,
        mesh=mesh,
        in_specs=(P("bx", "by"), P(None, "bx", "by"), P(), P("bx", "by", None), P("bx", "by")),
        out_specs=P("bx", "by"),
        check_vma=False,
    )
```

```python
import functools

import jax
import jax.numpy as jnp
import ml_dtypes
import numpy as np
from jax import lax
from jax.experimental import pallas as pl
from jax.experimental.pallas import tpu as pltpu
from jax.sharding import PartitionSpec as P

V = 8
K = 64
SZ = 64
HALF = K // 2
BX = 32
BY = 32
CMAX = 5
PX = 128
PY = 96
PZ = 96
KZ = PZ // 2
SLOT = 64
LANES = 128
WX = BX + K
VMEM_LIMIT = 60 * 1024 * 1024

F32 = jnp.float32
BF16 = jnp.bfloat16


def three_parts(table, axis):
    high = table.astype(ml_dtypes.bfloat16)
    low = (table - high.astype(np.float64)).astype(ml_dtypes.bfloat16)
    return np.concatenate([high, high, low], axis=axis)


def turn(frequency, position, period):
    turns = np.mod(frequency[:, None] * position[None, :], 2 * period)
    return turns * (np.pi / period)


def blocks(values, copies):
    rows, columns = values.shape
    out = np.zeros((copies, rows, copies, columns))
    for copy in range(copies):
        out[copy, :, copy, :] = values
    return out.reshape(copies * rows, copies * columns)


def z_angles(offset):
    return turn(2 * np.arange(KZ) + 1, np.arange(SZ) + offset, PZ)


def padded(values):
    return np.pad(values, ((0, 0), (0, SLOT - KZ)))


def z_forward(offset):
    angles = z_angles(offset).T
    parts = [blocks(padded(part), 2) for part in (np.cos(angles), -np.sin(angles))]
    return three_parts(np.concatenate(parts, axis=1), 0)


def z_inverse():
    angles = z_angles(0).T
    parts = [blocks(padded(part).T, 2) for part in (np.cos(angles), -np.sin(angles))]
    return three_parts(np.concatenate(parts, axis=0) * (2.0 / PZ), 0)


def x_forward(entries, offset, room, copies=1):
    angles = turn(2 * np.arange(PX), np.arange(entries) + offset, PX).T
    cosine, sine = [np.pad(f(angles), ((0, room - entries), (0, 0))) for f in (np.cos, np.sin)]
    return three_parts(blocks(np.block([[cosine, -sine], [sine, cosine]]), copies), 0)


def x_inverse(entries, offset):
    angles = turn(2 * np.arange(PX), np.arange(entries) + offset, PX).T
    cosine, sine = np.cos(angles) / PX, np.sin(angles) / PX
    return three_parts(np.block([[cosine, -sine], [sine, cosine]]), 1)


def y_forward(entries, offset):
    angles = turn(2 * np.arange(PY), np.arange(entries) + offset, PY)
    cosine, sine = np.cos(angles), np.sin(angles)
    return three_parts(np.block([[cosine, sine], [-sine, cosine]]), 1)


def y_inverse(entries, offset):
    angles = turn(2 * np.arange(PY), np.arange(entries) + offset, PY).T
    cosine, sine = np.cos(angles) / PY, np.sin(angles) / PY
    return three_parts(np.block([[cosine, -sine], [sine, cosine]]), 1)


def split(data):
    high = data.astype(BF16)
    low = (data - high.astype(F32)).astype(BF16)
    return high, low


def three(data, axis):
    high, low = split(data)
    return jnp.concatenate([high, low, high], axis=axis)


def dot(a, b):
    return lax.dot_general(a, b, (((1,), (0,)), ((), ())), preferred_element_type=F32)


def dot_nt(a, b):
    return lax.dot_general(a, b, (((1,), (1,)), ((), ())), preferred_element_type=F32)


def loop(count, body):
    def step(index, carry):
        body(index)
        return carry

    lax.fori_loop(0, count, step, 0)


def aligned(index, size):
    return pl.ds(pl.multiple_of(index * size, size), size)


def drop_padding(rows):
    return jnp.concatenate([rows[:KZ], rows[SLOT:SLOT + KZ]], axis=0)


def z_then_x(pieces, wz, wx, real_ref, imag_ref, first_pair, copies):
    rows = pieces[0].shape[0]
    along = dot(three(jnp.concatenate(pieces, axis=0), 1), wz)
    groups = []
    for at in range(0, len(pieces), copies):
        parts = []
        for pair in range(at, at + copies):
            piece = along[pair * rows:(pair + 1) * rows]
            parts += [piece[:, :LANES], piece[:, LANES:]]
        if rows * 2 * copies > LANES:
            sides = []
            for part in parts:
                if rows < LANES:
                    part = jnp.concatenate([part, jnp.zeros((LANES - rows, LANES), F32)], axis=0)
                sides.append(drop_padding(part.T))
            groups.append(jnp.concatenate(sides, axis=1))
        else:
            groups.append(drop_padding(jnp.concatenate(parts, axis=0).T))
    across = dot(three(jnp.concatenate(groups, axis=0), 1), wx)
    for at in range(len(groups)):
        piece = across[at * 2 * KZ:(at + 1) * 2 * KZ]
        for copy in range(copies):
            where = aligned(first_pair + at * copies + copy, 2 * KZ)
            real_ref[where, :] = piece[:, (2 * copy) * LANES:(2 * copy + 1) * LANES]
            imag_ref[where, :] = piece[:, (2 * copy + 1) * LANES:(2 * copy + 2) * LANES]


def along_y(table, reals, imags):
    data = jnp.concatenate(
        [jnp.concatenate(reals, axis=1), jnp.concatenate(imags, axis=1)], axis=0
    )
    out = dot(table, three(data, 0))
    half = table.shape[0] // 2
    return [
        (out[:half, at * LANES:(at + 1) * LANES], out[half:, at * LANES:(at + 1) * LANES])
        for at in range(2)
    ]


def strided(ref, start, count, stride):
    return ref[pl.ds(start, count, stride=stride), :]


def y_from_rows(table, real_ref, imag_ref, kz, count):
    reals = [strided(real_ref, kz + at, count, KZ) for at in range(2)]
    imags = [strided(imag_ref, kz + at, count, KZ) for at in range(2)]
    return along_y(table, reals, imags)


def x_from_rows(table, real_ref, imag_ref, ys, stride):
    empty = jnp.zeros((SLOT - KZ, 6 * LANES), BF16)
    rows = []
    for y in ys:
        data = jnp.concatenate(
            [strided(real_ref, y, KZ, stride), strided(imag_ref, y, KZ, stride)], axis=1
        )
        rows += [three(data, 1), empty]
    return dot_nt(table, jnp.concatenate(rows, axis=0))


def otf_kernel(count_ref, ids_ref, psf_ref, wz_ref, wx_ref, wy_ref, out_ref, real, imag):
    @pl.when(pl.program_id(0) < count_ref[0])
    def _():
        def zx(j):
            data = psf_ref[0, :, aligned(j, 4 * LANES)]
            pieces = [data[:, p * LANES:(p + 1) * LANES] for p in range(4)]
            z_then_x(pieces, wz_ref[...], wx_ref[...], real, imag, j * 4, 1)

        loop(K // 8, zx)

        def y(j):
            for pair in range(UY):
                kz = (j * UY + pair) * 2
                for at, out in enumerate(y_from_rows(wy_ref[...], real, imag, kz, K)):
                    out_ref[0, kz + at, 0] = out[0]
                    out_ref[0, kz + at, 1] = out[1]

        loop(KZ // (2 * UY), y)


UY = 4
UP = 4
UG = 4
UF = 2
UT = 2


def main_kernel(
    count_ref, ids_ref, left_ref, own_ref, right_ref, image_ref, otf_ref,
    wz_ref, wzi_ref, wxf_ref, wyf_ref, wyi_ref, wxi_ref, wxe_ref, wye_ref, wyo_ref, wxo_ref,
    left_out, own_out, right_out,
    field, total, big_real, big_imag, real, imag, lines, error,
):
    slot = pl.program_id(0)

    @pl.when(slot == 0)
    def _():
        for part, ref in enumerate((left_ref, own_ref, right_ref)):
            def zx(j, part=part, ref=ref):
                data = ref[:, aligned(j, 4 * LANES)]
                pieces = [data[:, p * LANES:(p + 1) * LANES] for p in range(4)]
                z_then_x(
                    pieces, wz_ref[...], wxf_ref[...], big_real, big_imag, part * (BY // 2) + j * 4, 1
                )

            loop(BY // 8, zx)

        def y(j):
            for pair in range(UF):
                kz = (j * UF + pair) * 2
                for at, out in enumerate(y_from_rows(wyf_ref[...], big_real, big_imag, kz, PY)):
                    for part in range(2):
                        field[kz + at, part] = out[part]
                        total[kz + at, part] = jnp.zeros((PY, LANES), F32)

        loop(KZ // (2 * UF), y)

    @pl.when(slot < count_ref[0])
    def _():
        def product(j):
            for pair in range(UP):
                kz = (j * UP + pair) * 2
                reals, imags = [], []
                for at in range(2):
                    fr, fi = field[kz + at, 0], field[kz + at, 1]
                    pr, pi = otf_ref[0, kz + at, 0], otf_ref[0, kz + at, 1]
                    reals.append(fr * pr - fi * pi)
                    imags.append(fr * pi + fi * pr)
                for at, out in enumerate(along_y(wyi_ref[...], reals, imags)):
                    where = aligned(kz + at, BY)
                    real[where, :] = out[0]
                    imag[where, :] = out[1]

        loop(KZ // (2 * UP), product)

        def inverse_x(j):
            for group in range(2):
                y = j * 8 + group * 4
                out = x_from_rows(wxi_ref[...], real, imag, [y + k for k in range(4)], BY)
                for pair in range(2):
                    piece = out[:, pair * LANES:(pair + 1) * LANES]
                    data = jnp.concatenate([piece[:BX], piece[BX:]], axis=1)
                    lines[aligned(j * 4 + group * 2 + pair, BX), :] = three(data, 1)

        loop(BY // 8, inverse_x)

        def relative(j):
            blurred = dot(lines[aligned(j, 8 * BX), :], wzi_ref[...])
            for pair in range(8):
                columns = aligned(j * 8 + pair, LANES)
                error[:, columns] = image_ref[0, :, columns] / blurred[pair * BX:(pair + 1) * BX] - 1.0

        loop(2, relative)

        def zx(j):
            data = error[:, aligned(j, 4 * LANES)]
            pieces = [data[:, p * LANES:(p + 1) * LANES] for p in range(4)]
            z_then_x(pieces, wz_ref[...], wxe_ref[...], real, imag, j * 4, 2)

        loop(BY // 8, zx)

        def gather(j):
            for pair in range(UG):
                kz = (j * UG + pair) * 2
                for at, (er, ei) in enumerate(y_from_rows(wye_ref[...], real, imag, kz, BY)):
                    pr, pi = otf_ref[0, kz + at, 0], otf_ref[0, kz + at, 1]
                    total[kz + at, 0] += er * pr + ei * pi
                    total[kz + at, 1] += ei * pr - er * pi

        loop(KZ // (2 * UG), gather)

    @pl.when(slot == CMAX - 1)
    def _():
        def inverse_y(j):
            for pair in range(UT):
                kz = (j * UT + pair) * 2
                reals = [total[kz + at, 0] for at in range(2)]
                imags = [total[kz + at, 1] for at in range(2)]
                for at, out in enumerate(along_y(wyo_ref[...], reals, imags)):
                    where = aligned(kz + at, PY)
                    big_real[where, :] = out[0]
                    big_imag[where, :] = out[1]

        loop(KZ // (2 * UT), inverse_y)

        for part, ref in enumerate((left_out, own_out, right_out)):
            def inverse_xz(j, part=part, ref=ref):
                rows = []
                for group in range(2):
                    y = part * BY + j * 8 + group * 4
                    out = x_from_rows(wxo_ref[...], big_real, big_imag, [y + k for k in range(4)], PY)
                    for pair in range(2):
                        piece = out[:, pair * LANES:(pair + 1) * LANES]
                        rows.append(jnp.concatenate([piece[:WX], piece[WX:]], axis=1))
                sums = dot(three(jnp.concatenate(rows, axis=0), 1), wzi_ref[...])
                for pair in range(4):
                    ref[:, aligned(j * 4 + pair, LANES)] = sums[pair * WX:(pair + 1) * WX]

            loop(BY // 8, inverse_xz)


def whole(shape):
    return pl.BlockSpec(shape, lambda *_: (0,) * len(shape))


def last_slot(slot, count):
    return jnp.minimum(slot, count[0] - 1)


SPECTRUM = (KZ, 2, PY, LANES)


def otf_call(count, ids, psf):
    tables = (z_forward(-HALF), x_forward(K, -HALF, K), y_forward(K, -HALF))
    return pl.pallas_call(
        otf_kernel,
        out_shape=jax.ShapeDtypeStruct((CMAX,) + SPECTRUM, F32),
        grid_spec=pltpu.PrefetchScalarGridSpec(
            num_scalar_prefetch=2,
            grid=(CMAX,),
            in_specs=[
                pl.BlockSpec((1, K, K * K), lambda s, c, i: (i[last_slot(s, c)], 0, 0)),
            ] + [whole(t.shape) for t in tables],
            out_specs=pl.BlockSpec(
                (1,) + SPECTRUM, lambda s, c, i: (last_slot(s, c), 0, 0, 0, 0)
            ),
            scratch_shapes=[pltpu.VMEM((K * KZ, LANES), F32)] * 2,
        ),
        compiler_params=pltpu.CompilerParams(vmem_limit_bytes=VMEM_LIMIT),
        cost_estimate=pl.CostEstimate(flops=20 * 10**9, bytes_accessed=30 * 10**6, transcendentals=0),
        name="otf",
    )(count, ids, psf, *[jnp.asarray(t) for t in tables])


def main_call(count, ids, window, views, otf):
    left, own, right = window
    rows_wide = (WX, BY * SZ)
    tables = (
        z_forward(0),
        z_inverse(),
        x_forward(WX, 0, LANES),
        y_forward(PY, 0),
        y_inverse(BY, HALF),
        x_inverse(BX, HALF),
        x_forward(BX, HALF, BX, 2),
        y_forward(BY, HALF),
        y_inverse(PY, 0),
        x_inverse(WX, 0),
    )
    return pl.pallas_call(
        main_kernel,
        out_shape=[jax.ShapeDtypeStruct(rows_wide, F32)] * 3,
        grid_spec=pltpu.PrefetchScalarGridSpec(
            num_scalar_prefetch=2,
            grid=(CMAX,),
            in_specs=[whole(rows_wide)] * 3 + [
                pl.BlockSpec((1, BX, BY * SZ), lambda s, c, i: (i[last_slot(s, c)], 0, 0)),
                pl.BlockSpec((1,) + SPECTRUM, lambda s, c, i: (last_slot(s, c), 0, 0, 0, 0)),
            ] + [whole(t.shape) for t in tables],
            out_specs=[whole(rows_wide)] * 3,
            scratch_shapes=[
                pltpu.VMEM(SPECTRUM, F32),
                pltpu.VMEM(SPECTRUM, F32),
                pltpu.VMEM((PY * KZ, LANES), F32),
                pltpu.VMEM((PY * KZ, LANES), F32),
                pltpu.VMEM((BY * KZ, LANES), F32),
                pltpu.VMEM((BY * KZ, LANES), F32),
                pltpu.VMEM((BX * BY // 2, 6 * LANES), BF16),
                pltpu.VMEM((BX, BY * SZ), F32),
            ],
        ),
        compiler_params=pltpu.CompilerParams(vmem_limit_bytes=VMEM_LIMIT),
        cost_estimate=pl.CostEstimate(flops=30 * 10**9, bytes_accessed=40 * 10**6, transcendentals=0),
        name="views",
    )(count, ids, left, own, right, views, otf, *[jnp.asarray(t) for t in tables])


def shifts(axis):
    devices = lax.axis_size(axis)
    up = [(i, i + 1) for i in range(devices - 1)]
    down = [(i + 1, i) for i in range(devices - 1)]
    return up, down


def per_device(estimate, views, psf, view_list, view_count):
    ids = view_list.reshape(V)
    count = view_count.reshape(1)
    up_x, down_x = shifts("bx")
    up_y, down_y = shifts("by")
    before = lax.ppermute(estimate, "bx", up_x)
    after = lax.ppermute(estimate, "bx", down_x)
    own = jnp.concatenate([before, estimate, after], axis=0)
    left = lax.ppermute(own, "by", up_y)
    right = lax.ppermute(own, "by", down_y)
    otf = otf_call(count, ids, psf)
    left_sum, own_sum, right_sum = main_call(count, ids, (left, own, right), views, otf)
    sums = own_sum + lax.ppermute(left_sum, "by", down_y) + lax.ppermute(right_sum, "by", up_y)
    correction = (
        sums[BX:2 * BX]
        + lax.ppermute(sums[:BX], "bx", down_x)
        + lax.ppermute(sums[2 * BX:], "bx", up_x)
    )
    return estimate * (1.0 + correction / count.astype(F32))


def solution(mesh):
    return jax.shard_map(
        per_device,
        mesh=mesh,
        in_specs=(P("bx", "by"), P(None, "bx", "by"), P(), P("bx", "by", None), P("bx", "by")),
        out_specs=P("bx", "by"),
        check_vma=False,
    )
```

```python
import functools

import jax
import jax.numpy as jnp
import ml_dtypes
import numpy as np
from jax import lax
from jax.experimental import pallas as pl
from jax.experimental.pallas import tpu as pltpu
from jax.sharding import PartitionSpec as P

V = 8
K = 64
SZ = 64
HALF = K // 2
BX = 32
BY = 32
CMAX = 5
PX = 128
PY = 96
PZ = 96
KZ = PZ // 2
SLOT = 64
LANES = 128
KPITCH = KZ + 4
YPITCH = BY + 4
BIGPITCH = PY + 4
WX = BX + K
VMEM_LIMIT = 60 * 1024 * 1024

F32 = jnp.float32
BF16 = jnp.bfloat16


def three_parts(table, axis=1):
    high = table.astype(ml_dtypes.bfloat16)
    low = (table - high.astype(np.float64)).astype(ml_dtypes.bfloat16)
    return np.concatenate([high, high, low], axis=axis)


def two_rows(table):
    high = table.astype(ml_dtypes.bfloat16)
    low = (table - high.astype(np.float64)).astype(ml_dtypes.bfloat16)
    return np.block([[high, high], [low, np.zeros_like(low)]])


def turn(frequency, position, period):
    turns = np.mod(frequency[:, None] * position[None, :], 2 * period)
    return turns * (np.pi / period)


def blocks(values, copies):
    rows, columns = values.shape
    out = np.zeros((copies, rows, copies, columns))
    for copy in range(copies):
        out[copy, :, copy, :] = values
    return out.reshape(copies * rows, copies * columns)


def z_angles(offset):
    return turn(2 * np.arange(KZ) + 1, np.arange(SZ) + offset, PZ)


def padded(values):
    return np.pad(values, ((0, 0), (0, SLOT - KZ)))


def z_forward(offset):
    angles = z_angles(offset).T
    parts = [blocks(padded(part), 2) for part in (np.cos(angles), -np.sin(angles))]
    return three_parts(np.concatenate(parts, axis=1), 0)


def z_inverse():
    angles = z_angles(0).T
    parts = [blocks(padded(part).T, 2) for part in (np.cos(angles), -np.sin(angles))]
    return three_parts(np.concatenate(parts, axis=0) * (2.0 / PZ), 0)


def x_forward(entries, offset, room, copies=1):
    angles = turn(2 * np.arange(PX), np.arange(entries) + offset, PX).T
    cosine, sine = [np.pad(f(angles), ((0, room - entries), (0, 0))) for f in (np.cos, np.sin)]
    return three_parts(blocks(np.block([[cosine, -sine], [sine, cosine]]), copies), 0)


def x_inverse(entries, offset, parts):
    angles = turn(2 * np.arange(PX), np.arange(entries) + offset, PX).T
    cosine, sine = np.cos(angles) / PX, np.sin(angles) / PX
    return parts(np.block([[cosine, -sine], [sine, cosine]]))


def y_forward(entries, offset):
    angles = turn(2 * np.arange(PY), np.arange(entries) + offset, PY)
    cosine, sine = np.cos(angles), np.sin(angles)
    return three_parts(np.block([[cosine, sine], [-sine, cosine]]), 1)


def y_inverse(entries, offset, parts):
    angles = turn(2 * np.arange(PY), np.arange(entries) + offset, PY).T
    cosine, sine = np.cos(angles) / PY, np.sin(angles) / PY
    return parts(np.block([[cosine, -sine], [sine, cosine]]))


def split(data):
    high = data.astype(BF16)
    low = (data - high.astype(F32)).astype(BF16)
    return high, low


def three(data, axis):
    high, low = split(data)
    return jnp.concatenate([high, low, high], axis=axis)


def dot(a, b):
    return lax.dot_general(a, b, (((1,), (0,)), ((), ())), preferred_element_type=F32)


def dot_nt(a, b):
    return lax.dot_general(a, b, (((1,), (1,)), ((), ())), preferred_element_type=F32)


def loop(count, body, unroll=1):
    def step(index, carry):
        for at in range(unroll):
            body(index * unroll + at)
        return carry

    lax.fori_loop(0, count // unroll, step, 0)


def aligned(index, size):
    return pl.ds(pl.multiple_of(index * size, size), size)


def drop_padding(rows):
    return jnp.concatenate([rows[:KZ], rows[SLOT:SLOT + KZ]], axis=0)


def z_stage(pieces, wz, copies):
    rows = pieces[0].shape[0]
    along = dot(three(jnp.concatenate(pieces, axis=0), 1), wz)
    groups = []
    for at in range(0, len(pieces), copies):
        parts = []
        for pair in range(at, at + copies):
            piece = along[pair * rows:(pair + 1) * rows]
            parts += [piece[:, :LANES], piece[:, LANES:]]
        if rows * 2 * copies > LANES:
            sides = []
            for part in parts:
                if rows < LANES:
                    part = jnp.concatenate([part, jnp.zeros((LANES - rows, LANES), F32)], axis=0)
                sides.append(drop_padding(part.T))
            groups.append(jnp.concatenate(sides, axis=1))
        else:
            groups.append(drop_padding(jnp.concatenate(parts, axis=0).T))
    return three(jnp.concatenate(groups, axis=0), 1)


def x_stage(stash, wx, real_ref, imag_ref, first_pair, copies):
    across = dot(stash, wx)
    for at in range(stash.shape[0] // (2 * KZ)):
        piece = across[at * 2 * KZ:(at + 1) * 2 * KZ]
        for copy in range(copies):
            for y in range(2):
                where = pl.ds((2 * (first_pair + at * copies + copy) + y) * KPITCH, KZ)
                part = piece[y * KZ:(y + 1) * KZ]
                real_ref[where, :] = part[:, (2 * copy) * LANES:(2 * copy + 1) * LANES]
                imag_ref[where, :] = part[:, (2 * copy + 1) * LANES:(2 * copy + 2) * LANES]


def pipelined(count, first, second, stash):
    first(0, stash[0])
    if count == 1:
        second(0, stash[0])

    def body(j):
        step = 2 * j
        first(step + 1, stash[1])
        second(step, stash[0])
        first(jnp.minimum(step + 2, count - 1), stash[0])
        second(step + 1, stash[1])

    loop(count // 2, body)


def z_then_x(read, count, wz, wx, real_ref, imag_ref, first_pair, copies, stash):
    pairs = stash[0].shape[0] // (2 * KZ) * copies
    count = count // pairs

    def first(step, ref):
        data = read(aligned(step, pairs * LANES))
        pieces = [data[:, p * LANES:(p + 1) * LANES] for p in range(pairs)]
        ref[...] = z_stage(pieces, wz[...], copies)

    def second(step, ref):
        x_stage(ref[...], wx[...], real_ref, imag_ref, first_pair + step * pairs, copies)

    pipelined(count, first, second, stash)


def along_y(table, reals, imags):
    data = jnp.concatenate(
        [jnp.concatenate(reals, axis=1), jnp.concatenate(imags, axis=1)], axis=0
    )
    if table.shape[1] == 2 * data.shape[0]:
        out = dot(table, jnp.concatenate(split(data), axis=0))
        out = out[:table.shape[0] // 2] + out[table.shape[0] // 2:]
    else:
        out = dot(table, three(data, 0))
    half = out.shape[0] // 2
    return [
        (out[:half, at * LANES:(at + 1) * LANES], out[half:, at * LANES:(at + 1) * LANES])
        for at in range(2)
    ]


def strided(ref, start, count, stride):
    return ref[pl.ds(start, count, stride=stride), :]


def y_from_rows(table, real_ref, imag_ref, kz, count):
    reals = [strided(real_ref, kz + at, count, KPITCH) for at in range(2)]
    imags = [strided(imag_ref, kz + at, count, KPITCH) for at in range(2)]
    return along_y(table, reals, imags)


def x_from_rows(table, real_ref, imag_ref, ys, stride):
    tall = table.shape[1] == 4 * LANES
    empty = jnp.zeros((SLOT - KZ, table.shape[1]), BF16)
    rows = []
    for y in ys:
        data = jnp.concatenate(
            [strided(real_ref, y, KZ, stride), strided(imag_ref, y, KZ, stride)], axis=1
        )
        rows += [jnp.concatenate(split(data), axis=1) if tall else three(data, 1), empty]
    out = dot_nt(table, jnp.concatenate(rows, axis=0))
    return out[:table.shape[0] // 2] + out[table.shape[0] // 2:] if tall else out


def otf_kernel(begin, count_ref, ids_ref, psf_ref, wz_ref, wx_ref, wy_ref, *rest):
    out_ref, real, imag, stash0, stash1 = rest[-5:]

    @pl.when(pl.program_id(0) + begin < count_ref[0])
    def _():
        def read(columns):
            return psf_ref[0, :, columns]

        z_then_x(read, K // 2, wz_ref, wx_ref, real, imag, 0, 1, (stash0, stash1))

        def y(j):
            for pair in range(UY):
                kz = (j * UY + pair) * 2
                for at, out in enumerate(y_from_rows(wy_ref[...], real, imag, kz, K)):
                    out_ref[0, kz + at, 0] = out[0]
                    out_ref[0, kz + at, 1] = out[1]

        loop(KZ // (2 * UY), y)


ZPO = 16
ZPF = 8
ZPE = 8
UX = 2
UXZ = 1
UY = 12
UP = 12
UG = 12
UF = 8
UT = 12


def main_kernel(
    count_ref, ids_ref, left_ref, own_ref, right_ref, image_ref, otf_ref,
    wz_ref, wzi_ref, wxf_ref, wyf_ref, wyi_ref, wxi_ref, wxe_ref, wye_ref, wyo_ref, wxo_ref,
    left_out, own_out, right_out,
    field, total, big_real, big_imag, real, imag, lines, error,
    wide0, wide1, thin0, thin1,
):
    slot = pl.program_id(0)

    @pl.when(slot == 0)
    def _():
        for part, ref in enumerate((left_ref, own_ref, right_ref)):
            def read(columns, ref=ref):
                return ref[:, columns]

            z_then_x(
                read, BY // 2, wz_ref, wxf_ref, big_real, big_imag, part * (BY // 2), 1, (wide0, wide1)
            )

        def y(j):
            for pair in range(UF):
                kz = (j * UF + pair) * 2
                for at, out in enumerate(y_from_rows(wyf_ref[...], big_real, big_imag, kz, PY)):
                    for part in range(2):
                        field[kz + at, part] = out[part]
                        total[kz + at, part] = jnp.zeros((PY, LANES), F32)

        loop(KZ // (2 * UF), y)

    @pl.when(slot < count_ref[0])
    def _():
        def product(j):
            for pair in range(UP):
                kz = (j * UP + pair) * 2
                reals, imags = [], []
                for at in range(2):
                    fr, fi = field[kz + at, 0], field[kz + at, 1]
                    pr, pi = otf_ref[0, kz + at, 0], otf_ref[0, kz + at, 1]
                    reals.append(fr * pr - fi * pi)
                    imags.append(fr * pi + fi * pr)
                for at, out in enumerate(along_y(wyi_ref[...], reals, imags)):
                    where = pl.ds((kz + at) * YPITCH, BY)
                    real[where, :] = out[0]
                    imag[where, :] = out[1]

        loop(KZ // (2 * UP), product)

        def inverse_x(j):
            for group in range(2):
                y = j * 8 + group * 4
                out = x_from_rows(wxi_ref[...], real, imag, [y + k for k in range(4)], YPITCH)
                for pair in range(2):
                    piece = out[:, pair * LANES:(pair + 1) * LANES]
                    data = jnp.concatenate([piece[:BX], piece[BX:]], axis=1)
                    lines[aligned(j * 4 + group * 2 + pair, BX), :] = three(data, 1)

        loop(BY // 8, inverse_x, UX)

        def relative(j):
            blurred = dot(lines[aligned(j, 8 * BX), :], wzi_ref[...])
            for pair in range(8):
                columns = aligned(j * 8 + pair, LANES)
                error[:, columns] = image_ref[0, :, columns] / blurred[pair * BX:(pair + 1) * BX] - 1.0

        loop(2, relative)

        def read(columns):
            return error[:, columns]

        z_then_x(read, BY // 2, wz_ref, wxe_ref, real, imag, 0, 2, (thin0, thin1))

        def gather(j):
            for pair in range(UG):
                kz = (j * UG + pair) * 2
                for at, (er, ei) in enumerate(y_from_rows(wye_ref[...], real, imag, kz, BY)):
                    pr, pi = otf_ref[0, kz + at, 0], otf_ref[0, kz + at, 1]
                    total[kz + at, 0] += er * pr + ei * pi
                    total[kz + at, 1] += ei * pr - er * pi

        loop(KZ // (2 * UG), gather)

    @pl.when(slot == CMAX - 1)
    def _():
        def inverse_y(j):
            for pair in range(UT):
                kz = (j * UT + pair) * 2
                reals = [total[kz + at, 0] for at in range(2)]
                imags = [total[kz + at, 1] for at in range(2)]
                for at, out in enumerate(along_y(wyo_ref[...], reals, imags)):
                    where = pl.ds((kz + at) * BIGPITCH, PY)
                    big_real[where, :] = out[0]
                    big_imag[where, :] = out[1]

        loop(KZ // (2 * UT), inverse_y)

        for part, ref in enumerate((left_out, own_out, right_out)):
            def inverse_xz(j, part=part, ref=ref):
                rows = []
                for group in range(2):
                    y = part * BY + j * 8 + group * 4
                    out = x_from_rows(wxo_ref[...], big_real, big_imag, [y + k for k in range(4)], BIGPITCH)
                    for pair in range(2):
                        piece = out[:, pair * LANES:(pair + 1) * LANES]
                        rows.append(jnp.concatenate([piece[:WX], piece[WX:]], axis=1))
                sums = dot(three(jnp.concatenate(rows, axis=0), 1), wzi_ref[...])
                for pair in range(4):
                    ref[:, aligned(j * 4 + pair, LANES)] = sums[pair * WX:(pair + 1) * WX]

            loop(BY // 8, inverse_xz, UXZ)


def whole(shape):
    return pl.BlockSpec(shape, lambda *_: (0,) * len(shape))


def last_slot(slot, count):
    return jnp.minimum(slot, count[0] - 1)


SPECTRUM = (KZ, 2, PY, LANES)


def otf_call(count, ids, psf, begin, end, held=None):
    tables = (z_forward(-HALF), x_forward(K, -HALF, K), y_forward(K, -HALF))

    def out_slot(s, c):
        return jnp.clip(s + begin, begin, jnp.maximum(c[0] - 1, begin))

    inputs = [count, ids, psf] + [jnp.asarray(t) for t in tables]
    specs = [
        pl.BlockSpec((1, K, K * K), lambda s, c, i: (i[last_slot(s + begin, c)], 0, 0)),
    ] + [whole(t.shape) for t in tables]
    aliases = {}
    if held is not None:
        aliases = {len(inputs): 0}
        inputs.append(held)
        specs.append(pl.BlockSpec(memory_space=pl.ANY))
    return pl.pallas_call(
        functools.partial(otf_kernel, begin),
        out_shape=jax.ShapeDtypeStruct((CMAX,) + SPECTRUM, F32),
        grid_spec=pltpu.PrefetchScalarGridSpec(
            num_scalar_prefetch=2,
            grid=(end - begin,),
            in_specs=specs,
            out_specs=pl.BlockSpec(
                (1,) + SPECTRUM, lambda s, c, i: (out_slot(s, c), 0, 0, 0, 0)
            ),
            scratch_shapes=[pltpu.VMEM((K * KPITCH, LANES), F32)] * 2
            + [pltpu.VMEM((ZPO * 2 * KZ, 3 * LANES), BF16)] * 2,
        ),
        input_output_aliases=aliases,
        compiler_params=pltpu.CompilerParams(vmem_limit_bytes=VMEM_LIMIT),
        cost_estimate=pl.CostEstimate(
            flops=4 * 10**9 * (end - begin), bytes_accessed=6 * 10**6 * (end - begin), transcendentals=0
        ),
        name="otf",
    )(*inputs)


def main_call(count, ids, window, views, otf):
    left, own, right = window
    rows_wide = (WX, BY * SZ)
    tables = (
        z_forward(0),
        z_inverse(),
        x_forward(WX, 0, LANES),
        y_forward(PY, 0),
        y_inverse(BY, HALF, two_rows),
        x_inverse(BX, HALF, two_rows),
        x_forward(BX, HALF, BX, 2),
        y_forward(BY, HALF),
        y_inverse(PY, 0, three_parts),
        x_inverse(WX, 0, three_parts),
    )
    return pl.pallas_call(
        main_kernel,
        out_shape=[jax.ShapeDtypeStruct(rows_wide, F32)] * 3,
        grid_spec=pltpu.PrefetchScalarGridSpec(
            num_scalar_prefetch=2,
            grid=(CMAX,),
            in_specs=[whole(rows_wide)] * 3 + [
                pl.BlockSpec((1, BX, BY * SZ), lambda s, c, i: (i[last_slot(s, c)], 0, 0)),
                pl.BlockSpec((1,) + SPECTRUM, lambda s, c, i: (last_slot(s, c), 0, 0, 0, 0)),
            ] + [whole(t.shape) for t in tables],
            out_specs=[whole(rows_wide)] * 3,
            scratch_shapes=[
                pltpu.VMEM(SPECTRUM, F32),
                pltpu.VMEM(SPECTRUM, F32),
                pltpu.VMEM((PY * KPITCH, LANES), F32),
                pltpu.VMEM((PY * KPITCH, LANES), F32),
                pltpu.VMEM((KZ * YPITCH, LANES), F32),
                pltpu.VMEM((KZ * YPITCH, LANES), F32),
                pltpu.VMEM((BX * BY // 2, 6 * LANES), BF16),
                pltpu.VMEM((BX, BY * SZ), F32),
                pltpu.VMEM((ZPF * 2 * KZ, 6 * LANES), BF16),
                pltpu.VMEM((ZPF * 2 * KZ, 6 * LANES), BF16),
                pltpu.VMEM((ZPE * KZ, 3 * LANES), BF16),
                pltpu.VMEM((ZPE * KZ, 3 * LANES), BF16),
            ],
        ),
        compiler_params=pltpu.CompilerParams(vmem_limit_bytes=VMEM_LIMIT),
        cost_estimate=pl.CostEstimate(flops=30 * 10**9, bytes_accessed=40 * 10**6, transcendentals=0),
        name="views",
    )(count, ids, left, own, right, views, otf, *[jnp.asarray(t) for t in tables])


def shifts(axis):
    devices = lax.axis_size(axis)
    up = [(i, i + 1) for i in range(devices - 1)]
    down = [(i + 1, i) for i in range(devices - 1)]
    return up, down


def per_device(estimate, views, psf, view_list, view_count):
    ids = view_list.reshape(V)
    count = view_count.reshape(1)
    up_x, down_x = shifts("bx")
    up_y, down_y = shifts("by")
    before = lax.ppermute(estimate, "bx", up_x)
    after = lax.ppermute(estimate, "bx", down_x)
    own = jnp.concatenate([before, estimate, after], axis=0)
    left = lax.ppermute(own, "by", up_y)
    right = lax.ppermute(own, "by", down_y)
    otf = otf_call(count, ids, psf, 0, 2)
    otf = otf_call(count, ids, psf, 2, CMAX, otf)
    left_sum, own_sum, right_sum = main_call(count, ids, (left, own, right), views, otf)
    sums = own_sum + lax.ppermute(left_sum, "by", down_y) + lax.ppermute(right_sum, "by", up_y)
    correction = (
        sums[BX:2 * BX]
        + lax.ppermute(sums[:BX], "bx", down_x)
        + lax.ppermute(sums[2 * BX:], "bx", up_x)
    )
    return estimate * (1.0 + correction / count.astype(F32))


def solution(mesh):
    return jax.shard_map(
        per_device,
        mesh=mesh,
        in_specs=(P("bx", "by"), P(None, "bx", "by"), P(), P("bx", "by", None), P("bx", "by")),
        out_specs=P("bx", "by"),
        check_vma=False,
    )
```

```python
import functools

import jax
import jax.numpy as jnp
import ml_dtypes
import numpy as np
from jax import lax
from jax.experimental import pallas as pl
from jax.experimental.pallas import tpu as pltpu
from jax.sharding import PartitionSpec as P

V = 8
K = 64
SZ = 64
HALF = K // 2
BX = 32
BY = 32
CMAX = 5
PX = 128
PY = 96
PZ = 96
KZ = PZ // 2
SLOT = 64
LANES = 128
KPITCH = KZ + 4
YPITCH = BY + 4
BIGPITCH = PY + 4
WX = BX + K
MIB = 1024 * 1024
OTF_LIMIT = 32 * MIB
MAIN_LIMIT = 48 * MIB
TAIL_LIMIT = 16 * MIB

F32 = jnp.float32
BF16 = jnp.bfloat16


def three_parts(table, axis=1):
    high = table.astype(ml_dtypes.bfloat16)
    low = (table - high.astype(np.float64)).astype(ml_dtypes.bfloat16)
    return np.concatenate([high, high, low], axis=axis)


def two_rows(table):
    high = table.astype(ml_dtypes.bfloat16)
    low = (table - high.astype(np.float64)).astype(ml_dtypes.bfloat16)
    return np.block([[high, high], [low, np.zeros_like(low)]])


def turn(frequency, position, period):
    turns = np.mod(frequency[:, None] * position[None, :], 2 * period)
    return turns * (np.pi / period)


def blocks(values, copies):
    rows, columns = values.shape
    out = np.zeros((copies, rows, copies, columns))
    for copy in range(copies):
        out[copy, :, copy, :] = values
    return out.reshape(copies * rows, copies * columns)


def z_angles(offset):
    return turn(2 * np.arange(KZ) + 1, np.arange(SZ) + offset, PZ)


def padded(values):
    return np.pad(values, ((0, 0), (0, SLOT - KZ)))


def z_forward(offset):
    angles = z_angles(offset).T
    parts = [blocks(padded(part), 2) for part in (np.cos(angles), -np.sin(angles))]
    return three_parts(np.concatenate(parts, axis=1), 0)


def z_inverse():
    angles = z_angles(0).T
    parts = [blocks(padded(part).T, 2) for part in (np.cos(angles), -np.sin(angles))]
    return three_parts(np.concatenate(parts, axis=0) * (2.0 / PZ), 0)


def x_forward(entries, offset, room, copies=1):
    angles = turn(2 * np.arange(PX), np.arange(entries) + offset, PX).T
    cosine, sine = [np.pad(f(angles), ((0, room - entries), (0, 0))) for f in (np.cos, np.sin)]
    return three_parts(blocks(np.block([[cosine, -sine], [sine, cosine]]), copies), 0)


def x_inverse(entries, offset, parts):
    angles = turn(2 * np.arange(PX), np.arange(entries) + offset, PX).T
    cosine, sine = np.cos(angles) / PX, np.sin(angles) / PX
    return parts(np.block([[cosine, -sine], [sine, cosine]]))


def y_forward(entries, offset):
    angles = turn(2 * np.arange(PY), np.arange(entries) + offset, PY)
    cosine, sine = np.cos(angles), np.sin(angles)
    return three_parts(np.block([[cosine, sine], [-sine, cosine]]), 1)


def y_inverse(entries, offset, parts):
    angles = turn(2 * np.arange(PY), np.arange(entries) + offset, PY).T
    cosine, sine = np.cos(angles) / PY, np.sin(angles) / PY
    return parts(np.block([[cosine, -sine], [sine, cosine]]))


def split(data):
    high = data.astype(BF16)
    low = (data - high.astype(F32)).astype(BF16)
    return high, low


def three(data, axis):
    high, low = split(data)
    return jnp.concatenate([high, low, high], axis=axis)


def dot(a, b):
    return lax.dot_general(a, b, (((1,), (0,)), ((), ())), preferred_element_type=F32)


def dot_nt(a, b):
    return lax.dot_general(a, b, (((1,), (1,)), ((), ())), preferred_element_type=F32)


def loop(count, body, unroll=1):
    def step(index, carry):
        for at in range(unroll):
            body(index * unroll + at)
        return carry

    lax.fori_loop(0, count // unroll, step, 0)


def aligned(index, size):
    return pl.ds(pl.multiple_of(index * size, size), size)


def columns(pair, pairs):
    return slice(pair * LANES, (pair + pairs) * LANES)


def drop_padding(rows):
    return jnp.concatenate([rows[:KZ], rows[SLOT:SLOT + KZ]], axis=0)


def z_stage(pieces, wz, copies):
    rows = pieces[0].shape[0]
    along = dot(three(jnp.concatenate(pieces, axis=0), 1), wz)
    groups = []
    for at in range(0, len(pieces), copies):
        parts = []
        for pair in range(at, at + copies):
            piece = along[pair * rows:(pair + 1) * rows]
            parts += [piece[:, :LANES], piece[:, LANES:]]
        if rows * 2 * copies > LANES:
            sides = []
            for part in parts:
                if rows < LANES:
                    part = jnp.concatenate([part, jnp.zeros((LANES - rows, LANES), F32)], axis=0)
                sides.append(drop_padding(part.T))
            groups.append(jnp.concatenate(sides, axis=1))
        else:
            groups.append(drop_padding(jnp.concatenate(parts, axis=0).T))
    return three(jnp.concatenate(groups, axis=0), 1)


def x_stage(stash, wx, real_ref, imag_ref, first_pair, copies):
    across = dot(stash, wx)
    for at in range(stash.shape[0] // (2 * KZ)):
        piece = across[at * 2 * KZ:(at + 1) * 2 * KZ]
        for copy in range(copies):
            for y in range(2):
                where = pl.ds((2 * (first_pair + at * copies + copy) + y) * KPITCH, KZ)
                part = piece[y * KZ:(y + 1) * KZ]
                real_ref[where, :] = part[:, (2 * copy) * LANES:(2 * copy + 1) * LANES]
                imag_ref[where, :] = part[:, (2 * copy + 1) * LANES:(2 * copy + 2) * LANES]


def pipelined(count, first, second, stash):
    first(0, stash[0])
    for step in range(count):
        if step + 1 < count:
            first(step + 1, stash[(step + 1) % 2])
        second(step, stash[step % 2])


def z_then_x(read, count, wz, wx, real_ref, imag_ref, copies, stash):
    pairs = stash[0].shape[0] // (2 * KZ) * copies

    def first(step, ref):
        data = read(step * pairs, pairs)
        pieces = [data[:, p * LANES:(p + 1) * LANES] for p in range(pairs)]
        ref[...] = z_stage(pieces, wz[...], copies)

    def second(step, ref):
        x_stage(ref[...], wx[...], real_ref, imag_ref, step * pairs, copies)

    pipelined(count // pairs, first, second, stash)


def along_y(table, reals, imags):
    data = jnp.concatenate(
        [jnp.concatenate(reals, axis=1), jnp.concatenate(imags, axis=1)], axis=0
    )
    if table.shape[1] == 2 * data.shape[0]:
        out = dot(table, jnp.concatenate(split(data), axis=0))
        out = out[:table.shape[0] // 2] + out[table.shape[0] // 2:]
    else:
        out = dot(table, three(data, 0))
    half = out.shape[0] // 2
    return [
        (out[:half, at * LANES:(at + 1) * LANES], out[half:, at * LANES:(at + 1) * LANES])
        for at in range(2)
    ]


def strided(ref, start, count, stride):
    return ref[pl.ds(start, count, stride=stride), :]


def y_from_rows(table, real_ref, imag_ref, kz, count):
    reals = [strided(real_ref, kz + at, count, KPITCH) for at in range(2)]
    imags = [strided(imag_ref, kz + at, count, KPITCH) for at in range(2)]
    return along_y(table, reals, imags)


def x_from_rows(table, real_ref, imag_ref, ys, stride):
    tall = table.shape[1] == 4 * LANES
    empty = jnp.zeros((SLOT - KZ, table.shape[1]), BF16)
    rows = []
    for y in ys:
        data = jnp.concatenate(
            [strided(real_ref, y, KZ, stride), strided(imag_ref, y, KZ, stride)], axis=1
        )
        rows += [jnp.concatenate(split(data), axis=1) if tall else three(data, 1), empty]
    out = dot_nt(table, jnp.concatenate(rows, axis=0))
    return out[:table.shape[0] // 2] + out[table.shape[0] // 2:] if tall else out


def otf_kernel(begin, end, count_ref, ids_ref, psf_hbm, wz_ref, wx_ref, wy_ref, *rest):
    out_hbm, psf, out, real, imag, stash0, stash1, psf_sem, out_sem = rest[-9:]
    steps = KZ // (2 * UY)

    def fetch(step):
        buffer = lax.rem(step, 2)
        return pltpu.make_async_copy(
            psf_hbm.at[ids_ref[begin + step]], psf.at[buffer], psf_sem.at[buffer]
        )

    def store(step, j):
        where = pl.ds(j * 2 * UY, 2 * UY)
        return pltpu.make_async_copy(
            out.at[where], out_hbm.at[begin + step, where], out_sem.at[j]
        )

    slots = jnp.maximum(jnp.minimum(count_ref[0], end) - begin, 0)

    @pl.when(slots > 0)
    def _():
        fetch(0).start()

    def body(step, carry):
        buffer = lax.rem(step, 2)
        fetch(step).wait()

        @pl.when(step + 1 < slots)
        def _():
            fetch(step + 1).start()

        def read(pair, pairs):
            return psf[buffer, :, columns(pair, pairs)]

        z_then_x(read, K // 2, wz_ref, wx_ref, real, imag, 1, (stash0, stash1))

        def y(j):
            @pl.when(step > 0)
            def _():
                store(step - 1, j).wait()

            for pair in range(UY):
                kz = (j * UY + pair) * 2
                for at, value in enumerate(y_from_rows(wy_ref[...], real, imag, kz, K)):
                    out[kz + at, 0] = value[0]
                    out[kz + at, 1] = value[1]
            store(step, j).start()

        loop(steps, y)
        return carry

    lax.fori_loop(0, slots, body, 0)

    @pl.when(slots > 0)
    def _():
        for j in range(steps):
            store(slots - 1, j).wait()


ZPO = 16
ZPF = 8
ZPE = 8
UX = 2
UY = 12
UP = 12
UG = 12
UF = 8
UT = 12


def final_sums(wxo, wzi, chunks, stash):
    def first(step, ref):
        real_ref, imag_ref, row, _, _ = chunks[step]
        for group in range(2):
            ys = [row + group * 4 + k for k in range(4)]
            out = x_from_rows(wxo[...], real_ref, imag_ref, ys, YPITCH)
            for pair in range(2):
                piece = out[:, pair * LANES:(pair + 1) * LANES]
                data = jnp.concatenate([piece[:WX], piece[WX:]], axis=1)
                at = (group * 2 + pair) * WX
                ref[at:at + WX, :] = three(data, 1)

    def second(step, ref):
        _, _, _, out, pair = chunks[step]
        sums = dot(ref[...], wzi[...])
        for at in range(4):
            out[:, columns(pair + at, 1)] = sums[at * WX:(at + 1) * WX]

    pipelined(len(chunks), first, second, stash)


def main_kernel(
    count_ref, ids_ref, left_ref, own_ref, right_ref, views_hbm, otf_hbm,
    wz_ref, wzi_ref, wxf_ref, wyf_ref, wyi_ref, wxi_ref, wxe_ref, wye_ref, wyo_ref, wxo_ref,
    left_out, right_out, real_hbm, imag_hbm,
    field, total, big_real, big_imag, real, imag, lines, error, otf, image,
    wide0, wide1, thin0, thin1, last0, last1, otf_sem, image_sem, own_sem,
):
    count = count_ref[0]

    def fetch(slot):
        buffer = lax.rem(slot, 2)
        return (
            pltpu.make_async_copy(otf_hbm.at[slot], otf.at[buffer], otf_sem.at[buffer]),
            pltpu.make_async_copy(
                views_hbm.at[ids_ref[slot]], image.at[buffer], image_sem.at[buffer]
            ),
        )

    for copy in fetch(0):
        copy.start()

    def read_window(pair, pairs):
        part, pair = divmod(pair, BY // 2)
        return (left_ref, own_ref, right_ref)[part][:, columns(pair, pairs)]

    z_then_x(read_window, PY // 2, wz_ref, wxf_ref, big_real, big_imag, 1, (wide0, wide1))

    def field_y(j):
        for pair in range(UF):
            kz = (j * UF + pair) * 2
            for at, out in enumerate(y_from_rows(wyf_ref[...], big_real, big_imag, kz, PY)):
                for part in range(2):
                    field[kz + at, part] = out[part]
                    total[kz + at, part] = jnp.zeros((PY, LANES), F32)

    loop(KZ // (2 * UF), field_y)

    def view(slot, carry):
        buffer = lax.rem(slot, 2)
        for copy in fetch(slot):
            copy.wait()

        @pl.when(slot + 1 < count)
        def _():
            for copy in fetch(slot + 1):
                copy.start()

        def product(j):
            for pair in range(UP):
                kz = (j * UP + pair) * 2
                reals, imags = [], []
                for at in range(2):
                    fr, fi = field[kz + at, 0], field[kz + at, 1]
                    pr, pi = otf[buffer, kz + at, 0], otf[buffer, kz + at, 1]
                    reals.append(fr * pr - fi * pi)
                    imags.append(fr * pi + fi * pr)
                for at, out in enumerate(along_y(wyi_ref[...], reals, imags)):
                    where = pl.ds((kz + at) * YPITCH, BY)
                    real[where, :] = out[0]
                    imag[where, :] = out[1]

        loop(KZ // (2 * UP), product)

        def inverse_x(j):
            for group in range(2):
                y = j * 8 + group * 4
                out = x_from_rows(wxi_ref[...], real, imag, [y + k for k in range(4)], YPITCH)
                for pair in range(2):
                    piece = out[:, pair * LANES:(pair + 1) * LANES]
                    data = jnp.concatenate([piece[:BX], piece[BX:]], axis=1)
                    lines[aligned(j * 4 + group * 2 + pair, BX), :] = three(data, 1)

        loop(BY // 8, inverse_x, UX)

        for j in range(2):
            blurred = dot(lines[j * 8 * BX:(j + 1) * 8 * BX, :], wzi_ref[...])
            for pair in range(8):
                where = columns(j * 8 + pair, 1)
                error[:, where] = image[buffer, :, where] / blurred[pair * BX:(pair + 1) * BX] - 1.0

        def read_error(pair, pairs):
            return error[:, columns(pair, pairs)]

        z_then_x(read_error, BY // 2, wz_ref, wxe_ref, real, imag, 2, (thin0, thin1))

        def gather(j):
            for pair in range(UG):
                kz = (j * UG + pair) * 2
                for at, (er, ei) in enumerate(y_from_rows(wye_ref[...], real, imag, kz, BY)):
                    pr, pi = otf[buffer, kz + at, 0], otf[buffer, kz + at, 1]
                    total[kz + at, 0] += er * pr + ei * pi
                    total[kz + at, 1] += ei * pr - er * pi

        loop(KZ // (2 * UG), gather)
        return carry

    lax.fori_loop(0, count, view, 0)

    def inverse_y(j):
        for pair in range(UT):
            kz = (j * UT + pair) * 2
            reals = [total[kz + at, 0] for at in range(2)]
            imags = [total[kz + at, 1] for at in range(2)]
            for at, out in enumerate(along_y(wyo_ref[...], reals, imags)):
                row = (kz + at) * YPITCH
                for value, big, own in zip(out, (big_real, big_imag), (real, imag)):
                    big[pl.ds(row, BY), :] = value[:BY]
                    own[pl.ds(row, BY), :] = value[BY:2 * BY]
                    big[pl.ds(KZ * YPITCH + row, BY), :] = value[2 * BY:]

    loop(KZ // (2 * UT), inverse_y)
    copies = (
        pltpu.make_async_copy(real, real_hbm, own_sem.at[0]),
        pltpu.make_async_copy(imag, imag_hbm, own_sem.at[1]),
    )
    for copy in copies:
        copy.start()
    chunks = [
        (big_real, big_imag, side * KZ * YPITCH + y, out, y // 2)
        for side, out in enumerate((left_out, right_out))
        for y in range(0, BY, 8)
    ]
    final_sums(wxo_ref, wzi_ref, chunks, (last0, last1))
    for copy in copies:
        copy.wait()


def tail_kernel(real, imag, wzi_ref, wxo_ref, out, last0, last1):
    chunks = [(real, imag, y, out, y // 2) for y in range(0, BY, 8)]
    final_sums(wxo_ref, wzi_ref, chunks, (last0, last1))


SPECTRUM = (KZ, 2, PY, LANES)
ROWS = (KZ * YPITCH, LANES)
WIDE = (WX, BY * SZ)
LAST = pltpu.VMEM((4 * WX, 6 * LANES), BF16)
IN_VMEM = pl.BlockSpec(memory_space=pltpu.VMEM)
IN_SMEM = pl.BlockSpec(memory_space=pltpu.SMEM)
ANYWHERE = pl.BlockSpec(memory_space=pl.ANY)


def otf_call(count, ids, psf, begin, end, held=None):
    tables = (z_forward(-HALF), x_forward(K, -HALF, K), y_forward(K, -HALF))
    inputs = [count, ids, psf] + [jnp.asarray(t) for t in tables]
    specs = [IN_SMEM, IN_SMEM, ANYWHERE] + [IN_VMEM] * len(tables)
    aliases = {}
    if held is not None:
        aliases = {len(inputs): 0}
        inputs.append(held)
        specs.append(ANYWHERE)
    return pl.pallas_call(
        functools.partial(otf_kernel, begin, end),
        out_shape=jax.ShapeDtypeStruct((CMAX,) + SPECTRUM, F32),
        in_specs=specs,
        out_specs=ANYWHERE,
        scratch_shapes=[
            pltpu.VMEM((2, K, K * K), F32),
            pltpu.VMEM(SPECTRUM, F32),
            pltpu.VMEM((K * KPITCH, LANES), F32),
            pltpu.VMEM((K * KPITCH, LANES), F32),
            pltpu.VMEM((ZPO * 2 * KZ, 3 * LANES), BF16),
            pltpu.VMEM((ZPO * 2 * KZ, 3 * LANES), BF16),
            pltpu.SemaphoreType.DMA((2,)),
            pltpu.SemaphoreType.DMA((KZ // (2 * UY),)),
        ],
        input_output_aliases=aliases,
        compiler_params=pltpu.CompilerParams(vmem_limit_bytes=OTF_LIMIT),
        cost_estimate=pl.CostEstimate(
            flops=4 * 10**9 * (end - begin), bytes_accessed=6 * 10**6 * (end - begin), transcendentals=0
        ),
        name="otf",
    )(*inputs)


def main_call(count, ids, window, views, otf):
    left, own, right = window
    tables = (
        z_forward(0),
        z_inverse(),
        x_forward(WX, 0, LANES),
        y_forward(PY, 0),
        y_inverse(BY, HALF, two_rows),
        x_inverse(BX, HALF, two_rows),
        x_forward(BX, HALF, BX, 2),
        y_forward(BY, HALF),
        y_inverse(PY, 0, three_parts),
        x_inverse(WX, 0, three_parts),
    )
    return pl.pallas_call(
        main_kernel,
        out_shape=[jax.ShapeDtypeStruct(WIDE, F32)] * 2 + [jax.ShapeDtypeStruct(ROWS, F32)] * 2,
        in_specs=[IN_SMEM] * 2 + [IN_VMEM] * 3 + [ANYWHERE] * 2 + [IN_VMEM] * len(tables),
        out_specs=[IN_VMEM] * 2 + [ANYWHERE] * 2,
        scratch_shapes=[
            pltpu.VMEM(SPECTRUM, F32),
            pltpu.VMEM(SPECTRUM, F32),
            pltpu.VMEM((PY * KPITCH, LANES), F32),
            pltpu.VMEM((PY * KPITCH, LANES), F32),
            pltpu.VMEM(ROWS, F32),
            pltpu.VMEM(ROWS, F32),
            pltpu.VMEM((BX * BY // 2, 6 * LANES), BF16),
            pltpu.VMEM((BX, BY * SZ), F32),
            pltpu.VMEM((2,) + SPECTRUM, F32),
            pltpu.VMEM((2, BX, BY * SZ), F32),
            pltpu.VMEM((ZPF * 2 * KZ, 6 * LANES), BF16),
            pltpu.VMEM((ZPF * 2 * KZ, 6 * LANES), BF16),
            pltpu.VMEM((ZPE * KZ, 3 * LANES), BF16),
            pltpu.VMEM((ZPE * KZ, 3 * LANES), BF16),
            LAST,
            LAST,
            pltpu.SemaphoreType.DMA((2,)),
            pltpu.SemaphoreType.DMA((2,)),
            pltpu.SemaphoreType.DMA((2,)),
        ],
        compiler_params=pltpu.CompilerParams(vmem_limit_bytes=MAIN_LIMIT),
        cost_estimate=pl.CostEstimate(flops=30 * 10**9, bytes_accessed=40 * 10**6, transcendentals=0),
        name="views",
    )(count, ids, left, own, right, views, otf, *[jnp.asarray(t) for t in tables])


def tail_call(real, imag):
    tables = (z_inverse(), x_inverse(WX, 0, three_parts))
    return pl.pallas_call(
        tail_kernel,
        out_shape=jax.ShapeDtypeStruct(WIDE, F32),
        in_specs=[IN_VMEM] * 4,
        out_specs=IN_VMEM,
        scratch_shapes=[LAST, LAST],
        compiler_params=pltpu.CompilerParams(vmem_limit_bytes=TAIL_LIMIT),
        cost_estimate=pl.CostEstimate(flops=4 * 10**9, bytes_accessed=3 * 10**6, transcendentals=0),
        name="tail",
    )(real, imag, *[jnp.asarray(t) for t in tables])


def shifts(axis):
    devices = lax.axis_size(axis)
    up = [(i, i + 1) for i in range(devices - 1)]
    down = [(i + 1, i) for i in range(devices - 1)]
    return up, down


def per_device(estimate, views, psf, view_list, view_count):
    ids = view_list.reshape(V)
    count = view_count.reshape(1)
    up_x, down_x = shifts("bx")
    up_y, down_y = shifts("by")
    before = lax.ppermute(estimate, "bx", up_x)
    after = lax.ppermute(estimate, "bx", down_x)
    own = jnp.concatenate([before, estimate, after], axis=0)
    left = lax.ppermute(own, "by", up_y)
    right = lax.ppermute(own, "by", down_y)
    otf = otf_call(count, ids, psf, 0, 2)
    otf = otf_call(count, ids, psf, 2, CMAX, otf)
    left_sum, right_sum, real, imag = main_call(count, ids, (left, own, right), views, otf)
    from_right = lax.ppermute(left_sum, "by", down_y)
    from_left = lax.ppermute(right_sum, "by", up_y)
    sums = tail_call(real, imag) + from_right + from_left
    correction = (
        sums[BX:2 * BX]
        + lax.ppermute(sums[:BX], "bx", down_x)
        + lax.ppermute(sums[2 * BX:], "bx", up_x)
    )
    return estimate * (1.0 + correction / count.astype(F32))


def solution(mesh):
    return jax.shard_map(
        per_device,
        mesh=mesh,
        in_specs=(P("bx", "by"), P(None, "bx", "by"), P(), P("bx", "by", None), P("bx", "by")),
        out_specs=P("bx", "by"),
        check_vma=False,
    )
```

```python
import functools

import jax
import jax.numpy as jnp
import ml_dtypes
import numpy as np
from jax import lax
from jax.experimental import pallas as pl
from jax.experimental.pallas import tpu as pltpu
from jax.sharding import PartitionSpec as P

V = 8
K = 64
SZ = 64
HALF = K // 2
BX = 32
BY = 32
CMAX = 5
PX = 128
PY = 96
PZ = 96
KZ = PZ // 2
SLOT = 64
LANES = 128
KPITCH = KZ + 4
YPITCH = BY + 4
BIGPITCH = PY + 4
WX = BX + K
MIB = 1024 * 1024

F32 = jnp.float32
BF16 = jnp.bfloat16


def three_parts(table, axis=1):
    high = table.astype(ml_dtypes.bfloat16)
    low = (table - high.astype(np.float64)).astype(ml_dtypes.bfloat16)
    return np.concatenate([high, high, low], axis=axis)


def two_rows(table):
    high = table.astype(ml_dtypes.bfloat16)
    low = (table - high.astype(np.float64)).astype(ml_dtypes.bfloat16)
    return np.block([[high, high], [low, np.zeros_like(low)]])


def turn(frequency, position, period):
    turns = np.mod(frequency[:, None] * position[None, :], 2 * period)
    return turns * (np.pi / period)


def blocks(values, copies):
    rows, columns = values.shape
    out = np.zeros((copies, rows, copies, columns))
    for copy in range(copies):
        out[copy, :, copy, :] = values
    return out.reshape(copies * rows, copies * columns)


def z_angles(offset):
    return turn(2 * np.arange(KZ) + 1, np.arange(SZ) + offset, PZ)


def padded(values):
    return np.pad(values, ((0, 0), (0, SLOT - KZ)))


def z_forward(offset):
    angles = z_angles(offset).T
    parts = [blocks(padded(part), 2) for part in (np.cos(angles), -np.sin(angles))]
    return three_parts(np.concatenate(parts, axis=1), 0)


def z_inverse():
    angles = z_angles(0).T
    parts = [blocks(padded(part).T, 2) for part in (np.cos(angles), -np.sin(angles))]
    return three_parts(np.concatenate(parts, axis=0) * (2.0 / PZ), 0)


def x_forward(entries, offset, room, copies=1):
    angles = turn(2 * np.arange(PX), np.arange(entries) + offset, PX).T
    cosine, sine = [np.pad(f(angles), ((0, room - entries), (0, 0))) for f in (np.cos, np.sin)]
    return three_parts(blocks(np.block([[cosine, -sine], [sine, cosine]]), copies), 0)


def x_inverse(entries, offset, parts):
    angles = turn(2 * np.arange(PX), np.arange(entries) + offset, PX).T
    cosine, sine = np.cos(angles) / PX, np.sin(angles) / PX
    return parts(np.block([[cosine, -sine], [sine, cosine]]))


def y_forward(entries, offset):
    angles = turn(2 * np.arange(PY), np.arange(entries) + offset, PY)
    cosine, sine = np.cos(angles), np.sin(angles)
    return three_parts(np.block([[cosine, sine], [-sine, cosine]]), 1)


def y_inverse(entries, offset, parts):
    angles = turn(2 * np.arange(PY), np.arange(entries) + offset, PY).T
    cosine, sine = np.cos(angles) / PY, np.sin(angles) / PY
    return parts(np.block([[cosine, -sine], [sine, cosine]]))


def split(data):
    high = data.astype(BF16)
    low = (data - high.astype(F32)).astype(BF16)
    return high, low


def three(data, axis):
    high, low = split(data)
    return jnp.concatenate([high, low, high], axis=axis)


def dot(a, b):
    return lax.dot_general(a, b, (((1,), (0,)), ((), ())), preferred_element_type=F32)


def dot_nt(a, b):
    return lax.dot_general(a, b, (((1,), (1,)), ((), ())), preferred_element_type=F32)


def loop(count, body, unroll=1):
    def step(index, carry):
        for at in range(unroll):
            body(index * unroll + at)
        return carry

    lax.fori_loop(0, count // unroll, step, 0)


def aligned(index, size):
    return pl.ds(pl.multiple_of(index * size, size), size)


def columns(pair, pairs):
    return slice(pair * LANES, (pair + pairs) * LANES)


def drop_padding(rows):
    return jnp.concatenate([rows[:KZ], rows[SLOT:SLOT + KZ]], axis=0)


def z_stage(pieces, wz, copies):
    rows = pieces[0].shape[0]
    along = dot(three(jnp.concatenate(pieces, axis=0), 1), wz)
    groups = []
    for at in range(0, len(pieces), copies):
        parts = []
        for pair in range(at, at + copies):
            piece = along[pair * rows:(pair + 1) * rows]
            parts += [piece[:, :LANES], piece[:, LANES:]]
        if rows * 2 * copies > LANES:
            sides = []
            for part in parts:
                if rows < LANES:
                    part = jnp.concatenate([part, jnp.zeros((LANES - rows, LANES), F32)], axis=0)
                sides.append(drop_padding(part.T))
            groups.append(jnp.concatenate(sides, axis=1))
        else:
            groups.append(drop_padding(jnp.concatenate(parts, axis=0).T))
    return three(jnp.concatenate(groups, axis=0), 1)


def x_stage(stash, wx, real_ref, imag_ref, first_pair, copies):
    across = dot(stash, wx)
    for at in range(stash.shape[0] // (2 * KZ)):
        piece = across[at * 2 * KZ:(at + 1) * 2 * KZ]
        for copy in range(copies):
            for y in range(2):
                where = pl.ds((2 * (first_pair + at * copies + copy) + y) * KPITCH, KZ)
                part = piece[y * KZ:(y + 1) * KZ]
                real_ref[where, :] = part[:, (2 * copy) * LANES:(2 * copy + 1) * LANES]
                imag_ref[where, :] = part[:, (2 * copy + 1) * LANES:(2 * copy + 2) * LANES]


def pipelined(count, first, second, stash):
    first(0, stash[0])
    for step in range(count):
        if step + 1 < count:
            first(step + 1, stash[(step + 1) % 2])
        second(step, stash[step % 2])


def z_then_x(read, count, wz, wx, real_ref, imag_ref, copies, stash):
    pairs = stash[0].shape[0] // (2 * KZ) * copies

    def first(step, ref):
        data = read(step * pairs, pairs)
        pieces = [data[:, p * LANES:(p + 1) * LANES] for p in range(pairs)]
        ref[...] = z_stage(pieces, wz[...], copies)

    def second(step, ref):
        x_stage(ref[...], wx[...], real_ref, imag_ref, step * pairs, copies)

    pipelined(count // pairs, first, second, stash)


def along_y(table, reals, imags):
    data = jnp.concatenate(
        [jnp.concatenate(reals, axis=1), jnp.concatenate(imags, axis=1)], axis=0
    )
    if table.shape[1] == 2 * data.shape[0]:
        out = dot(table, jnp.concatenate(split(data), axis=0))
        out = out[:table.shape[0] // 2] + out[table.shape[0] // 2:]
    else:
        out = dot(table, three(data, 0))
    half = out.shape[0] // 2
    return [
        (out[:half, at * LANES:(at + 1) * LANES], out[half:, at * LANES:(at + 1) * LANES])
        for at in range(2)
    ]


def strided(ref, start, count, stride):
    return ref[pl.ds(start, count, stride=stride), :]


def y_from_rows(table, real_ref, imag_ref, kz, count):
    reals = [strided(real_ref, kz + at, count, KPITCH) for at in range(2)]
    imags = [strided(imag_ref, kz + at, count, KPITCH) for at in range(2)]
    return along_y(table, reals, imags)


def x_from_rows(table, real_ref, imag_ref, ys, stride):
    tall = table.shape[1] == 4 * LANES
    empty = jnp.zeros((SLOT - KZ, table.shape[1]), BF16)
    rows = []
    for y in ys:
        data = jnp.concatenate(
            [strided(real_ref, y, KZ, stride), strided(imag_ref, y, KZ, stride)], axis=1
        )
        rows += [jnp.concatenate(split(data), axis=1) if tall else three(data, 1), empty]
    out = dot_nt(table, jnp.concatenate(rows, axis=0))
    return out[:table.shape[0] // 2] + out[table.shape[0] // 2:] if tall else out


def table_copies(sources, targets, sems):
    return [
        pltpu.make_async_copy(source, target, sems.at[at])
        for at, (source, target) in enumerate(zip(sources, targets))
    ]


def room_for(tables):
    return [pltpu.VMEM(t.shape, BF16) for t in tables]


def otf_kernel(begin, end, count_ref, ids_ref, psf_hbm, wz_hbm, wx_hbm, wy_hbm, *rest):
    out_hbm, psf, out, real, imag, stash0, stash1, *rest = rest[-13:]
    wz_ref, wx_ref, wy_ref, psf_sem, out_sem, table_sem = rest
    steps = KZ // (2 * UY)

    def fetch(step):
        buffer = lax.rem(step, 2)
        return pltpu.make_async_copy(
            psf_hbm.at[ids_ref[begin + step]], psf.at[buffer], psf_sem.at[buffer]
        )

    def store(step, j):
        where = pl.ds(j * UY, UY)
        return pltpu.make_async_copy(
            out.at[where], out_hbm.at[begin + step, where], out_sem.at[j]
        )

    slots = jnp.maximum(jnp.minimum(count_ref[0], end) - begin, 0)

    @pl.when(slots > 0)
    def _():
        fetch(0).start()

    tables = table_copies((wz_hbm, wx_hbm, wy_hbm), (wz_ref, wx_ref, wy_ref), table_sem)
    for copy in tables:
        copy.start()
    for copy in tables:
        copy.wait()

    def body(step, carry):
        buffer = lax.rem(step, 2)
        fetch(step).wait()

        @pl.when(step + 1 < slots)
        def _():
            fetch(step + 1).start()

        def read(pair, pairs):
            return psf[buffer, :, columns(pair, pairs)]

        z_then_x(read, K // 2, wz_ref, wx_ref, real, imag, 1, (stash0, stash1))

        def y(j):
            @pl.when(step > 0)
            def _():
                store(step - 1, 2 * j).wait()
                store(step - 1, 2 * j + 1).wait()

            for pair in range(UY):
                kz = (j * UY + pair) * 2
                for at, value in enumerate(y_from_rows(wy_ref[...], real, imag, kz, K)):
                    out[kz + at, 0] = value[0]
                    out[kz + at, 1] = value[1]
                if pair == UY // 2 - 1:
                    store(step, 2 * j).start()
            store(step, 2 * j + 1).start()

        loop(steps, y)
        return carry

    lax.fori_loop(0, slots, body, 0)

    @pl.when(slots > 0)
    def _():
        for j in range(2 * steps):
            store(slots - 1, j).wait()


ZPO = 16
ZPF = 8
ZPE = 8
UX = 4
OTF_LIMITS = (60 * MIB, 60 * MIB)
MAIN_LIMIT = 48 * MIB
TAIL_LIMIT = 16 * MIB
UY = 12
UP = 12
UG = 12
UF = 8
UT = 12


def final_sums(wxo, wzi, chunks, stash):
    def first(step, ref):
        real_ref, imag_ref, row, _, _ = chunks[step]
        for group in range(2):
            ys = [row + group * 4 + k for k in range(4)]
            out = x_from_rows(wxo[...], real_ref, imag_ref, ys, YPITCH)
            for pair in range(2):
                piece = out[:, pair * LANES:(pair + 1) * LANES]
                data = jnp.concatenate([piece[:WX], piece[WX:]], axis=1)
                at = (group * 2 + pair) * WX
                ref[at:at + WX, :] = three(data, 1)

    def second(step, ref):
        _, _, _, out, pair = chunks[step]
        sums = dot(ref[...], wzi[...])
        for at in range(4):
            out[:, columns(pair + at, 1)] = sums[at * WX:(at + 1) * WX]

    pipelined(len(chunks), first, second, stash)


def main_kernel(
    count_ref, ids_ref, left_ref, own_ref, right_ref, views_hbm, otf_hbm,
    wz_ref, wzi_ref, wxf_ref, wyf_ref, wyi_ref, wxi_ref, wxe_ref, wye_ref, wyo_ref, wxo_ref,
    left_out, right_out, real_hbm, imag_hbm,
    field, total, big_real, big_imag, real, imag, lines, error, otf, image,
    wide0, wide1, thin0, thin1, last0, last1, otf_sem, image_sem, own_sem,
):
    count = count_ref[0]

    def fetch(slot):
        buffer = lax.rem(slot, 2)
        return (
            pltpu.make_async_copy(otf_hbm.at[slot], otf.at[buffer], otf_sem.at[buffer]),
            pltpu.make_async_copy(
                views_hbm.at[ids_ref[slot]], image.at[buffer], image_sem.at[buffer]
            ),
        )

    for copy in fetch(0):
        copy.start()

    def read_window(pair, pairs):
        part, pair = divmod(pair, BY // 2)
        return (left_ref, own_ref, right_ref)[part][:, columns(pair, pairs)]

    z_then_x(read_window, PY // 2, wz_ref, wxf_ref, big_real, big_imag, 1, (wide0, wide1))

    def field_y(j):
        for pair in range(UF):
            kz = (j * UF + pair) * 2
            for at, out in enumerate(y_from_rows(wyf_ref[...], big_real, big_imag, kz, PY)):
                for part in range(2):
                    field[kz + at, part] = out[part]
                    total[kz + at, part] = jnp.zeros((PY, LANES), F32)

    loop(KZ // (2 * UF), field_y)

    def view(slot, carry):
        buffer = lax.rem(slot, 2)
        for copy in fetch(slot):
            copy.wait()

        @pl.when(slot + 1 < count)
        def _():
            for copy in fetch(slot + 1):
                copy.start()

        def product(j):
            for pair in range(UP):
                kz = (j * UP + pair) * 2
                reals, imags = [], []
                for at in range(2):
                    fr, fi = field[kz + at, 0], field[kz + at, 1]
                    pr, pi = otf[buffer, kz + at, 0], otf[buffer, kz + at, 1]
                    reals.append(fr * pr - fi * pi)
                    imags.append(fr * pi + fi * pr)
                for at, out in enumerate(along_y(wyi_ref[...], reals, imags)):
                    where = pl.ds((kz + at) * YPITCH, BY)
                    real[where, :] = out[0]
                    imag[where, :] = out[1]

        loop(KZ // (2 * UP), product)

        def inverse_x(j):
            for group in range(2):
                y = j * 8 + group * 4
                out = x_from_rows(wxi_ref[...], real, imag, [y + k for k in range(4)], YPITCH)
                for pair in range(2):
                    piece = out[:, pair * LANES:(pair + 1) * LANES]
                    data = jnp.concatenate([piece[:BX], piece[BX:]], axis=1)
                    lines[aligned(j * 4 + group * 2 + pair, BX), :] = three(data, 1)

        loop(BY // 8, inverse_x, UX)

        for j in range(2):
            blurred = dot(lines[j * 8 * BX:(j + 1) * 8 * BX, :], wzi_ref[...])
            for pair in range(8):
                where = columns(j * 8 + pair, 1)
                error[:, where] = image[buffer, :, where] / blurred[pair * BX:(pair + 1) * BX] - 1.0

        def read_error(pair, pairs):
            return error[:, columns(pair, pairs)]

        z_then_x(read_error, BY // 2, wz_ref, wxe_ref, real, imag, 2, (thin0, thin1))

        def gather(j):
            for pair in range(UG):
                kz = (j * UG + pair) * 2
                for at, (er, ei) in enumerate(y_from_rows(wye_ref[...], real, imag, kz, BY)):
                    pr, pi = otf[buffer, kz + at, 0], otf[buffer, kz + at, 1]
                    total[kz + at, 0] += er * pr + ei * pi
                    total[kz + at, 1] += ei * pr - er * pi

        loop(KZ // (2 * UG), gather)
        return carry

    lax.fori_loop(0, count, view, 0)

    def inverse_y(j):
        for pair in range(UT):
            kz = (j * UT + pair) * 2
            reals = [total[kz + at, 0] for at in range(2)]
            imags = [total[kz + at, 1] for at in range(2)]
            for at, out in enumerate(along_y(wyo_ref[...], reals, imags)):
                row = (kz + at) * YPITCH
                for value, big, own in zip(out, (big_real, big_imag), (real, imag)):
                    big[pl.ds(row, BY), :] = value[:BY]
                    own[pl.ds(row, BY), :] = value[BY:2 * BY]
                    big[pl.ds(KZ * YPITCH + row, BY), :] = value[2 * BY:]

    loop(KZ // (2 * UT), inverse_y)
    copies = (
        pltpu.make_async_copy(real, real_hbm, own_sem.at[0]),
        pltpu.make_async_copy(imag, imag_hbm, own_sem.at[1]),
    )
    for copy in copies:
        copy.start()
    chunks = [
        (big_real, big_imag, side * KZ * YPITCH + y, out, y // 2)
        for side, out in enumerate((left_out, right_out))
        for y in range(0, BY, 8)
    ]
    final_sums(wxo_ref, wzi_ref, chunks, (last0, last1))
    for copy in copies:
        copy.wait()


def tail_kernel(real, imag, wzi_ref, wxo_ref, out, last0, last1):
    chunks = [(real, imag, y, out, y // 2) for y in range(0, BY, 8)]
    final_sums(wxo_ref, wzi_ref, chunks, (last0, last1))


SPECTRUM = (KZ, 2, PY, LANES)
ROWS = (KZ * YPITCH, LANES)
WIDE = (WX, BY * SZ)
LAST = pltpu.VMEM((4 * WX, 6 * LANES), BF16)
IN_VMEM = pl.BlockSpec(memory_space=pltpu.VMEM)
IN_SMEM = pl.BlockSpec(memory_space=pltpu.SMEM)
ANYWHERE = pl.BlockSpec(memory_space=pl.ANY)


def otf_call(count, ids, psf, begin, end, held=None):
    tables = (z_forward(-HALF), x_forward(K, -HALF, K), y_forward(K, -HALF))
    inputs = [count, ids, psf] + [jnp.asarray(t) for t in tables]
    specs = [IN_SMEM, IN_SMEM, ANYWHERE] + [ANYWHERE] * len(tables)
    aliases = {}
    if held is not None:
        aliases = {len(inputs): 0}
        inputs.append(held)
        specs.append(ANYWHERE)
    return pl.pallas_call(
        functools.partial(otf_kernel, begin, end),
        out_shape=jax.ShapeDtypeStruct((CMAX,) + SPECTRUM, F32),
        in_specs=specs,
        out_specs=ANYWHERE,
        scratch_shapes=[
            pltpu.VMEM((2, K, K * K), F32),
            pltpu.VMEM(SPECTRUM, F32),
            pltpu.VMEM((K * KPITCH, LANES), F32),
            pltpu.VMEM((K * KPITCH, LANES), F32),
            pltpu.VMEM((ZPO * 2 * KZ, 3 * LANES), BF16),
            pltpu.VMEM((ZPO * 2 * KZ, 3 * LANES), BF16),
        ] + room_for(tables) + [
            pltpu.SemaphoreType.DMA((2,)),
            pltpu.SemaphoreType.DMA((2 * KZ // (2 * UY),)),
            pltpu.SemaphoreType.DMA((len(tables),)),
        ],
        input_output_aliases=aliases,
        compiler_params=pltpu.CompilerParams(vmem_limit_bytes=OTF_LIMITS[0 if held is None else 1]),
        cost_estimate=pl.CostEstimate(
            flops=4 * 10**9 * (end - begin), bytes_accessed=6 * 10**6 * (end - begin), transcendentals=0
        ),
        name="otf",
    )(*inputs)


def main_call(count, ids, window, views, otf):
    left, own, right = window
    tables = (
        z_forward(0),
        z_inverse(),
        x_forward(WX, 0, LANES),
        y_forward(PY, 0),
        y_inverse(BY, HALF, two_rows),
        x_inverse(BX, HALF, two_rows),
        x_forward(BX, HALF, BX, 2),
        y_forward(BY, HALF),
        y_inverse(PY, 0, three_parts),
        x_inverse(WX, 0, three_parts),
    )
    return pl.pallas_call(
        main_kernel,
        out_shape=[jax.ShapeDtypeStruct(WIDE, F32)] * 2 + [jax.ShapeDtypeStruct(ROWS, F32)] * 2,
        in_specs=[IN_SMEM] * 2 + [IN_VMEM] * 3 + [ANYWHERE] * 2 + [IN_VMEM] * len(tables),
        out_specs=[IN_VMEM] * 2 + [ANYWHERE] * 2,
        scratch_shapes=[
            pltpu.VMEM(SPECTRUM, F32),
            pltpu.VMEM(SPECTRUM, F32),
            pltpu.VMEM((PY * KPITCH, LANES), F32),
            pltpu.VMEM((PY * KPITCH, LANES), F32),
            pltpu.VMEM(ROWS, F32),
            pltpu.VMEM(ROWS, F32),
            pltpu.VMEM((BX * BY // 2, 6 * LANES), BF16),
            pltpu.VMEM((BX, BY * SZ), F32),
            pltpu.VMEM((2,) + SPECTRUM, F32),
            pltpu.VMEM((2, BX, BY * SZ), F32),
            pltpu.VMEM((ZPF * 2 * KZ, 6 * LANES), BF16),
            pltpu.VMEM((ZPF * 2 * KZ, 6 * LANES), BF16),
            pltpu.VMEM((ZPE * KZ, 3 * LANES), BF16),
            pltpu.VMEM((ZPE * KZ, 3 * LANES), BF16),
            LAST,
            LAST,
            pltpu.SemaphoreType.DMA((2,)),
            pltpu.SemaphoreType.DMA((2,)),
            pltpu.SemaphoreType.DMA((2,)),
        ],
        compiler_params=pltpu.CompilerParams(vmem_limit_bytes=MAIN_LIMIT),
        cost_estimate=pl.CostEstimate(flops=30 * 10**9, bytes_accessed=40 * 10**6, transcendentals=0),
        name="views",
    )(count, ids, left, own, right, views, otf, *[jnp.asarray(t) for t in tables])


def tail_call(real, imag):
    tables = (z_inverse(), x_inverse(WX, 0, three_parts))
    return pl.pallas_call(
        tail_kernel,
        out_shape=jax.ShapeDtypeStruct(WIDE, F32),
        in_specs=[IN_VMEM] * 4,
        out_specs=IN_VMEM,
        scratch_shapes=[LAST, LAST],
        compiler_params=pltpu.CompilerParams(vmem_limit_bytes=TAIL_LIMIT),
        cost_estimate=pl.CostEstimate(flops=4 * 10**9, bytes_accessed=3 * 10**6, transcendentals=0),
        name="tail",
    )(real, imag, *[jnp.asarray(t) for t in tables])


def shifts(axis):
    devices = lax.axis_size(axis)
    up = [(i, i + 1) for i in range(devices - 1)]
    down = [(i + 1, i) for i in range(devices - 1)]
    return up, down


def per_device(estimate, views, psf, view_list, view_count):
    ids = view_list.reshape(V)
    count = view_count.reshape(1)
    up_x, down_x = shifts("bx")
    up_y, down_y = shifts("by")
    before = lax.ppermute(estimate, "bx", up_x)
    after = lax.ppermute(estimate, "bx", down_x)
    own = jnp.concatenate([before, estimate, after], axis=0)
    left = lax.ppermute(own, "by", up_y)
    right = lax.ppermute(own, "by", down_y)
    otf = otf_call(count, ids, psf, 0, 2)
    otf = otf_call(count, ids, psf, 2, CMAX, otf)
    left_sum, right_sum, real, imag = main_call(count, ids, (left, own, right), views, otf)
    from_right = lax.ppermute(left_sum, "by", down_y)
    from_left = lax.ppermute(right_sum, "by", up_y)
    sums = tail_call(real, imag) + from_right + from_left
    correction = (
        sums[BX:2 * BX]
        + lax.ppermute(sums[:BX], "bx", down_x)
        + lax.ppermute(sums[2 * BX:], "bx", up_x)
    )
    return estimate * (1.0 + correction / count.astype(F32))


def solution(mesh):
    return jax.shard_map(
        per_device,
        mesh=mesh,
        in_specs=(P("bx", "by"), P(None, "bx", "by"), P(), P("bx", "by", None), P("bx", "by")),
        out_specs=P("bx", "by"),
        check_vma=False,
    )
```

```python
import functools

import jax
import jax.numpy as jnp
import ml_dtypes
import numpy as np
from jax import lax
from jax.experimental import pallas as pl
from jax.experimental.pallas import tpu as pltpu
from jax.sharding import PartitionSpec as P

V = 8
K = 64
SZ = 64
HALF = K // 2
BX = 32
BY = 32
CMAX = 5
PX = 128
PY = 96
PZ = 96
KZ = PZ // 2
SLOT = 64
LANES = 128
KPITCH = KZ + 4
YPITCH = BY + 4
BIGPITCH = PY + 4
WX = BX + K
MIB = 1024 * 1024

F32 = jnp.float32
BF16 = jnp.bfloat16


def three_parts(table, axis=1):
    high = table.astype(ml_dtypes.bfloat16)
    low = (table - high.astype(np.float64)).astype(ml_dtypes.bfloat16)
    return np.concatenate([high, high, low], axis=axis)


def two_rows(table):
    high = table.astype(ml_dtypes.bfloat16)
    low = (table - high.astype(np.float64)).astype(ml_dtypes.bfloat16)
    return np.block([[high, high], [low, np.zeros_like(low)]])


def turn(frequency, position, period):
    turns = np.mod(frequency[:, None] * position[None, :], 2 * period)
    return turns * (np.pi / period)


def blocks(values, copies):
    rows, columns = values.shape
    out = np.zeros((copies, rows, copies, columns))
    for copy in range(copies):
        out[copy, :, copy, :] = values
    return out.reshape(copies * rows, copies * columns)


def z_angles(offset):
    return turn(2 * np.arange(KZ) + 1, np.arange(SZ) + offset, PZ)


def padded(values):
    return np.pad(values, ((0, 0), (0, SLOT - KZ)))


def z_forward(offset):
    angles = z_angles(offset).T
    parts = [blocks(padded(part), 2) for part in (np.cos(angles), -np.sin(angles))]
    return three_parts(np.concatenate(parts, axis=1), 0)


def z_inverse():
    angles = z_angles(0).T
    parts = [blocks(padded(part).T, 2) for part in (np.cos(angles), -np.sin(angles))]
    return three_parts(np.concatenate(parts, axis=0) * (2.0 / PZ), 0)


def x_forward(entries, offset, room, copies=1):
    angles = turn(2 * np.arange(PX), np.arange(entries) + offset, PX).T
    cosine, sine = [np.pad(f(angles), ((0, room - entries), (0, 0))) for f in (np.cos, np.sin)]
    return three_parts(blocks(np.block([[cosine, -sine], [sine, cosine]]), copies), 0)


def x_inverse(entries, offset, parts):
    angles = turn(2 * np.arange(PX), np.arange(entries) + offset, PX).T
    cosine, sine = np.cos(angles) / PX, np.sin(angles) / PX
    return parts(np.block([[cosine, -sine], [sine, cosine]]))


def y_forward(entries, offset):
    angles = turn(2 * np.arange(PY), np.arange(entries) + offset, PY)
    cosine, sine = np.cos(angles), np.sin(angles)
    return three_parts(np.block([[cosine, sine], [-sine, cosine]]), 1)


def y_inverse(entries, offset, parts):
    angles = turn(2 * np.arange(PY), np.arange(entries) + offset, PY).T
    cosine, sine = np.cos(angles) / PY, np.sin(angles) / PY
    return parts(np.block([[cosine, -sine], [sine, cosine]]))


def split(data):
    high = data.astype(BF16)
    low = (data - high.astype(F32)).astype(BF16)
    return high, low


def three(data, axis):
    high, low = split(data)
    return jnp.concatenate([high, low, high], axis=axis)


def dot(a, b):
    return lax.dot_general(a, b, (((1,), (0,)), ((), ())), preferred_element_type=F32)


def dot_nt(a, b):
    return lax.dot_general(a, b, (((1,), (1,)), ((), ())), preferred_element_type=F32)


def loop(count, body, unroll=1):
    def step(index, carry):
        for at in range(unroll):
            body(index * unroll + at)
        return carry

    lax.fori_loop(0, count // unroll, step, 0)


def aligned(index, size):
    return pl.ds(pl.multiple_of(index * size, size), size)


def columns(pair, pairs):
    return slice(pair * LANES, (pair + pairs) * LANES)


def drop_padding(rows):
    return jnp.concatenate([rows[:KZ], rows[SLOT:SLOT + KZ]], axis=0)


def z_stage(pieces, wz, copies):
    rows = pieces[0].shape[0]
    along = dot(three(jnp.concatenate(pieces, axis=0), 1), wz)
    groups = []
    for at in range(0, len(pieces), copies):
        parts = []
        for pair in range(at, at + copies):
            piece = along[pair * rows:(pair + 1) * rows]
            parts += [piece[:, :LANES], piece[:, LANES:]]
        if rows * 2 * copies > LANES:
            sides = []
            for part in parts:
                if rows < LANES:
                    part = jnp.concatenate([part, jnp.zeros((LANES - rows, LANES), F32)], axis=0)
                sides.append(drop_padding(part.T))
            groups.append(jnp.concatenate(sides, axis=1))
        else:
            groups.append(drop_padding(jnp.concatenate(parts, axis=0).T))
    return three(jnp.concatenate(groups, axis=0), 1)


def x_stage(stash, wx, real_ref, imag_ref, first_y, copies):
    across = dot(stash, wx)
    for at in range(stash.shape[0] // (2 * KZ)):
        piece = across[at * 2 * KZ:(at + 1) * 2 * KZ]
        for copy in range(copies):
            for y in range(2):
                where = pl.ds((first_y + 2 * (at * copies + copy) + y) * KPITCH, KZ)
                part = piece[y * KZ:(y + 1) * KZ]
                real_ref[where, :] = part[:, (2 * copy) * LANES:(2 * copy + 1) * LANES]
                imag_ref[where, :] = part[:, (2 * copy + 1) * LANES:(2 * copy + 2) * LANES]


def pipelined(count, first, second, stash):
    first(0, stash[0])
    for step in range(count):
        if step + 1 < count:
            first(step + 1, stash[(step + 1) % 2])
        second(step, stash[step % 2])


def z_then_x(read, count, wz, wx, real_ref, imag_ref, copies, stash, place=lambda pair: 2 * pair):
    pairs = stash[0].shape[0] // (2 * KZ) * copies

    def first(step, ref):
        data = read(step * pairs, pairs)
        pieces = [data[:, p * LANES:(p + 1) * LANES] for p in range(pairs)]
        ref[...] = z_stage(pieces, wz[...], copies)

    def second(step, ref):
        x_stage(ref[...], wx[...], real_ref, imag_ref, place(step * pairs), copies)

    pipelined(count // pairs, first, second, stash)


def along_y(table, reals, imags):
    data = jnp.concatenate(
        [jnp.concatenate(reals, axis=1), jnp.concatenate(imags, axis=1)], axis=0
    )
    if table.shape[1] == 2 * data.shape[0]:
        out = dot(table, jnp.concatenate(split(data), axis=0))
        out = out[:table.shape[0] // 2] + out[table.shape[0] // 2:]
    else:
        out = dot(table, three(data, 0))
    half = out.shape[0] // 2
    return [
        (out[:half, at * LANES:(at + 1) * LANES], out[half:, at * LANES:(at + 1) * LANES])
        for at in range(2)
    ]


def strided(ref, start, count, stride):
    return ref[pl.ds(start, count, stride=stride), :]


def y_from_rows(table, real_ref, imag_ref, kz, count):
    reals = [strided(real_ref, kz + at, count, KPITCH) for at in range(2)]
    imags = [strided(imag_ref, kz + at, count, KPITCH) for at in range(2)]
    return along_y(table, reals, imags)


def x_from_rows(table, real_ref, imag_ref, ys, stride):
    tall = table.shape[1] == 4 * LANES
    empty = jnp.zeros((SLOT - KZ, table.shape[1]), BF16)
    rows = []
    for y in ys:
        data = jnp.concatenate(
            [strided(real_ref, y, KZ, stride), strided(imag_ref, y, KZ, stride)], axis=1
        )
        rows += [jnp.concatenate(split(data), axis=1) if tall else three(data, 1), empty]
    out = dot_nt(table, jnp.concatenate(rows, axis=0))
    return out[:table.shape[0] // 2] + out[table.shape[0] // 2:] if tall else out


def table_copies(sources, targets, sems):
    return [
        pltpu.make_async_copy(source, target, sems.at[at])
        for at, (source, target) in enumerate(zip(sources, targets))
    ]


def room_for(tables):
    return [pltpu.VMEM(t.shape, BF16) for t in tables]


def otf_kernel(begin, end, count_ref, ids_ref, psf_hbm, wz_hbm, wx_hbm, wy_hbm, *rest):
    out_hbm, psf, out, real, imag, stash0, stash1, *rest = rest[-13:]
    wz_ref, wx_ref, wy_ref, psf_sem, out_sem, table_sem = rest
    steps = KZ // (2 * UY)

    def fetch(step):
        buffer = lax.rem(step, 2)
        return pltpu.make_async_copy(
            psf_hbm.at[ids_ref[begin + step]], psf.at[buffer], psf_sem.at[buffer]
        )

    def store(step, j):
        where = pl.ds(j * UY, UY)
        return pltpu.make_async_copy(
            out.at[where], out_hbm.at[begin + step, where], out_sem.at[j]
        )

    slots = jnp.maximum(jnp.minimum(count_ref[0], end) - begin, 0)

    @pl.when(slots > 0)
    def _():
        fetch(0).start()

    tables = table_copies((wz_hbm, wx_hbm, wy_hbm), (wz_ref, wx_ref, wy_ref), table_sem)
    for copy in tables:
        copy.start()
    for copy in tables:
        copy.wait()

    def body(step, carry):
        buffer = lax.rem(step, 2)
        fetch(step).wait()

        @pl.when(step + 1 < slots)
        def _():
            fetch(step + 1).start()

        def read(pair, pairs):
            return psf[buffer, :, columns(pair, pairs)]

        z_then_x(read, K // 2, wz_ref, wx_ref, real, imag, 1, (stash0, stash1))

        def y(j):
            @pl.when(step > 0)
            def _():
                store(step - 1, 2 * j).wait()
                store(step - 1, 2 * j + 1).wait()

            for pair in range(UY):
                kz = (j * UY + pair) * 2
                for at, value in enumerate(y_from_rows(wy_ref[...], real, imag, kz, K)):
                    out[kz + at, 0] = value[0]
                    out[kz + at, 1] = value[1]
                if pair == UY // 2 - 1:
                    store(step, 2 * j).start()
            store(step, 2 * j + 1).start()

        loop(steps, y)
        return carry

    lax.fori_loop(0, slots, body, 0)

    @pl.when(slots > 0)
    def _():
        for j in range(2 * steps):
            store(slots - 1, j).wait()


ZPO = 16
ZPF = 8
ZPE = 8
UX = 4
OTF_LIMITS = (60 * MIB, 60 * MIB)
MAIN_LIMIT = 48 * MIB
TAIL_LIMIT = 16 * MIB
UY = 12
UP = 12
UG = 12
UF = 8
UT = 12


def final_sums(wxo, wzi, chunks, stash):
    def first(step, ref):
        real_ref, imag_ref, row, _, _ = chunks[step]
        for group in range(2):
            ys = [row + group * 4 + k for k in range(4)]
            out = x_from_rows(wxo[...], real_ref, imag_ref, ys, YPITCH)
            for pair in range(2):
                piece = out[:, pair * LANES:(pair + 1) * LANES]
                data = jnp.concatenate([piece[:WX], piece[WX:]], axis=1)
                at = (group * 2 + pair) * WX
                ref[at:at + WX, :] = three(data, 1)

    def second(step, ref):
        _, _, _, out, pair = chunks[step]
        sums = dot(ref[...], wzi[...])
        for at in range(4):
            out[:, columns(pair + at, 1)] = sums[at * WX:(at + 1) * WX]

    pipelined(len(chunks), first, second, stash)


def main_kernel(
    count_ref, ids_ref, odd_ref, own_ref, first_ref, second_ref, views_hbm, otf_hbm,
    wz_ref, wzi_ref, wxf_ref, wyf_ref, wyi_ref, wxi_ref, wxe_ref, wye_ref, wyo_ref, wxo_ref,
    first_out, second_out, real_hbm, imag_hbm,
    field, total, big_real, big_imag, real, imag, lines, error, otf, image,
    wide0, wide1, thin0, thin1, last0, last1, otf_sem, image_sem, own_sem,
):
    count = count_ref[0]

    def fetch(slot):
        buffer = lax.rem(slot, 2)
        return (
            pltpu.make_async_copy(otf_hbm.at[slot], otf.at[buffer], otf_sem.at[buffer]),
            pltpu.make_async_copy(
                views_hbm.at[ids_ref[slot]], image.at[buffer], image_sem.at[buffer]
            ),
        )

    for copy in fetch(0):
        copy.start()

    odd = odd_ref[0]

    def read_window(pair, pairs):
        part, pair = divmod(pair, BY // 2)
        return (own_ref, first_ref, second_ref)[part][:, columns(pair, pairs)]

    def place_window(pair):
        part, pair = divmod(pair, BY // 2)
        return (1, 2 - 2 * odd, 2 * odd)[part] * BY + 2 * pair

    z_then_x(
        read_window, PY // 2, wz_ref, wxf_ref, big_real, big_imag, 1, (wide0, wide1), place_window
    )

    def field_y(j):
        for pair in range(UF):
            kz = (j * UF + pair) * 2
            for at, out in enumerate(y_from_rows(wyf_ref[...], big_real, big_imag, kz, PY)):
                for part in range(2):
                    field[kz + at, part] = out[part]
                    total[kz + at, part] = jnp.zeros((PY, LANES), F32)

    loop(KZ // (2 * UF), field_y)

    def view(slot, carry):
        buffer = lax.rem(slot, 2)
        for copy in fetch(slot):
            copy.wait()

        @pl.when(slot + 1 < count)
        def _():
            for copy in fetch(slot + 1):
                copy.start()

        def product(j):
            for pair in range(UP):
                kz = (j * UP + pair) * 2
                reals, imags = [], []
                for at in range(2):
                    fr, fi = field[kz + at, 0], field[kz + at, 1]
                    pr, pi = otf[buffer, kz + at, 0], otf[buffer, kz + at, 1]
                    reals.append(fr * pr - fi * pi)
                    imags.append(fr * pi + fi * pr)
                for at, out in enumerate(along_y(wyi_ref[...], reals, imags)):
                    where = pl.ds((kz + at) * YPITCH, BY)
                    real[where, :] = out[0]
                    imag[where, :] = out[1]

        loop(KZ // (2 * UP), product)

        def inverse_x(j):
            for group in range(2):
                y = j * 8 + group * 4
                out = x_from_rows(wxi_ref[...], real, imag, [y + k for k in range(4)], YPITCH)
                for pair in range(2):
                    piece = out[:, pair * LANES:(pair + 1) * LANES]
                    data = jnp.concatenate([piece[:BX], piece[BX:]], axis=1)
                    lines[aligned(j * 4 + group * 2 + pair, BX), :] = three(data, 1)

        loop(BY // 8, inverse_x, UX)

        for j in range(2):
            blurred = dot(lines[j * 8 * BX:(j + 1) * 8 * BX, :], wzi_ref[...])
            for pair in range(8):
                where = columns(j * 8 + pair, 1)
                error[:, where] = image[buffer, :, where] / blurred[pair * BX:(pair + 1) * BX] - 1.0

        def read_error(pair, pairs):
            return error[:, columns(pair, pairs)]

        z_then_x(read_error, BY // 2, wz_ref, wxe_ref, real, imag, 2, (thin0, thin1))

        def gather(j):
            for pair in range(UG):
                kz = (j * UG + pair) * 2
                for at, (er, ei) in enumerate(y_from_rows(wye_ref[...], real, imag, kz, BY)):
                    pr, pi = otf[buffer, kz + at, 0], otf[buffer, kz + at, 1]
                    total[kz + at, 0] += er * pr + ei * pi
                    total[kz + at, 1] += ei * pr - er * pi

        loop(KZ // (2 * UG), gather)
        return carry

    lax.fori_loop(0, count, view, 0)

    def inverse_y(j):
        for pair in range(UT):
            kz = (j * UT + pair) * 2
            reals = [total[kz + at, 0] for at in range(2)]
            imags = [total[kz + at, 1] for at in range(2)]
            for at, out in enumerate(along_y(wyo_ref[...], reals, imags)):
                row = (kz + at) * YPITCH
                for value, big, own in zip(out, (big_real, big_imag), (real, imag)):
                    big[pl.ds(row, BY), :] = value[:BY]
                    own[pl.ds(row, BY), :] = value[BY:2 * BY]
                    big[pl.ds(KZ * YPITCH + row, BY), :] = value[2 * BY:]

    loop(KZ // (2 * UT), inverse_y)
    copies = (
        pltpu.make_async_copy(real, real_hbm, own_sem.at[0]),
        pltpu.make_async_copy(imag, imag_hbm, own_sem.at[1]),
    )
    for copy in copies:
        copy.start()
    chunks = [
        (big_real, big_imag, side * KZ * YPITCH + y, out, y // 2)
        for side, out in ((1 - odd, first_out), (odd, second_out))
        for y in range(0, BY, 8)
    ]
    final_sums(wxo_ref, wzi_ref, chunks, (last0, last1))
    for copy in copies:
        copy.wait()


def tail_kernel(real, imag, wzi_ref, wxo_ref, out, last0, last1):
    chunks = [(real, imag, y, out, y // 2) for y in range(0, BY, 8)]
    final_sums(wxo_ref, wzi_ref, chunks, (last0, last1))


SPECTRUM = (KZ, 2, PY, LANES)
ROWS = (KZ * YPITCH, LANES)
WIDE = (WX, BY * SZ)
LAST = pltpu.VMEM((4 * WX, 6 * LANES), BF16)
IN_VMEM = pl.BlockSpec(memory_space=pltpu.VMEM)
IN_SMEM = pl.BlockSpec(memory_space=pltpu.SMEM)
ANYWHERE = pl.BlockSpec(memory_space=pl.ANY)


def otf_call(count, ids, psf, begin, end, held=None):
    tables = (z_forward(-HALF), x_forward(K, -HALF, K), y_forward(K, -HALF))
    inputs = [count, ids, psf] + [jnp.asarray(t) for t in tables]
    specs = [IN_SMEM, IN_SMEM, ANYWHERE] + [ANYWHERE] * len(tables)
    aliases = {}
    if held is not None:
        aliases = {len(inputs): 0}
        inputs.append(held)
        specs.append(ANYWHERE)
    return pl.pallas_call(
        functools.partial(otf_kernel, begin, end),
        out_shape=jax.ShapeDtypeStruct((CMAX,) + SPECTRUM, F32),
        in_specs=specs,
        out_specs=ANYWHERE,
        scratch_shapes=[
            pltpu.VMEM((2, K, K * K), F32),
            pltpu.VMEM(SPECTRUM, F32),
            pltpu.VMEM((K * KPITCH, LANES), F32),
            pltpu.VMEM((K * KPITCH, LANES), F32),
            pltpu.VMEM((ZPO * 2 * KZ, 3 * LANES), BF16),
            pltpu.VMEM((ZPO * 2 * KZ, 3 * LANES), BF16),
        ] + room_for(tables) + [
            pltpu.SemaphoreType.DMA((2,)),
            pltpu.SemaphoreType.DMA((2 * KZ // (2 * UY),)),
            pltpu.SemaphoreType.DMA((len(tables),)),
        ],
        input_output_aliases=aliases,
        compiler_params=pltpu.CompilerParams(vmem_limit_bytes=OTF_LIMITS[0 if held is None else 1]),
        cost_estimate=pl.CostEstimate(
            flops=4 * 10**9 * (end - begin), bytes_accessed=6 * 10**6 * (end - begin), transcendentals=0
        ),
        name="otf",
    )(*inputs)


def main_call(count, ids, odd, window, views, otf):
    own, first, second = window
    tables = (
        z_forward(0),
        z_inverse(),
        x_forward(WX, 0, LANES),
        y_forward(PY, 0),
        y_inverse(BY, HALF, two_rows),
        x_inverse(BX, HALF, two_rows),
        x_forward(BX, HALF, BX, 2),
        y_forward(BY, HALF),
        y_inverse(PY, 0, three_parts),
        x_inverse(WX, 0, three_parts),
    )
    return pl.pallas_call(
        main_kernel,
        out_shape=[jax.ShapeDtypeStruct(WIDE, F32)] * 2 + [jax.ShapeDtypeStruct(ROWS, F32)] * 2,
        in_specs=[IN_SMEM] * 3 + [IN_VMEM] * 3 + [ANYWHERE] * 2 + [IN_VMEM] * len(tables),
        out_specs=[IN_VMEM] * 2 + [ANYWHERE] * 2,
        scratch_shapes=[
            pltpu.VMEM(SPECTRUM, F32),
            pltpu.VMEM(SPECTRUM, F32),
            pltpu.VMEM((PY * KPITCH, LANES), F32),
            pltpu.VMEM((PY * KPITCH, LANES), F32),
            pltpu.VMEM(ROWS, F32),
            pltpu.VMEM(ROWS, F32),
            pltpu.VMEM((BX * BY // 2, 6 * LANES), BF16),
            pltpu.VMEM((BX, BY * SZ), F32),
            pltpu.VMEM((2,) + SPECTRUM, F32),
            pltpu.VMEM((2, BX, BY * SZ), F32),
            pltpu.VMEM((ZPF * 2 * KZ, 6 * LANES), BF16),
            pltpu.VMEM((ZPF * 2 * KZ, 6 * LANES), BF16),
            pltpu.VMEM((ZPE * KZ, 3 * LANES), BF16),
            pltpu.VMEM((ZPE * KZ, 3 * LANES), BF16),
            LAST,
            LAST,
            pltpu.SemaphoreType.DMA((2,)),
            pltpu.SemaphoreType.DMA((2,)),
            pltpu.SemaphoreType.DMA((2,)),
        ],
        compiler_params=pltpu.CompilerParams(vmem_limit_bytes=MAIN_LIMIT),
        cost_estimate=pl.CostEstimate(flops=30 * 10**9, bytes_accessed=40 * 10**6, transcendentals=0),
        name="views",
    )(count, ids, odd, own, first, second, views, otf, *[jnp.asarray(t) for t in tables])


def tail_call(real, imag):
    tables = (z_inverse(), x_inverse(WX, 0, three_parts))
    return pl.pallas_call(
        tail_kernel,
        out_shape=jax.ShapeDtypeStruct(WIDE, F32),
        in_specs=[IN_VMEM] * 4,
        out_specs=IN_VMEM,
        scratch_shapes=[LAST, LAST],
        compiler_params=pltpu.CompilerParams(vmem_limit_bytes=TAIL_LIMIT),
        cost_estimate=pl.CostEstimate(flops=4 * 10**9, bytes_accessed=3 * 10**6, transcendentals=0),
        name="tail",
    )(real, imag, *[jnp.asarray(t) for t in tables])


def swaps(axis):
    devices = lax.axis_size(axis)
    first = [(i, i ^ 1) for i in range(devices) if i ^ 1 < devices]
    second = [(i, i + 1 if i % 2 else i - 1) for i in range(1, devices)]
    second = [(i, j) for i, j in second if j < devices]
    return lax.rem(lax.axis_index(axis), 2), first, second


def per_device(estimate, views, psf, view_list, view_count):
    ids = view_list.reshape(V)
    count = view_count.reshape(1)
    odd_x, first_x, second_x = swaps("bx")
    odd_y, first_y, second_y = swaps("by")
    one = lax.ppermute(estimate, "bx", first_x)
    other = lax.ppermute(estimate, "bx", second_x)
    before = jnp.where(odd_x == 1, one, other)
    after = jnp.where(odd_x == 1, other, one)
    own = jnp.concatenate([before, estimate, after], axis=0)
    window = (own, lax.ppermute(own, "by", first_y), lax.ppermute(own, "by", second_y))
    otf = otf_call(count, ids, psf, 0, 2)
    otf = otf_call(count, ids, psf, 2, CMAX, otf)
    rim, other_rim, real, imag = main_call(count, ids, odd_y.reshape(1), window, views, otf)
    one = lax.ppermute(rim, "by", first_y)
    other = lax.ppermute(other_rim, "by", second_y)
    sums = tail_call(real, imag) + one + other
    low, high = sums[:BX], sums[2 * BX:]
    one = lax.ppermute(jnp.where(odd_x == 1, low, high), "bx", first_x)
    other = lax.ppermute(jnp.where(odd_x == 1, high, low), "bx", second_x)
    correction = sums[BX:2 * BX] + one + other
    return estimate * (1.0 + correction / count.astype(F32))


def solution(mesh):
    return jax.shard_map(
        per_device,
        mesh=mesh,
        in_specs=(P("bx", "by"), P(None, "bx", "by"), P(), P("bx", "by", None), P("bx", "by")),
        out_specs=P("bx", "by"),
        check_vma=False,
    )
```

```python
import functools

import jax
import jax.numpy as jnp
import ml_dtypes
import numpy as np
from jax import lax
from jax.experimental import pallas as pl
from jax.experimental.pallas import tpu as pltpu
from jax.sharding import PartitionSpec as P

V = 8
K = 64
SZ = 64
HALF = K // 2
BX = 32
BY = 32
CMAX = 5
PX = 128
PY = 96
PZ = 96
KZ = PZ // 2
SLOT = 64
LANES = 128
KPITCH = KZ + 4
YPITCH = BY + 4
BIGPITCH = PY + 4
WX = BX + K
MIB = 1024 * 1024

F32 = jnp.float32
BF16 = jnp.bfloat16


def three_parts(table, axis=1):
    high = table.astype(ml_dtypes.bfloat16)
    low = (table - high.astype(np.float64)).astype(ml_dtypes.bfloat16)
    return np.concatenate([high, high, low], axis=axis)


def two_rows(table):
    high = table.astype(ml_dtypes.bfloat16)
    low = (table - high.astype(np.float64)).astype(ml_dtypes.bfloat16)
    return np.block([[high, high], [low, np.zeros_like(low)]])


def turn(frequency, position, period):
    turns = np.mod(frequency[:, None] * position[None, :], 2 * period)
    return turns * (np.pi / period)


def blocks(values, copies):
    rows, columns = values.shape
    out = np.zeros((copies, rows, copies, columns))
    for copy in range(copies):
        out[copy, :, copy, :] = values
    return out.reshape(copies * rows, copies * columns)


def z_angles(offset):
    return turn(2 * np.arange(KZ) + 1, np.arange(SZ) + offset, PZ)


def padded(values):
    return np.pad(values, ((0, 0), (0, SLOT - KZ)))


def z_forward(offset):
    angles = z_angles(offset).T
    parts = [blocks(padded(part), 2) for part in (np.cos(angles), -np.sin(angles))]
    return three_parts(np.concatenate(parts, axis=1), 0)


def z_inverse():
    angles = z_angles(0).T
    parts = [blocks(padded(part).T, 2) for part in (np.cos(angles), -np.sin(angles))]
    return three_parts(np.concatenate(parts, axis=0) * (2.0 / PZ), 0)


def x_forward(entries, offset, room, copies=1):
    angles = turn(2 * np.arange(PX), np.arange(entries) + offset, PX).T
    cosine, sine = [np.pad(f(angles), ((0, room - entries), (0, 0))) for f in (np.cos, np.sin)]
    return three_parts(blocks(np.block([[cosine, -sine], [sine, cosine]]), copies), 0)


def x_inverse(entries, offset, parts):
    angles = turn(2 * np.arange(PX), np.arange(entries) + offset, PX).T
    cosine, sine = np.cos(angles) / PX, np.sin(angles) / PX
    return parts(np.block([[cosine, -sine], [sine, cosine]]))


def y_forward(entries, offset):
    angles = turn(2 * np.arange(PY), np.arange(entries) + offset, PY)
    cosine, sine = np.cos(angles), np.sin(angles)
    return three_parts(np.block([[cosine, sine], [-sine, cosine]]), 1)


def y_inverse(entries, offset, parts):
    angles = turn(2 * np.arange(PY), np.arange(entries) + offset, PY).T
    cosine, sine = np.cos(angles) / PY, np.sin(angles) / PY
    return parts(np.block([[cosine, -sine], [sine, cosine]]))


def split(data):
    high = data.astype(BF16)
    low = (data - high.astype(F32)).astype(BF16)
    return high, low


def three(data, axis):
    high, low = split(data)
    return jnp.concatenate([high, low, high], axis=axis)


def dot(a, b):
    return lax.dot_general(a, b, (((1,), (0,)), ((), ())), preferred_element_type=F32)


def dot_nt(a, b):
    return lax.dot_general(a, b, (((1,), (1,)), ((), ())), preferred_element_type=F32)


def loop(count, body, unroll=1):
    def step(index, carry):
        for at in range(unroll):
            body(index * unroll + at)
        return carry

    lax.fori_loop(0, count // unroll, step, 0)


def aligned(index, size):
    return pl.ds(pl.multiple_of(index * size, size), size)


def columns(pair, pairs):
    return slice(pair * LANES, (pair + pairs) * LANES)


def drop_padding(rows):
    return jnp.concatenate([rows[:KZ], rows[SLOT:SLOT + KZ]], axis=0)


def z_stage(pieces, wz, copies):
    rows = pieces[0].shape[0]
    along = dot(three(jnp.concatenate(pieces, axis=0), 1), wz)
    groups = []
    for at in range(0, len(pieces), copies):
        parts = []
        for pair in range(at, at + copies):
            piece = along[pair * rows:(pair + 1) * rows]
            parts += [piece[:, :LANES], piece[:, LANES:]]
        if rows * 2 * copies > LANES:
            sides = []
            for part in parts:
                if rows < LANES:
                    part = jnp.concatenate([part, jnp.zeros((LANES - rows, LANES), F32)], axis=0)
                sides.append(drop_padding(part.T))
            groups.append(jnp.concatenate(sides, axis=1))
        else:
            groups.append(drop_padding(jnp.concatenate(parts, axis=0).T))
    return three(jnp.concatenate(groups, axis=0), 1)


def x_stage(stash, wx, real_ref, imag_ref, first_y, copies):
    across = dot(stash, wx)
    for at in range(stash.shape[0] // (2 * KZ)):
        piece = across[at * 2 * KZ:(at + 1) * 2 * KZ]
        for copy in range(copies):
            for y in range(2):
                where = pl.ds((first_y + 2 * (at * copies + copy) + y) * KPITCH, KZ)
                part = piece[y * KZ:(y + 1) * KZ]
                real_ref[where, :] = part[:, (2 * copy) * LANES:(2 * copy + 1) * LANES]
                imag_ref[where, :] = part[:, (2 * copy + 1) * LANES:(2 * copy + 2) * LANES]


def pipelined(count, first, second, stash):
    first(0, stash[0])
    for step in range(count):
        if step + 1 < count:
            first(step + 1, stash[(step + 1) % 2])
        second(step, stash[step % 2])


def z_then_x(read, count, wz, wx, real_ref, imag_ref, copies, stash, place=lambda pair: 2 * pair):
    pairs = stash[0].shape[0] // (2 * KZ) * copies

    def first(step, ref):
        data = read(step * pairs, pairs)
        pieces = [data[:, p * LANES:(p + 1) * LANES] for p in range(pairs)]
        ref[...] = z_stage(pieces, wz[...], copies)

    def second(step, ref):
        x_stage(ref[...], wx[...], real_ref, imag_ref, place(step * pairs), copies)

    pipelined(count // pairs, first, second, stash)


def along_y(table, reals, imags):
    data = jnp.concatenate(
        [jnp.concatenate(reals, axis=1), jnp.concatenate(imags, axis=1)], axis=0
    )
    if table.shape[1] == 2 * data.shape[0]:
        out = dot(table, jnp.concatenate(split(data), axis=0))
        out = out[:table.shape[0] // 2] + out[table.shape[0] // 2:]
    else:
        out = dot(table, three(data, 0))
    half = out.shape[0] // 2
    return [
        (out[:half, at * LANES:(at + 1) * LANES], out[half:, at * LANES:(at + 1) * LANES])
        for at in range(2)
    ]


def strided(ref, start, count, stride):
    return ref[pl.ds(start, count, stride=stride), :]


def y_from_rows(table, real_ref, imag_ref, kz, count):
    reals = [strided(real_ref, kz + at, count, KPITCH) for at in range(2)]
    imags = [strided(imag_ref, kz + at, count, KPITCH) for at in range(2)]
    return along_y(table, reals, imags)


def x_from_rows(table, real_ref, imag_ref, ys, stride):
    tall = table.shape[1] == 4 * LANES
    empty = jnp.zeros((SLOT - KZ, table.shape[1]), BF16)
    rows = []
    for y in ys:
        data = jnp.concatenate(
            [strided(real_ref, y, KZ, stride), strided(imag_ref, y, KZ, stride)], axis=1
        )
        rows += [jnp.concatenate(split(data), axis=1) if tall else three(data, 1), empty]
    out = dot_nt(table, jnp.concatenate(rows, axis=0))
    return out[:table.shape[0] // 2] + out[table.shape[0] // 2:] if tall else out


def table_copies(sources, targets, sems):
    return [
        pltpu.make_async_copy(source, target, sems.at[at])
        for at, (source, target) in enumerate(zip(sources, targets))
    ]


def room_for(tables):
    return [pltpu.VMEM(t.shape, BF16) for t in tables]


def otf_kernel(begin, end, count_ref, ids_ref, psf_hbm, wz_hbm, wx_hbm, wy_hbm, *rest):
    out_hbm, psf, out, real, imag, stash0, stash1, *rest = rest[-13:]
    wz_ref, wx_ref, wy_ref, psf_sem, out_sem, table_sem = rest
    steps = KZ // (2 * UY)

    def fetch(step):
        buffer = lax.rem(step, 2)
        return pltpu.make_async_copy(
            psf_hbm.at[ids_ref[begin + step]], psf.at[buffer], psf_sem.at[buffer]
        )

    def store(step, j):
        where = pl.ds(j * UY, UY)
        return pltpu.make_async_copy(
            out.at[where], out_hbm.at[begin + step, where], out_sem.at[j]
        )

    slots = jnp.maximum(jnp.minimum(count_ref[0], end) - begin, 0)

    @pl.when(slots > 0)
    def _():
        fetch(0).start()

    tables = table_copies((wz_hbm, wx_hbm, wy_hbm), (wz_ref, wx_ref, wy_ref), table_sem)
    for copy in tables:
        copy.start()
    for copy in tables:
        copy.wait()

    def body(step, carry):
        buffer = lax.rem(step, 2)
        fetch(step).wait()

        @pl.when(step + 1 < slots)
        def _():
            fetch(step + 1).start()

        def read(pair, pairs):
            return psf[buffer, :, columns(pair, pairs)]

        z_then_x(read, K // 2, wz_ref, wx_ref, real, imag, 1, (stash0, stash1))

        def y(j):
            @pl.when(step > 0)
            def _():
                store(step - 1, 2 * j).wait()
                store(step - 1, 2 * j + 1).wait()

            for pair in range(UY):
                kz = (j * UY + pair) * 2
                for at, value in enumerate(y_from_rows(wy_ref[...], real, imag, kz, K)):
                    out[kz + at, 0] = value[0]
                    out[kz + at, 1] = value[1]
                if pair == UY // 2 - 1:
                    store(step, 2 * j).start()
            store(step, 2 * j + 1).start()

        loop(steps, y)
        return carry

    lax.fori_loop(0, slots, body, 0)

    @pl.when(slots > 0)
    def _():
        for j in range(2 * steps):
            store(slots - 1, j).wait()


ZPO = 16
ZPF = 8
ZPE = 8
UX = 4
OTF_LIMITS = (60 * MIB, 60 * MIB)
MAIN_LIMIT = 48 * MIB
TAIL_LIMIT = 16 * MIB
UY = 12
UP = 12
UG = 12
UF = 8
UT = 12


def final_sums(wxo, wzi, chunks, stash):
    def first(step, ref):
        real_ref, imag_ref, row, _, _ = chunks[step]
        for group in range(2):
            ys = [row + group * 4 + k for k in range(4)]
            out = x_from_rows(wxo[...], real_ref, imag_ref, ys, YPITCH)
            for pair in range(2):
                piece = out[:, pair * LANES:(pair + 1) * LANES]
                data = jnp.concatenate([piece[:WX], piece[WX:]], axis=1)
                at = (group * 2 + pair) * WX
                ref[at:at + WX, :] = three(data, 1)

    def second(step, ref):
        _, _, _, out, pair = chunks[step]
        sums = dot(ref[...], wzi[...])
        for at in range(4):
            lanes, part = columns(pair + at, 1), sums[at * WX:(at + 1) * WX]
            if len(out) == 1:
                out[0][:, lanes] = part
            else:
                out[0][:BX, lanes] = part[:BX]
                out[0][BX:, lanes] = part[2 * BX:]
                out[1][:, lanes] = part[BX:2 * BX]

    pipelined(len(chunks), first, second, stash)


def main_kernel(
    count_ref, ids_ref, odd_ref, own_ref, first_ref, second_ref, views_hbm, otf_hbm,
    wz_ref, wzi_ref, wxf_ref, wyf_ref, wyi_ref, wxi_ref, wxe_ref, wye_ref, wyo_ref, wxo_ref,
    first_out, outer_out, inner_out, real_hbm, imag_hbm,
    field, total, big_real, big_imag, real, imag, lines, error, otf, image,
    wide0, wide1, thin0, thin1, last0, last1, otf_sem, image_sem, own_sem,
):
    count = count_ref[0]

    def fetch(slot):
        buffer = lax.rem(slot, 2)
        return (
            pltpu.make_async_copy(otf_hbm.at[slot], otf.at[buffer], otf_sem.at[buffer]),
            pltpu.make_async_copy(
                views_hbm.at[ids_ref[slot]], image.at[buffer], image_sem.at[buffer]
            ),
        )

    for copy in fetch(0):
        copy.start()

    odd = odd_ref[0]

    def read_window(pair, pairs):
        part, pair = divmod(pair, BY // 2)
        return (own_ref, first_ref, second_ref)[part][:, columns(pair, pairs)]

    def place_window(pair):
        part, pair = divmod(pair, BY // 2)
        return (1, 2 - 2 * odd, 2 * odd)[part] * BY + 2 * pair

    z_then_x(
        read_window, PY // 2, wz_ref, wxf_ref, big_real, big_imag, 1, (wide0, wide1), place_window
    )

    def field_y(j):
        for pair in range(UF):
            kz = (j * UF + pair) * 2
            for at, out in enumerate(y_from_rows(wyf_ref[...], big_real, big_imag, kz, PY)):
                for part in range(2):
                    field[kz + at, part] = out[part]
                    total[kz + at, part] = jnp.zeros((PY, LANES), F32)

    loop(KZ // (2 * UF), field_y)

    def view(slot, carry):
        buffer = lax.rem(slot, 2)
        for copy in fetch(slot):
            copy.wait()

        @pl.when(slot + 1 < count)
        def _():
            for copy in fetch(slot + 1):
                copy.start()

        def product(j):
            for pair in range(UP):
                kz = (j * UP + pair) * 2
                reals, imags = [], []
                for at in range(2):
                    fr, fi = field[kz + at, 0], field[kz + at, 1]
                    pr, pi = otf[buffer, kz + at, 0], otf[buffer, kz + at, 1]
                    reals.append(fr * pr - fi * pi)
                    imags.append(fr * pi + fi * pr)
                for at, out in enumerate(along_y(wyi_ref[...], reals, imags)):
                    where = pl.ds((kz + at) * YPITCH, BY)
                    real[where, :] = out[0]
                    imag[where, :] = out[1]

        loop(KZ // (2 * UP), product)

        def inverse_x(j):
            for group in range(2):
                y = j * 8 + group * 4
                out = x_from_rows(wxi_ref[...], real, imag, [y + k for k in range(4)], YPITCH)
                for pair in range(2):
                    piece = out[:, pair * LANES:(pair + 1) * LANES]
                    data = jnp.concatenate([piece[:BX], piece[BX:]], axis=1)
                    lines[aligned(j * 4 + group * 2 + pair, BX), :] = three(data, 1)

        loop(BY // 8, inverse_x, UX)

        for j in range(2):
            blurred = dot(lines[j * 8 * BX:(j + 1) * 8 * BX, :], wzi_ref[...])
            for pair in range(8):
                where = columns(j * 8 + pair, 1)
                error[:, where] = image[buffer, :, where] / blurred[pair * BX:(pair + 1) * BX] - 1.0

        def read_error(pair, pairs):
            return error[:, columns(pair, pairs)]

        z_then_x(read_error, BY // 2, wz_ref, wxe_ref, real, imag, 2, (thin0, thin1))

        def gather(j):
            for pair in range(UG):
                kz = (j * UG + pair) * 2
                for at, (er, ei) in enumerate(y_from_rows(wye_ref[...], real, imag, kz, BY)):
                    pr, pi = otf[buffer, kz + at, 0], otf[buffer, kz + at, 1]
                    total[kz + at, 0] += er * pr + ei * pi
                    total[kz + at, 1] += ei * pr - er * pi

        loop(KZ // (2 * UG), gather)
        return carry

    lax.fori_loop(0, count, view, 0)

    def inverse_y(j):
        for pair in range(UT):
            kz = (j * UT + pair) * 2
            reals = [total[kz + at, 0] for at in range(2)]
            imags = [total[kz + at, 1] for at in range(2)]
            for at, out in enumerate(along_y(wyo_ref[...], reals, imags)):
                row = (kz + at) * YPITCH
                for value, big, own in zip(out, (big_real, big_imag), (real, imag)):
                    big[pl.ds(row, BY), :] = value[:BY]
                    own[pl.ds(row, BY), :] = value[BY:2 * BY]
                    big[pl.ds(KZ * YPITCH + row, BY), :] = value[2 * BY:]

    loop(KZ // (2 * UT), inverse_y)
    copies = (
        pltpu.make_async_copy(real, real_hbm, own_sem.at[0]),
        pltpu.make_async_copy(imag, imag_hbm, own_sem.at[1]),
    )
    for copy in copies:
        copy.start()
    chunks = [
        (big_real, big_imag, side * KZ * YPITCH + y, out, y // 2)
        for side, out in ((odd, (outer_out, inner_out)), (1 - odd, (first_out,)))
        for y in range(0, BY, 8)
    ]
    final_sums(wxo_ref, wzi_ref, chunks, (last0, last1))
    for copy in copies:
        copy.wait()


def tail_kernel(real, imag, wzi_ref, wxo_ref, out, last0, last1):
    chunks = [(real, imag, y, (out,), y // 2) for y in range(0, BY, 8)]
    final_sums(wxo_ref, wzi_ref, chunks, (last0, last1))


SPECTRUM = (KZ, 2, PY, LANES)
ROWS = (KZ * YPITCH, LANES)
WIDE = (WX, BY * SZ)
LAST = pltpu.VMEM((4 * WX, 6 * LANES), BF16)
IN_VMEM = pl.BlockSpec(memory_space=pltpu.VMEM)
IN_SMEM = pl.BlockSpec(memory_space=pltpu.SMEM)
ANYWHERE = pl.BlockSpec(memory_space=pl.ANY)


def otf_call(count, ids, psf, begin, end, held=None):
    tables = (z_forward(-HALF), x_forward(K, -HALF, K), y_forward(K, -HALF))
    inputs = [count, ids, psf] + [jnp.asarray(t) for t in tables]
    specs = [IN_SMEM, IN_SMEM, ANYWHERE] + [ANYWHERE] * len(tables)
    aliases = {}
    if held is not None:
        aliases = {len(inputs): 0}
        inputs.append(held)
        specs.append(ANYWHERE)
    return pl.pallas_call(
        functools.partial(otf_kernel, begin, end),
        out_shape=jax.ShapeDtypeStruct((CMAX,) + SPECTRUM, F32),
        in_specs=specs,
        out_specs=ANYWHERE,
        scratch_shapes=[
            pltpu.VMEM((2, K, K * K), F32),
            pltpu.VMEM(SPECTRUM, F32),
            pltpu.VMEM((K * KPITCH, LANES), F32),
            pltpu.VMEM((K * KPITCH, LANES), F32),
            pltpu.VMEM((ZPO * 2 * KZ, 3 * LANES), BF16),
            pltpu.VMEM((ZPO * 2 * KZ, 3 * LANES), BF16),
        ] + room_for(tables) + [
            pltpu.SemaphoreType.DMA((2,)),
            pltpu.SemaphoreType.DMA((2 * KZ // (2 * UY),)),
            pltpu.SemaphoreType.DMA((len(tables),)),
        ],
        input_output_aliases=aliases,
        compiler_params=pltpu.CompilerParams(vmem_limit_bytes=OTF_LIMITS[0 if held is None else 1]),
        cost_estimate=pl.CostEstimate(
            flops=4 * 10**9 * (end - begin), bytes_accessed=6 * 10**6 * (end - begin), transcendentals=0
        ),
        name="otf",
    )(*inputs)


def main_call(count, ids, odd, window, views, otf):
    own, first, second = window
    tables = (
        z_forward(0),
        z_inverse(),
        x_forward(WX, 0, LANES),
        y_forward(PY, 0),
        y_inverse(BY, HALF, two_rows),
        x_inverse(BX, HALF, two_rows),
        x_forward(BX, HALF, BX, 2),
        y_forward(BY, HALF),
        y_inverse(PY, 0, three_parts),
        x_inverse(WX, 0, three_parts),
    )
    return pl.pallas_call(
        main_kernel,
        out_shape=[
            jax.ShapeDtypeStruct(shape, F32)
            for shape in (WIDE, (2 * BX, BY * SZ), (BX, BY * SZ), ROWS, ROWS)
        ],
        in_specs=[IN_SMEM] * 3 + [IN_VMEM] * 3 + [ANYWHERE] * 2 + [IN_VMEM] * len(tables),
        out_specs=[IN_VMEM] * 3 + [ANYWHERE] * 2,
        scratch_shapes=[
            pltpu.VMEM(SPECTRUM, F32),
            pltpu.VMEM(SPECTRUM, F32),
            pltpu.VMEM((PY * KPITCH, LANES), F32),
            pltpu.VMEM((PY * KPITCH, LANES), F32),
            pltpu.VMEM(ROWS, F32),
            pltpu.VMEM(ROWS, F32),
            pltpu.VMEM((BX * BY // 2, 6 * LANES), BF16),
            pltpu.VMEM((BX, BY * SZ), F32),
            pltpu.VMEM((2,) + SPECTRUM, F32),
            pltpu.VMEM((2, BX, BY * SZ), F32),
            pltpu.VMEM((ZPF * 2 * KZ, 6 * LANES), BF16),
            pltpu.VMEM((ZPF * 2 * KZ, 6 * LANES), BF16),
            pltpu.VMEM((ZPE * KZ, 3 * LANES), BF16),
            pltpu.VMEM((ZPE * KZ, 3 * LANES), BF16),
            LAST,
            LAST,
            pltpu.SemaphoreType.DMA((2,)),
            pltpu.SemaphoreType.DMA((2,)),
            pltpu.SemaphoreType.DMA((2,)),
        ],
        compiler_params=pltpu.CompilerParams(vmem_limit_bytes=MAIN_LIMIT),
        cost_estimate=pl.CostEstimate(flops=30 * 10**9, bytes_accessed=40 * 10**6, transcendentals=0),
        name="views",
    )(count, ids, odd, own, first, second, views, otf, *[jnp.asarray(t) for t in tables])


def tail_call(real, imag):
    tables = (z_inverse(), x_inverse(WX, 0, three_parts))
    return pl.pallas_call(
        tail_kernel,
        out_shape=jax.ShapeDtypeStruct(WIDE, F32),
        in_specs=[IN_VMEM] * 4,
        out_specs=IN_VMEM,
        scratch_shapes=[LAST, LAST],
        compiler_params=pltpu.CompilerParams(vmem_limit_bytes=TAIL_LIMIT),
        cost_estimate=pl.CostEstimate(flops=4 * 10**9, bytes_accessed=3 * 10**6, transcendentals=0),
        name="tail",
    )(real, imag, *[jnp.asarray(t) for t in tables])


def swaps(axis):
    devices = lax.axis_size(axis)
    first = [(i, i ^ 1) for i in range(devices) if i ^ 1 < devices]
    second = [(i, i + 1 if i % 2 else i - 1) for i in range(1, devices)]
    second = [(i, j) for i, j in second if j < devices]
    return lax.rem(lax.axis_index(axis), 2), first, second


def per_device(estimate, views, psf, view_list, view_count):
    ids = view_list.reshape(V)
    count = view_count.reshape(1)
    odd_x, first_x, second_x = swaps("bx")
    odd_y, first_y, second_y = swaps("by")
    one = lax.ppermute(estimate, "bx", first_x)
    other = lax.ppermute(estimate, "bx", second_x)
    before = jnp.where(odd_x == 1, one, other)
    after = jnp.where(odd_x == 1, other, one)
    own = jnp.concatenate([before, estimate, after], axis=0)
    window = (own, lax.ppermute(own, "by", first_y), lax.ppermute(own, "by", second_y))
    otf = otf_call(count, ids, psf, 0, 2)
    otf = otf_call(count, ids, psf, 2, CMAX, otf)
    rim, outer, inner, real, imag = main_call(
        count, ids, odd_y.reshape(1), window, views, otf
    )
    other_outer = lax.ppermute(outer, "by", second_y)
    one = lax.ppermute(rim, "by", first_y)
    other_inner = lax.ppermute(inner, "by", second_y)
    sums = tail_call(real, imag) + one
    low = sums[:BX] + other_outer[:BX]
    high = sums[2 * BX:] + other_outer[BX:]
    other = lax.ppermute(jnp.where(odd_x == 1, high, low), "bx", second_x)
    one = lax.ppermute(jnp.where(odd_x == 1, low, high), "bx", first_x)
    correction = sums[BX:2 * BX] + other_inner + one + other
    return estimate * (1.0 + correction / count.astype(F32))


def solution(mesh):
    return jax.shard_map(
        per_device,
        mesh=mesh,
        in_specs=(P("bx", "by"), P(None, "bx", "by"), P(), P("bx", "by", None), P("bx", "by")),
        out_specs=P("bx", "by"),
        check_vma=False,
    )
```

```python
import functools

import jax
import jax.numpy as jnp
import ml_dtypes
import numpy as np
from jax import lax
from jax.experimental import pallas as pl
from jax.experimental.pallas import tpu as pltpu
from jax.sharding import PartitionSpec as P

V = 8
K = 64
SZ = 64
HALF = K // 2
BX = 32
BY = 32
CMAX = 5
PX = 128
PY = 96
PZ = 96
KZ = PZ // 2
SLOT = 64
LANES = 128
KPITCH = KZ + 4
YPITCH = BY + 4
BIGPITCH = PY + 4
WX = BX + K
MIB = 1024 * 1024

F32 = jnp.float32
BF16 = jnp.bfloat16


def three_parts(table, axis=1):
    high = table.astype(ml_dtypes.bfloat16)
    low = (table - high.astype(np.float64)).astype(ml_dtypes.bfloat16)
    return np.concatenate([high, high, low], axis=axis)


def two_rows(table):
    high = table.astype(ml_dtypes.bfloat16)
    low = (table - high.astype(np.float64)).astype(ml_dtypes.bfloat16)
    return np.block([[high, high], [low, np.zeros_like(low)]])


def turn(frequency, position, period):
    turns = np.mod(frequency[:, None] * position[None, :], 2 * period)
    return turns * (np.pi / period)


def blocks(values, copies):
    rows, columns = values.shape
    out = np.zeros((copies, rows, copies, columns))
    for copy in range(copies):
        out[copy, :, copy, :] = values
    return out.reshape(copies * rows, copies * columns)


def z_angles(offset):
    return turn(2 * np.arange(KZ) + 1, np.arange(SZ) + offset, PZ)


def padded(values):
    return np.pad(values, ((0, 0), (0, SLOT - KZ)))


def z_forward(offset):
    angles = z_angles(offset).T
    parts = [blocks(padded(part), 2) for part in (np.cos(angles), -np.sin(angles))]
    return three_parts(np.concatenate(parts, axis=1), 0)


def z_inverse():
    angles = z_angles(0).T
    parts = [blocks(padded(part).T, 2) for part in (np.cos(angles), -np.sin(angles))]
    return three_parts(np.concatenate(parts, axis=0) * (2.0 / PZ), 0)


def x_forward(entries, offset, room, copies=1):
    angles = turn(2 * np.arange(PX), np.arange(entries) + offset, PX).T
    cosine, sine = [np.pad(f(angles), ((0, room - entries), (0, 0))) for f in (np.cos, np.sin)]
    return three_parts(blocks(np.block([[cosine, -sine], [sine, cosine]]), copies), 0)


def x_inverse(entries, offset, parts):
    angles = turn(2 * np.arange(PX), np.arange(entries) + offset, PX).T
    cosine, sine = np.cos(angles) / PX, np.sin(angles) / PX
    return parts(np.block([[cosine, -sine], [sine, cosine]]))


def y_forward(entries, offset):
    angles = turn(2 * np.arange(PY), np.arange(entries) + offset, PY)
    cosine, sine = np.cos(angles), np.sin(angles)
    return three_parts(np.block([[cosine, sine], [-sine, cosine]]), 1)


def y_inverse(entries, offset, parts):
    angles = turn(2 * np.arange(PY), np.arange(entries) + offset, PY).T
    cosine, sine = np.cos(angles) / PY, np.sin(angles) / PY
    return parts(np.block([[cosine, -sine], [sine, cosine]]))


def split(data):
    high = data.astype(BF16)
    low = (data - high.astype(F32)).astype(BF16)
    return high, low


def three(data, axis):
    high, low = split(data)
    return jnp.concatenate([high, low, high], axis=axis)


def dot(a, b):
    return lax.dot_general(a, b, (((1,), (0,)), ((), ())), preferred_element_type=F32)


def dot_nt(a, b):
    return lax.dot_general(a, b, (((1,), (1,)), ((), ())), preferred_element_type=F32)


def loop(count, body, unroll=1):
    def step(index, carry):
        for at in range(unroll):
            body(index * unroll + at)
        return carry

    lax.fori_loop(0, count // unroll, step, 0)


def aligned(index, size):
    return pl.ds(pl.multiple_of(index * size, size), size)


def columns(pair, pairs):
    return slice(pair * LANES, (pair + pairs) * LANES)


def drop_padding(rows):
    return jnp.concatenate([rows[:KZ], rows[SLOT:SLOT + KZ]], axis=0)


def z_stage(pieces, wz, copies):
    rows = pieces[0].shape[0]
    along = dot(three(jnp.concatenate(pieces, axis=0), 1), wz)
    groups = []
    for at in range(0, len(pieces), copies):
        parts = []
        for pair in range(at, at + copies):
            piece = along[pair * rows:(pair + 1) * rows]
            parts += [piece[:, :LANES], piece[:, LANES:]]
        if rows * 2 * copies > LANES:
            sides = []
            for part in parts:
                if rows < LANES:
                    part = jnp.concatenate([part, jnp.zeros((LANES - rows, LANES), F32)], axis=0)
                sides.append(drop_padding(part.T))
            groups.append(jnp.concatenate(sides, axis=1))
        else:
            groups.append(drop_padding(jnp.concatenate(parts, axis=0).T))
    return three(jnp.concatenate(groups, axis=0), 1)


def x_stage(stash, wx, real_ref, imag_ref, first_y, copies):
    across = dot(stash, wx)
    for at in range(stash.shape[0] // (2 * KZ)):
        piece = across[at * 2 * KZ:(at + 1) * 2 * KZ]
        for copy in range(copies):
            for y in range(2):
                where = pl.ds((first_y + 2 * (at * copies + copy) + y) * KPITCH, KZ)
                part = piece[y * KZ:(y + 1) * KZ]
                real_ref[where, :] = part[:, (2 * copy) * LANES:(2 * copy + 1) * LANES]
                imag_ref[where, :] = part[:, (2 * copy + 1) * LANES:(2 * copy + 2) * LANES]


def pipelined(count, first, second, stash):
    first(0, stash[0])
    for step in range(count):
        if step + 1 < count:
            first(step + 1, stash[(step + 1) % 2])
        second(step, stash[step % 2])


def z_then_x(read, count, wz, wx, real_ref, imag_ref, copies, stash, place=lambda pair: 2 * pair):
    pairs = stash[0].shape[0] // (2 * KZ) * copies

    def first(step, ref):
        data = read(step * pairs, pairs)
        pieces = [data[:, p * LANES:(p + 1) * LANES] for p in range(pairs)]
        ref[...] = z_stage(pieces, wz[...], copies)

    def second(step, ref):
        x_stage(ref[...], wx[...], real_ref, imag_ref, place(step * pairs), copies)

    pipelined(count // pairs, first, second, stash)


def along_y(table, reals, imags):
    data = jnp.concatenate(
        [jnp.concatenate(reals, axis=1), jnp.concatenate(imags, axis=1)], axis=0
    )
    if table.shape[1] == 2 * data.shape[0]:
        out = dot(table, jnp.concatenate(split(data), axis=0))
        out = out[:table.shape[0] // 2] + out[table.shape[0] // 2:]
    else:
        out = dot(table, three(data, 0))
    half = out.shape[0] // 2
    return [
        (out[:half, at * LANES:(at + 1) * LANES], out[half:, at * LANES:(at + 1) * LANES])
        for at in range(2)
    ]


def strided(ref, start, count, stride):
    return ref[pl.ds(start, count, stride=stride), :]


def y_from_rows(table, real_ref, imag_ref, kz, count):
    reals = [strided(real_ref, kz + at, count, KPITCH) for at in range(2)]
    imags = [strided(imag_ref, kz + at, count, KPITCH) for at in range(2)]
    return along_y(table, reals, imags)


def x_from_rows(table, real_ref, imag_ref, ys, stride):
    tall = table.shape[1] == 4 * LANES
    empty = jnp.zeros((SLOT - KZ, table.shape[1]), BF16)
    rows = []
    for y in ys:
        data = jnp.concatenate(
            [strided(real_ref, y, KZ, stride), strided(imag_ref, y, KZ, stride)], axis=1
        )
        rows += [jnp.concatenate(split(data), axis=1) if tall else three(data, 1), empty]
    out = dot_nt(table, jnp.concatenate(rows, axis=0))
    return out[:table.shape[0] // 2] + out[table.shape[0] // 2:] if tall else out


def table_copies(sources, targets, sems):
    return [
        pltpu.make_async_copy(source, target, sems.at[at])
        for at, (source, target) in enumerate(zip(sources, targets))
    ]


def room_for(tables):
    return [pltpu.VMEM(t.shape, BF16) for t in tables]


def otf_kernel(begin, end, count_ref, ids_ref, psf_hbm, wz_hbm, wx_hbm, wy_hbm, *rest):
    out_hbm, psf, out, real, imag, stash0, stash1, *rest = rest[-13:]
    wz_ref, wx_ref, wy_ref, psf_sem, out_sem, table_sem = rest
    steps = KZ // (2 * UY)

    def fetch(step):
        buffer = lax.rem(step, 2)
        return pltpu.make_async_copy(
            psf_hbm.at[ids_ref[begin + step]], psf.at[buffer], psf_sem.at[buffer]
        )

    def store(step, j):
        where = pl.ds(j * UY, UY)
        return pltpu.make_async_copy(
            out.at[where], out_hbm.at[begin + step, where], out_sem.at[j]
        )

    slots = jnp.maximum(jnp.minimum(count_ref[0], end) - begin, 0)

    @pl.when(slots > 0)
    def _():
        fetch(0).start()

    tables = table_copies((wz_hbm, wx_hbm, wy_hbm), (wz_ref, wx_ref, wy_ref), table_sem)
    for copy in tables:
        copy.start()
    for copy in tables:
        copy.wait()

    def body(step, carry):
        buffer = lax.rem(step, 2)
        fetch(step).wait()

        @pl.when(step + 1 < slots)
        def _():
            fetch(step + 1).start()

        def read(pair, pairs):
            return psf[buffer, :, columns(pair, pairs)]

        z_then_x(read, K // 2, wz_ref, wx_ref, real, imag, 1, (stash0, stash1))

        def y(j):
            @pl.when(step > 0)
            def _():
                store(step - 1, 2 * j).wait()
                store(step - 1, 2 * j + 1).wait()

            for pair in range(UY):
                kz = (j * UY + pair) * 2
                for at, value in enumerate(y_from_rows(wy_ref[...], real, imag, kz, K)):
                    out[kz + at, 0] = value[0]
                    out[kz + at, 1] = value[1]
                if pair == UY // 2 - 1:
                    store(step, 2 * j).start()
            store(step, 2 * j + 1).start()

        loop(steps, y)
        return carry

    lax.fori_loop(0, slots, body, 0)

    @pl.when(slots > 0)
    def _():
        for j in range(2 * steps):
            store(slots - 1, j).wait()


ZPO = 16
ZPF = 8
ZPE = 8
UX = 4
OTF_LIMITS = (60 * MIB, 60 * MIB)
MAIN_LIMIT = 48 * MIB
TAIL_LIMIT = 16 * MIB
UY = 12
UP = 24
UG = 24
UF = 8
UT = 12


def final_sums(wxo, wzi, chunks, stash):
    def first(step, ref):
        real_ref, imag_ref, row, _, _ = chunks[step]
        for group in range(2):
            ys = [row + group * 4 + k for k in range(4)]
            out = x_from_rows(wxo[...], real_ref, imag_ref, ys, YPITCH)
            for pair in range(2):
                piece = out[:, pair * LANES:(pair + 1) * LANES]
                data = jnp.concatenate([piece[:WX], piece[WX:]], axis=1)
                at = (group * 2 + pair) * WX
                ref[at:at + WX, :] = three(data, 1)

    def second(step, ref):
        _, _, _, out, pair = chunks[step]
        sums = dot(ref[...], wzi[...])
        for at in range(4):
            lanes, part = columns(pair + at, 1), sums[at * WX:(at + 1) * WX]
            if len(out) == 1:
                out[0][:, lanes] = part
            else:
                out[0][:BX, lanes] = part[:BX]
                out[0][BX:, lanes] = part[2 * BX:]
                out[1][:, lanes] = part[BX:2 * BX]

    pipelined(len(chunks), first, second, stash)


def main_kernel(
    count_ref, ids_ref, odd_ref, own_ref, first_ref, second_ref, views_hbm, otf_hbm,
    wz_ref, wzi_ref, wxf_ref, wyf_ref, wyi_ref, wxi_ref, wxe_ref, wye_ref, wyo_ref, wxo_ref,
    first_out, outer_out, inner_out, real_hbm, imag_hbm,
    field, total, big_real, big_imag, real, imag, lines, error, otf, image,
    wide0, wide1, thin0, thin1, last0, last1, otf_sem, image_sem, own_sem,
):
    count = count_ref[0]

    def fetch(slot):
        buffer = lax.rem(slot, 2)
        return (
            pltpu.make_async_copy(otf_hbm.at[slot], otf.at[buffer], otf_sem.at[buffer]),
            pltpu.make_async_copy(
                views_hbm.at[ids_ref[slot]], image.at[buffer], image_sem.at[buffer]
            ),
        )

    for copy in fetch(0):
        copy.start()

    odd = odd_ref[0]

    def read_window(pair, pairs):
        part, pair = divmod(pair, BY // 2)
        return (own_ref, first_ref, second_ref)[part][:, columns(pair, pairs)]

    def place_window(pair):
        part, pair = divmod(pair, BY // 2)
        return (1, 2 - 2 * odd, 2 * odd)[part] * BY + 2 * pair

    z_then_x(
        read_window, PY // 2, wz_ref, wxf_ref, big_real, big_imag, 1, (wide0, wide1), place_window
    )

    def field_y(j):
        for pair in range(UF):
            kz = (j * UF + pair) * 2
            for at, out in enumerate(y_from_rows(wyf_ref[...], big_real, big_imag, kz, PY)):
                for part in range(2):
                    field[kz + at, part] = out[part]
                    total[kz + at, part] = jnp.zeros((PY, LANES), F32)

    loop(KZ // (2 * UF), field_y)

    def view(slot, carry):
        buffer = lax.rem(slot, 2)
        for copy in fetch(slot):
            copy.wait()

        @pl.when(slot + 1 < count)
        def _():
            for copy in fetch(slot + 1):
                copy.start()

        def product(j):
            for pair in range(UP):
                kz = (j * UP + pair) * 2
                reals, imags = [], []
                for at in range(2):
                    fr, fi = field[kz + at, 0], field[kz + at, 1]
                    pr, pi = otf[buffer, kz + at, 0], otf[buffer, kz + at, 1]
                    reals.append(fr * pr - fi * pi)
                    imags.append(fr * pi + fi * pr)
                for at, out in enumerate(along_y(wyi_ref[...], reals, imags)):
                    where = pl.ds((kz + at) * YPITCH, BY)
                    real[where, :] = out[0]
                    imag[where, :] = out[1]

        loop(KZ // (2 * UP), product)

        def inverse_x(j):
            for group in range(2):
                y = j * 8 + group * 4
                out = x_from_rows(wxi_ref[...], real, imag, [y + k for k in range(4)], YPITCH)
                for pair in range(2):
                    piece = out[:, pair * LANES:(pair + 1) * LANES]
                    data = jnp.concatenate([piece[:BX], piece[BX:]], axis=1)
                    lines[aligned(j * 4 + group * 2 + pair, BX), :] = three(data, 1)

        loop(BY // 8, inverse_x, UX)

        for j in range(2):
            blurred = dot(lines[j * 8 * BX:(j + 1) * 8 * BX, :], wzi_ref[...])
            for pair in range(8):
                where = columns(j * 8 + pair, 1)
                error[:, where] = image[buffer, :, where] / blurred[pair * BX:(pair + 1) * BX] - 1.0

        def read_error(pair, pairs):
            return error[:, columns(pair, pairs)]

        z_then_x(read_error, BY // 2, wz_ref, wxe_ref, real, imag, 2, (thin0, thin1))

        def gather(j):
            for pair in range(UG):
                kz = (j * UG + pair) * 2
                for at, (er, ei) in enumerate(y_from_rows(wye_ref[...], real, imag, kz, BY)):
                    pr, pi = otf[buffer, kz + at, 0], otf[buffer, kz + at, 1]
                    total[kz + at, 0] += er * pr + ei * pi
                    total[kz + at, 1] += ei * pr - er * pi

        loop(KZ // (2 * UG), gather)
        return carry

    lax.fori_loop(0, count, view, 0)

    def inverse_y(j):
        for pair in range(UT):
            kz = (j * UT + pair) * 2
            reals = [total[kz + at, 0] for at in range(2)]
            imags = [total[kz + at, 1] for at in range(2)]
            for at, out in enumerate(along_y(wyo_ref[...], reals, imags)):
                row = (kz + at) * YPITCH
                for value, big, own in zip(out, (big_real, big_imag), (real, imag)):
                    big[pl.ds(row, BY), :] = value[:BY]
                    own[pl.ds(row, BY), :] = value[BY:2 * BY]
                    big[pl.ds(KZ * YPITCH + row, BY), :] = value[2 * BY:]

    loop(KZ // (2 * UT), inverse_y)
    copies = (
        pltpu.make_async_copy(real, real_hbm, own_sem.at[0]),
        pltpu.make_async_copy(imag, imag_hbm, own_sem.at[1]),
    )
    for copy in copies:
        copy.start()
    chunks = [
        (big_real, big_imag, side * KZ * YPITCH + y, out, y // 2)
        for side, out in ((odd, (outer_out, inner_out)), (1 - odd, (first_out,)))
        for y in range(0, BY, 8)
    ]
    final_sums(wxo_ref, wzi_ref, chunks, (last0, last1))
    for copy in copies:
        copy.wait()


def tail_kernel(real, imag, wzi_ref, wxo_ref, out, last0, last1):
    chunks = [(real, imag, y, (out,), y // 2) for y in range(0, BY, 8)]
    final_sums(wxo_ref, wzi_ref, chunks, (last0, last1))


SPECTRUM = (KZ, 2, PY, LANES)
ROWS = (KZ * YPITCH, LANES)
WIDE = (WX, BY * SZ)
LAST = pltpu.VMEM((4 * WX, 6 * LANES), BF16)
IN_VMEM = pl.BlockSpec(memory_space=pltpu.VMEM)
IN_SMEM = pl.BlockSpec(memory_space=pltpu.SMEM)
ANYWHERE = pl.BlockSpec(memory_space=pl.ANY)


def otf_call(count, ids, psf, begin, end, held=None):
    tables = (z_forward(-HALF), x_forward(K, -HALF, K), y_forward(K, -HALF))
    inputs = [count, ids, psf] + [jnp.asarray(t) for t in tables]
    specs = [IN_SMEM, IN_SMEM, ANYWHERE] + [ANYWHERE] * len(tables)
    aliases = {}
    if held is not None:
        aliases = {len(inputs): 0}
        inputs.append(held)
        specs.append(ANYWHERE)
    return pl.pallas_call(
        functools.partial(otf_kernel, begin, end),
        out_shape=jax.ShapeDtypeStruct((CMAX,) + SPECTRUM, F32),
        in_specs=specs,
        out_specs=ANYWHERE,
        scratch_shapes=[
            pltpu.VMEM((2, K, K * K), F32),
            pltpu.VMEM(SPECTRUM, F32),
            pltpu.VMEM((K * KPITCH, LANES), F32),
            pltpu.VMEM((K * KPITCH, LANES), F32),
            pltpu.VMEM((ZPO * 2 * KZ, 3 * LANES), BF16),
            pltpu.VMEM((ZPO * 2 * KZ, 3 * LANES), BF16),
        ] + room_for(tables) + [
            pltpu.SemaphoreType.DMA((2,)),
            pltpu.SemaphoreType.DMA((2 * KZ // (2 * UY),)),
            pltpu.SemaphoreType.DMA((len(tables),)),
        ],
        input_output_aliases=aliases,
        compiler_params=pltpu.CompilerParams(vmem_limit_bytes=OTF_LIMITS[0 if held is None else 1]),
        cost_estimate=pl.CostEstimate(
            flops=4 * 10**9 * (end - begin), bytes_accessed=6 * 10**6 * (end - begin), transcendentals=0
        ),
        name="otf",
    )(*inputs)


def main_call(count, ids, odd, window, views, otf):
    own, first, second = window
    tables = (
        z_forward(0),
        z_inverse(),
        x_forward(WX, 0, LANES),
        y_forward(PY, 0),
        y_inverse(BY, HALF, two_rows),
        x_inverse(BX, HALF, two_rows),
        x_forward(BX, HALF, BX, 2),
        y_forward(BY, HALF),
        y_inverse(PY, 0, three_parts),
        x_inverse(WX, 0, three_parts),
    )
    return pl.pallas_call(
        main_kernel,
        out_shape=[
            jax.ShapeDtypeStruct(shape, F32)
            for shape in (WIDE, (2 * BX, BY * SZ), (BX, BY * SZ), ROWS, ROWS)
        ],
        in_specs=[IN_SMEM] * 3 + [IN_VMEM] * 3 + [ANYWHERE] * 2 + [IN_VMEM] * len(tables),
        out_specs=[IN_VMEM] * 3 + [ANYWHERE] * 2,
        scratch_shapes=[
            pltpu.VMEM(SPECTRUM, F32),
            pltpu.VMEM(SPECTRUM, F32),
            pltpu.VMEM((PY * KPITCH, LANES), F32),
            pltpu.VMEM((PY * KPITCH, LANES), F32),
            pltpu.VMEM(ROWS, F32),
            pltpu.VMEM(ROWS, F32),
            pltpu.VMEM((BX * BY // 2, 6 * LANES), BF16),
            pltpu.VMEM((BX, BY * SZ), F32),
            pltpu.VMEM((2,) + SPECTRUM, F32),
            pltpu.VMEM((2, BX, BY * SZ), F32),
            pltpu.VMEM((ZPF * 2 * KZ, 6 * LANES), BF16),
            pltpu.VMEM((ZPF * 2 * KZ, 6 * LANES), BF16),
            pltpu.VMEM((ZPE * KZ, 3 * LANES), BF16),
            pltpu.VMEM((ZPE * KZ, 3 * LANES), BF16),
            LAST,
            LAST,
            pltpu.SemaphoreType.DMA((2,)),
            pltpu.SemaphoreType.DMA((2,)),
            pltpu.SemaphoreType.DMA((2,)),
        ],
        compiler_params=pltpu.CompilerParams(vmem_limit_bytes=MAIN_LIMIT),
        cost_estimate=pl.CostEstimate(flops=30 * 10**9, bytes_accessed=40 * 10**6, transcendentals=0),
        name="views",
    )(count, ids, odd, own, first, second, views, otf, *[jnp.asarray(t) for t in tables])


def tail_call(real, imag):
    tables = (z_inverse(), x_inverse(WX, 0, three_parts))
    return pl.pallas_call(
        tail_kernel,
        out_shape=jax.ShapeDtypeStruct(WIDE, F32),
        in_specs=[IN_VMEM] * 4,
        out_specs=IN_VMEM,
        scratch_shapes=[LAST, LAST],
        compiler_params=pltpu.CompilerParams(vmem_limit_bytes=TAIL_LIMIT),
        cost_estimate=pl.CostEstimate(flops=4 * 10**9, bytes_accessed=3 * 10**6, transcendentals=0),
        name="tail",
    )(real, imag, *[jnp.asarray(t) for t in tables])


def swaps(axis):
    devices = lax.axis_size(axis)
    first = [(i, i ^ 1) for i in range(devices) if i ^ 1 < devices]
    second = [(i, i + 1 if i % 2 else i - 1) for i in range(1, devices)]
    second = [(i, j) for i, j in second if j < devices]
    return lax.rem(lax.axis_index(axis), 2), first, second


def per_device(estimate, views, psf, view_list, view_count):
    ids = view_list.reshape(V)
    count = view_count.reshape(1)
    odd_x, first_x, second_x = swaps("bx")
    odd_y, first_y, second_y = swaps("by")
    one = lax.ppermute(estimate, "bx", first_x)
    other = lax.ppermute(estimate, "bx", second_x)
    before = jnp.where(odd_x == 1, one, other)
    after = jnp.where(odd_x == 1, other, one)
    own = jnp.concatenate([before, estimate, after], axis=0)
    window = (own, lax.ppermute(own, "by", first_y), lax.ppermute(own, "by", second_y))
    otf = otf_call(count, ids, psf, 0, 2)
    otf = otf_call(count, ids, psf, 2, CMAX, otf)
    rim, outer, inner, real, imag = main_call(
        count, ids, odd_y.reshape(1), window, views, otf
    )
    other_outer = lax.ppermute(outer, "by", second_y)
    one = lax.ppermute(rim, "by", first_y)
    center, inner = lax.optimization_barrier((tail_call(real, imag), inner))
    other_inner = lax.ppermute(inner, "by", second_y)
    sums = center + one
    low = sums[:BX] + other_outer[:BX]
    high = sums[2 * BX:] + other_outer[BX:]
    other = lax.ppermute(jnp.where(odd_x == 1, high, low), "bx", second_x)
    one = lax.ppermute(jnp.where(odd_x == 1, low, high), "bx", first_x)
    correction = sums[BX:2 * BX] + other_inner + one + other
    return estimate * (1.0 + correction / count.astype(F32))


def solution(mesh):
    return jax.shard_map(
        per_device,
        mesh=mesh,
        in_specs=(P("bx", "by"), P(None, "bx", "by"), P(), P("bx", "by", None), P("bx", "by")),
        out_specs=P("bx", "by"),
        check_vma=False,
    )
```

```python
import functools

import jax
import jax.numpy as jnp
import ml_dtypes
import numpy as np
from jax import lax
from jax.experimental import pallas as pl
from jax.experimental.pallas import tpu as pltpu
from jax.sharding import PartitionSpec as P

V = 8
K = 64
SZ = 64
HALF = K // 2
BX = 32
BY = 32
CMAX = 5
PX = 128
PY = 96
PZ = 96
KZ = PZ // 2
SLOT = 64
LANES = 128
KPITCH = KZ + 4
YPITCH = BY + 4
BIGPITCH = PY + 4
WX = BX + K
MIB = 1024 * 1024

F32 = jnp.float32
BF16 = jnp.bfloat16


def three_parts(table, axis=1):
    high = table.astype(ml_dtypes.bfloat16)
    low = (table - high.astype(np.float64)).astype(ml_dtypes.bfloat16)
    return np.concatenate([high, high, low], axis=axis)


def two_rows(table):
    high = table.astype(ml_dtypes.bfloat16)
    low = (table - high.astype(np.float64)).astype(ml_dtypes.bfloat16)
    return np.block([[high, high], [low, np.zeros_like(low)]])


def turn(frequency, position, period):
    turns = np.mod(frequency[:, None] * position[None, :], 2 * period)
    return turns * (np.pi / period)


def blocks(values, copies):
    rows, columns = values.shape
    out = np.zeros((copies, rows, copies, columns))
    for copy in range(copies):
        out[copy, :, copy, :] = values
    return out.reshape(copies * rows, copies * columns)


def z_angles(offset):
    return turn(2 * np.arange(KZ) + 1, np.arange(SZ) + offset, PZ)


def padded(values):
    return np.pad(values, ((0, 0), (0, SLOT - KZ)))


def z_forward(offset):
    angles = z_angles(offset).T
    parts = [blocks(padded(part), 2) for part in (np.cos(angles), -np.sin(angles))]
    return three_parts(np.concatenate(parts, axis=1), 0)


def z_inverse():
    angles = z_angles(0).T
    parts = [blocks(padded(part).T, 2) for part in (np.cos(angles), -np.sin(angles))]
    return three_parts(np.concatenate(parts, axis=0) * (2.0 / PZ), 0)


def x_forward(entries, offset, room, copies=1):
    angles = turn(2 * np.arange(PX), np.arange(entries) + offset, PX).T
    cosine, sine = [np.pad(f(angles), ((0, room - entries), (0, 0))) for f in (np.cos, np.sin)]
    return three_parts(blocks(np.block([[cosine, -sine], [sine, cosine]]), copies), 0)


def x_inverse(entries, offset, parts):
    angles = turn(2 * np.arange(PX), np.arange(entries) + offset, PX).T
    cosine, sine = np.cos(angles) / PX, np.sin(angles) / PX
    return parts(np.block([[cosine, -sine], [sine, cosine]]))


def y_forward(entries, offset):
    angles = turn(2 * np.arange(PY), np.arange(entries) + offset, PY)
    cosine, sine = np.cos(angles), np.sin(angles)
    return three_parts(np.block([[cosine, sine], [-sine, cosine]]), 1)


def y_inverse(entries, offset, parts):
    angles = turn(2 * np.arange(PY), np.arange(entries) + offset, PY).T
    cosine, sine = np.cos(angles) / PY, np.sin(angles) / PY
    return parts(np.block([[cosine, -sine], [sine, cosine]]))


def split(data):
    high = data.astype(BF16)
    low = (data - high.astype(F32)).astype(BF16)
    return high, low


def three(data, axis):
    high, low = split(data)
    return jnp.concatenate([high, low, high], axis=axis)


def dot(a, b):
    return lax.dot_general(a, b, (((1,), (0,)), ((), ())), preferred_element_type=F32)


def dot_nt(a, b):
    return lax.dot_general(a, b, (((1,), (1,)), ((), ())), preferred_element_type=F32)


def loop(count, body, unroll=1):
    def step(index, carry):
        for at in range(unroll):
            body(index * unroll + at)
        return carry

    lax.fori_loop(0, count // unroll, step, 0)


def aligned(index, size):
    return pl.ds(pl.multiple_of(index * size, size), size)


def columns(pair, pairs):
    return slice(pair * LANES, (pair + pairs) * LANES)


def drop_padding(rows):
    return jnp.concatenate([rows[:KZ], rows[SLOT:SLOT + KZ]], axis=0)


def z_stage(pieces, wz, copies):
    rows = pieces[0].shape[0]
    along = dot(three(jnp.concatenate(pieces, axis=0), 1), wz)
    groups = []
    for at in range(0, len(pieces), copies):
        parts = []
        for pair in range(at, at + copies):
            piece = along[pair * rows:(pair + 1) * rows]
            parts += [piece[:, :LANES], piece[:, LANES:]]
        if rows * 2 * copies > LANES:
            sides = []
            for part in parts:
                if rows < LANES:
                    part = jnp.concatenate([part, jnp.zeros((LANES - rows, LANES), F32)], axis=0)
                sides.append(drop_padding(part.T))
            groups.append(jnp.concatenate(sides, axis=1))
        else:
            groups.append(drop_padding(jnp.concatenate(parts, axis=0).T))
    return three(jnp.concatenate(groups, axis=0), 1)


def x_stage(stash, wx, real_ref, imag_ref, first_y, copies):
    across = dot(stash, wx)
    for at in range(stash.shape[0] // (2 * KZ)):
        piece = across[at * 2 * KZ:(at + 1) * 2 * KZ]
        for copy in range(copies):
            for y in range(2):
                where = pl.ds((first_y + 2 * (at * copies + copy) + y) * KPITCH, KZ)
                part = piece[y * KZ:(y + 1) * KZ]
                real_ref[where, :] = part[:, (2 * copy) * LANES:(2 * copy + 1) * LANES]
                imag_ref[where, :] = part[:, (2 * copy + 1) * LANES:(2 * copy + 2) * LANES]


def pipelined(count, first, second, stash):
    first(0, stash[0])
    for step in range(count):
        if step + 1 < count:
            first(step + 1, stash[(step + 1) % 2])
        second(step, stash[step % 2])


def z_then_x(read, count, wz, wx, real_ref, imag_ref, copies, stash, place=lambda pair: 2 * pair):
    pairs = stash[0].shape[0] // (2 * KZ) * copies

    def first(step, ref):
        data = read(step * pairs, pairs)
        pieces = [data[:, p * LANES:(p + 1) * LANES] for p in range(pairs)]
        ref[...] = z_stage(pieces, wz[...], copies)

    def second(step, ref):
        x_stage(ref[...], wx[...], real_ref, imag_ref, place(step * pairs), copies)

    pipelined(count // pairs, first, second, stash)


def along_y(table, reals, imags):
    data = jnp.concatenate(
        [jnp.concatenate(reals, axis=1), jnp.concatenate(imags, axis=1)], axis=0
    )
    if table.shape[1] == 2 * data.shape[0]:
        out = dot(table, jnp.concatenate(split(data), axis=0))
        out = out[:table.shape[0] // 2] + out[table.shape[0] // 2:]
    else:
        out = dot(table, three(data, 0))
    half = out.shape[0] // 2
    return [
        (out[:half, at * LANES:(at + 1) * LANES], out[half:, at * LANES:(at + 1) * LANES])
        for at in range(2)
    ]


def strided(ref, start, count, stride):
    return ref[pl.ds(start, count, stride=stride), :]


def y_from_rows(table, real_ref, imag_ref, kz, count):
    reals = [strided(real_ref, kz + at, count, KPITCH) for at in range(2)]
    imags = [strided(imag_ref, kz + at, count, KPITCH) for at in range(2)]
    return along_y(table, reals, imags)


def x_from_rows(table, real_ref, imag_ref, ys, stride):
    tall = table.shape[1] == 4 * LANES
    empty = jnp.zeros((SLOT - KZ, table.shape[1]), BF16)
    rows = []
    for y in ys:
        data = jnp.concatenate(
            [strided(real_ref, y, KZ, stride), strided(imag_ref, y, KZ, stride)], axis=1
        )
        rows += [jnp.concatenate(split(data), axis=1) if tall else three(data, 1), empty]
    out = dot_nt(table, jnp.concatenate(rows, axis=0))
    return out[:table.shape[0] // 2] + out[table.shape[0] // 2:] if tall else out


def table_copies(sources, targets, sems):
    return [
        pltpu.make_async_copy(source, target, sems.at[at])
        for at, (source, target) in enumerate(zip(sources, targets))
    ]


def room_for(tables):
    return [pltpu.VMEM(t.shape, BF16) for t in tables]


def otf_kernel(begin, end, count_ref, ids_ref, psf_hbm, wz_hbm, wx_hbm, wy_hbm, *rest):
    out_hbm, psf, out, real, imag, stash0, stash1, *rest = rest[-13:]
    wz_ref, wx_ref, wy_ref, psf_sem, out_sem, table_sem = rest
    steps = KZ // (2 * UY)

    def fetch(step):
        buffer = lax.rem(step, 2)
        return pltpu.make_async_copy(
            psf_hbm.at[ids_ref[begin + step]], psf.at[buffer], psf_sem.at[buffer]
        )

    def store(step, j):
        where = pl.ds(j * UY, UY)
        return pltpu.make_async_copy(
            out.at[where], out_hbm.at[begin + step, where], out_sem.at[j]
        )

    slots = jnp.maximum(jnp.minimum(count_ref[0], end) - begin, 0)

    @pl.when(slots > 0)
    def _():
        fetch(0).start()

    tables = table_copies((wz_hbm, wx_hbm, wy_hbm), (wz_ref, wx_ref, wy_ref), table_sem)
    for copy in tables:
        copy.start()
    for copy in tables:
        copy.wait()

    def body(step, carry):
        buffer = lax.rem(step, 2)
        fetch(step).wait()

        @pl.when(step + 1 < slots)
        def _():
            fetch(step + 1).start()

        def read(pair, pairs):
            return psf[buffer, :, columns(pair, pairs)]

        z_then_x(read, K // 2, wz_ref, wx_ref, real, imag, 1, (stash0, stash1))

        def y(j):
            @pl.when(step > 0)
            def _():
                store(step - 1, 2 * j).wait()
                store(step - 1, 2 * j + 1).wait()

            for pair in range(UY):
                kz = (j * UY + pair) * 2
                for at, value in enumerate(y_from_rows(wy_ref[...], real, imag, kz, K)):
                    out[kz + at, 0] = value[0]
                    out[kz + at, 1] = value[1]
                if pair == UY // 2 - 1:
                    store(step, 2 * j).start()
            store(step, 2 * j + 1).start()

        loop(steps, y)
        return carry

    lax.fori_loop(0, slots, body, 0)

    @pl.when(slots > 0)
    def _():
        for j in range(2 * steps):
            store(slots - 1, j).wait()


ZPO = 16
ZPF = 8
ZPE = 8
UX = 4
OTF_LIMITS = (60 * MIB, 60 * MIB)
MAIN_LIMIT = 48 * MIB
TAIL_LIMIT = 16 * MIB
UY = 12
UP = 24
UG = 24
UF = 8
UT = 12


def final_sums(wxo, wzi, chunks, stash):
    def first(step, ref):
        real_ref, imag_ref, row, _, _ = chunks[step]
        for group in range(2):
            ys = [row + group * 4 + k for k in range(4)]
            out = x_from_rows(wxo[...], real_ref, imag_ref, ys, YPITCH)
            for pair in range(2):
                piece = out[:, pair * LANES:(pair + 1) * LANES]
                data = jnp.concatenate([piece[:WX], piece[WX:]], axis=1)
                at = (group * 2 + pair) * WX
                ref[at:at + WX, :] = three(data, 1)

    def second(step, ref):
        _, _, _, out, pair = chunks[step]
        sums = dot(ref[...], wzi[...])
        for at in range(4):
            lanes, part = columns(pair + at, 1), sums[at * WX:(at + 1) * WX]
            if len(out) == 1:
                out[0][:, lanes] = part
            else:
                out[0][:BX, lanes] = part[:BX]
                out[0][BX:, lanes] = part[2 * BX:]
                out[1][:, lanes] = part[BX:2 * BX]

    pipelined(len(chunks), first, second, stash)


def main_kernel(
    count_ref, ids_ref, odd_ref, own_ref, first_ref, second_ref, views_hbm, otf_hbm,
    wz_ref, wzi_ref, wxf_ref, wyf_ref, wyi_ref, wxi_ref, wxe_ref, wye_ref, wyo_ref, wxo_ref,
    first_out, outer_out, inner_out, real_out, imag_out,
    field, total, big_real, big_imag, real, imag, lines, error, otf, image,
    wide0, wide1, thin0, thin1, last0, last1, otf_sem, image_sem,
):
    count = count_ref[0]

    def fetch(slot):
        buffer = lax.rem(slot, 2)
        return (
            pltpu.make_async_copy(otf_hbm.at[slot], otf.at[buffer], otf_sem.at[buffer]),
            pltpu.make_async_copy(
                views_hbm.at[ids_ref[slot]], image.at[buffer], image_sem.at[buffer]
            ),
        )

    for copy in fetch(0):
        copy.start()

    odd = odd_ref[0]

    def read_window(pair, pairs):
        part, pair = divmod(pair, BY // 2)
        return (own_ref, first_ref, second_ref)[part][:, columns(pair, pairs)]

    def place_window(pair):
        part, pair = divmod(pair, BY // 2)
        return (1, 2 - 2 * odd, 2 * odd)[part] * BY + 2 * pair

    z_then_x(
        read_window, PY // 2, wz_ref, wxf_ref, big_real, big_imag, 1, (wide0, wide1), place_window
    )

    def field_y(j):
        for pair in range(UF):
            kz = (j * UF + pair) * 2
            for at, out in enumerate(y_from_rows(wyf_ref[...], big_real, big_imag, kz, PY)):
                for part in range(2):
                    field[kz + at, part] = out[part]
                    total[kz + at, part] = jnp.zeros((PY, LANES), F32)

    loop(KZ // (2 * UF), field_y)

    def view(slot, carry):
        buffer = lax.rem(slot, 2)
        for copy in fetch(slot):
            copy.wait()

        @pl.when(slot + 1 < count)
        def _():
            for copy in fetch(slot + 1):
                copy.start()

        def product(j):
            for pair in range(UP):
                kz = (j * UP + pair) * 2
                reals, imags = [], []
                for at in range(2):
                    fr, fi = field[kz + at, 0], field[kz + at, 1]
                    pr, pi = otf[buffer, kz + at, 0], otf[buffer, kz + at, 1]
                    reals.append(fr * pr - fi * pi)
                    imags.append(fr * pi + fi * pr)
                for at, out in enumerate(along_y(wyi_ref[...], reals, imags)):
                    where = pl.ds((kz + at) * YPITCH, BY)
                    real[where, :] = out[0]
                    imag[where, :] = out[1]

        loop(KZ // (2 * UP), product)

        def inverse_x(j):
            for group in range(2):
                y = j * 8 + group * 4
                out = x_from_rows(wxi_ref[...], real, imag, [y + k for k in range(4)], YPITCH)
                for pair in range(2):
                    piece = out[:, pair * LANES:(pair + 1) * LANES]
                    data = jnp.concatenate([piece[:BX], piece[BX:]], axis=1)
                    lines[aligned(j * 4 + group * 2 + pair, BX), :] = three(data, 1)

        loop(BY // 8, inverse_x, UX)

        for j in range(2):
            blurred = dot(lines[j * 8 * BX:(j + 1) * 8 * BX, :], wzi_ref[...])
            for pair in range(8):
                where = columns(j * 8 + pair, 1)
                error[:, where] = image[buffer, :, where] / blurred[pair * BX:(pair + 1) * BX] - 1.0

        def read_error(pair, pairs):
            return error[:, columns(pair, pairs)]

        z_then_x(read_error, BY // 2, wz_ref, wxe_ref, real, imag, 2, (thin0, thin1))

        def gather(j):
            for pair in range(UG):
                kz = (j * UG + pair) * 2
                for at, (er, ei) in enumerate(y_from_rows(wye_ref[...], real, imag, kz, BY)):
                    pr, pi = otf[buffer, kz + at, 0], otf[buffer, kz + at, 1]
                    total[kz + at, 0] += er * pr + ei * pi
                    total[kz + at, 1] += ei * pr - er * pi

        loop(KZ // (2 * UG), gather)
        return carry

    lax.fori_loop(0, count, view, 0)

    def inverse_y(j):
        for pair in range(UT):
            kz = (j * UT + pair) * 2
            reals = [total[kz + at, 0] for at in range(2)]
            imags = [total[kz + at, 1] for at in range(2)]
            for at, out in enumerate(along_y(wyo_ref[...], reals, imags)):
                row = (kz + at) * YPITCH
                for value, big, own in zip(out, (big_real, big_imag), (real_out, imag_out)):
                    big[pl.ds(row, BY), :] = value[:BY]
                    own[pl.ds(row, BY), :] = value[BY:2 * BY]
                    big[pl.ds(KZ * YPITCH + row, BY), :] = value[2 * BY:]

    loop(KZ // (2 * UT), inverse_y)
    chunks = [
        (big_real, big_imag, side * KZ * YPITCH + y, out, y // 2)
        for side, out in ((odd, (outer_out, inner_out)), (1 - odd, (first_out,)))
        for y in range(0, BY, 8)
    ]
    final_sums(wxo_ref, wzi_ref, chunks, (last0, last1))


def tail_kernel(real, imag, wzi_ref, wxo_ref, out, last0, last1):
    chunks = [(real, imag, y, (out,), y // 2) for y in range(0, BY, 8)]
    final_sums(wxo_ref, wzi_ref, chunks, (last0, last1))


SPECTRUM = (KZ, 2, PY, LANES)
ROWS = (KZ * YPITCH, LANES)
WIDE = (WX, BY * SZ)
LAST = pltpu.VMEM((4 * WX, 6 * LANES), BF16)
IN_VMEM = pl.BlockSpec(memory_space=pltpu.VMEM)
IN_SMEM = pl.BlockSpec(memory_space=pltpu.SMEM)
ANYWHERE = pl.BlockSpec(memory_space=pl.ANY)


def otf_call(count, ids, psf, begin, end, held=None):
    tables = (z_forward(-HALF), x_forward(K, -HALF, K), y_forward(K, -HALF))
    inputs = [count, ids, psf] + [jnp.asarray(t) for t in tables]
    specs = [IN_SMEM, IN_SMEM, ANYWHERE] + [ANYWHERE] * len(tables)
    aliases = {}
    if held is not None:
        aliases = {len(inputs): 0}
        inputs.append(held)
        specs.append(ANYWHERE)
    return pl.pallas_call(
        functools.partial(otf_kernel, begin, end),
        out_shape=jax.ShapeDtypeStruct((CMAX,) + SPECTRUM, F32),
        in_specs=specs,
        out_specs=ANYWHERE,
        scratch_shapes=[
            pltpu.VMEM((2, K, K * K), F32),
            pltpu.VMEM(SPECTRUM, F32),
            pltpu.VMEM((K * KPITCH, LANES), F32),
            pltpu.VMEM((K * KPITCH, LANES), F32),
            pltpu.VMEM((ZPO * 2 * KZ, 3 * LANES), BF16),
            pltpu.VMEM((ZPO * 2 * KZ, 3 * LANES), BF16),
        ] + room_for(tables) + [
            pltpu.SemaphoreType.DMA((2,)),
            pltpu.SemaphoreType.DMA((2 * KZ // (2 * UY),)),
            pltpu.SemaphoreType.DMA((len(tables),)),
        ],
        input_output_aliases=aliases,
        compiler_params=pltpu.CompilerParams(vmem_limit_bytes=OTF_LIMITS[0 if held is None else 1]),
        cost_estimate=pl.CostEstimate(
            flops=4 * 10**9 * (end - begin), bytes_accessed=6 * 10**6 * (end - begin), transcendentals=0
        ),
        name="otf",
    )(*inputs)


def main_call(count, ids, odd, window, views, otf):
    own, first, second = window
    tables = (
        z_forward(0),
        z_inverse(),
        x_forward(WX, 0, LANES),
        y_forward(PY, 0),
        y_inverse(BY, HALF, two_rows),
        x_inverse(BX, HALF, two_rows),
        x_forward(BX, HALF, BX, 2),
        y_forward(BY, HALF),
        y_inverse(PY, 0, three_parts),
        x_inverse(WX, 0, three_parts),
    )
    return pl.pallas_call(
        main_kernel,
        out_shape=[
            jax.ShapeDtypeStruct(shape, F32)
            for shape in (WIDE, (2 * BX, BY * SZ), (BX, BY * SZ), ROWS, ROWS)
        ],
        in_specs=[IN_SMEM] * 3 + [IN_VMEM] * 3 + [ANYWHERE] * 2 + [IN_VMEM] * len(tables),
        out_specs=[IN_VMEM] * 5,
        scratch_shapes=[
            pltpu.VMEM(SPECTRUM, F32),
            pltpu.VMEM(SPECTRUM, F32),
            pltpu.VMEM((PY * KPITCH, LANES), F32),
            pltpu.VMEM((PY * KPITCH, LANES), F32),
            pltpu.VMEM(ROWS, F32),
            pltpu.VMEM(ROWS, F32),
            pltpu.VMEM((BX * BY // 2, 6 * LANES), BF16),
            pltpu.VMEM((BX, BY * SZ), F32),
            pltpu.VMEM((2,) + SPECTRUM, F32),
            pltpu.VMEM((2, BX, BY * SZ), F32),
            pltpu.VMEM((ZPF * 2 * KZ, 6 * LANES), BF16),
            pltpu.VMEM((ZPF * 2 * KZ, 6 * LANES), BF16),
            pltpu.VMEM((ZPE * KZ, 3 * LANES), BF16),
            pltpu.VMEM((ZPE * KZ, 3 * LANES), BF16),
            LAST,
            LAST,
            pltpu.SemaphoreType.DMA((2,)),
            pltpu.SemaphoreType.DMA((2,)),
        ],
        compiler_params=pltpu.CompilerParams(vmem_limit_bytes=MAIN_LIMIT),
        cost_estimate=pl.CostEstimate(flops=30 * 10**9, bytes_accessed=40 * 10**6, transcendentals=0),
        name="views",
    )(count, ids, odd, own, first, second, views, otf, *[jnp.asarray(t) for t in tables])


def tail_call(real, imag):
    tables = (z_inverse(), x_inverse(WX, 0, three_parts))
    return pl.pallas_call(
        tail_kernel,
        out_shape=jax.ShapeDtypeStruct(WIDE, F32),
        in_specs=[IN_VMEM] * 4,
        out_specs=IN_VMEM,
        scratch_shapes=[LAST, LAST],
        compiler_params=pltpu.CompilerParams(vmem_limit_bytes=TAIL_LIMIT),
        cost_estimate=pl.CostEstimate(flops=4 * 10**9, bytes_accessed=3 * 10**6, transcendentals=0),
        name="tail",
    )(real, imag, *[jnp.asarray(t) for t in tables])


def swaps(axis):
    devices = lax.axis_size(axis)
    first = [(i, i ^ 1) for i in range(devices) if i ^ 1 < devices]
    second = [(i, i + 1 if i % 2 else i - 1) for i in range(1, devices)]
    second = [(i, j) for i, j in second if j < devices]
    return lax.rem(lax.axis_index(axis), 2), first, second


def per_device(estimate, views, psf, view_list, view_count):
    ids = view_list.reshape(V)
    count = view_count.reshape(1)
    odd_x, first_x, second_x = swaps("bx")
    odd_y, first_y, second_y = swaps("by")
    one = lax.ppermute(estimate, "bx", first_x)
    other = lax.ppermute(estimate, "bx", second_x)
    before = jnp.where(odd_x == 1, one, other)
    after = jnp.where(odd_x == 1, other, one)
    own = jnp.concatenate([before, estimate, after], axis=0)
    window = (own, lax.ppermute(own, "by", first_y), lax.ppermute(own, "by", second_y))
    otf = otf_call(count, ids, psf, 0, 2)
    otf = otf_call(count, ids, psf, 2, CMAX, otf)
    rim, outer, inner, real, imag = main_call(
        count, ids, odd_y.reshape(1), window, views, otf
    )
    other_outer = lax.ppermute(outer, "by", second_y)
    one = lax.ppermute(rim, "by", first_y)
    center, inner = lax.optimization_barrier((tail_call(real, imag), inner))
    other_inner = lax.ppermute(inner, "by", second_y)
    sums = center + one
    low = sums[:BX] + other_outer[:BX]
    high = sums[2 * BX:] + other_outer[BX:]
    other = lax.ppermute(jnp.where(odd_x == 1, high, low), "bx", second_x)
    one = lax.ppermute(jnp.where(odd_x == 1, low, high), "bx", first_x)
    correction = sums[BX:2 * BX] + other_inner + one + other
    return estimate * (1.0 + correction / count.astype(F32))


def solution(mesh):
    return jax.shard_map(
        per_device,
        mesh=mesh,
        in_specs=(P("bx", "by"), P(None, "bx", "by"), P(), P("bx", "by", None), P("bx", "by")),
        out_specs=P("bx", "by"),
        check_vma=False,
    )
```
